32 devices in a mesh: seq: 4 (over y, core), fsdp: 8 (over z, x).
Axes of the slice: x: 2, y: 2, z: 4, core: 2. Of those that a mesh axis runs over, the one named last changes fastest.
Arguments:
- tokens: bfloat16 [2, 8, 1024, 1024], P(None, 'fsdp', 'seq'), may hold values from -6 to 6
- segment_ids: int32 [2, 8, 1024], P(None, 'fsdp'), may hold values from 0 to 8, never falling along the last dimension, each value on 1 to 512 neighbouring positions
- norm1_gain: bfloat16 [1024], P('fsdp'), may hold values from 0.5 to 1.5
- norm1_bias: bfloat16 [1024], P('fsdp'), may hold values from -3 to 3
- w_qkv: bfloat16 [1024, 3072], P('fsdp'), may hold values from -0.1875 to 0.1875
- w_out: bfloat16 [1024, 1024], P('fsdp'), may hold values from -1.5 to 1.5
- norm2_gain: bfloat16 [1024], P('fsdp'), may hold values from 0.5 to 1.5
- norm2_bias: bfloat16 [1024], P('fsdp'), may hold values from -3 to 3
- w_up: bfloat16 [1024, 4096], P('fsdp'), may hold values from -0.1875 to 0.1875
- w_down: bfloat16 [4096, 1024], P('fsdp'), may hold values from -0.125 to 0.125
- cotangent: bfloat16 [2, 8, 1024, 1024], P(None, 'fsdp', 'seq'), may hold values from -6 to 6
Outputs:
- output: bfloat16 [2, 8, 1024, 1024], P(None, 'fsdp', 'seq')
- grad_tokens: float32 [2, 8, 1024, 1024], P(None, 'fsdp', 'seq')
- grad_norm1_gain: float32 [1024], P('fsdp')
- grad_norm1_bias: float32 [1024], P('fsdp')
- grad_w_qkv: float32 [1024, 3072], P('fsdp')
- grad_w_out: float32 [1024, 1024], P('fsdp')
- grad_norm2_gain: float32 [1024], P('fsdp')
- grad_norm2_bias: float32 [1024], P('fsdp')
- grad_w_up: float32 [1024, 4096], P('fsdp')
- grad_w_down: float32 [4096, 1024], P('fsdp')
The draws below stay inside these ranges and needn't reach their ends.
Inputs may be any that keep to these rules, and one draw needn't show every extreme that they name: `segment_ids`: in each sequence the ids start at 0 and rise by one at each new document; every document has 1 to 512 tokens, and in every sequence one has exactly 512.
All inputs are finite; a program needn't handle non-finite values.
Results may differ from the reference program's by a relative error of at most 0.018.
Values may be sent and summed in bfloat16 or wider, within the bound.
No kernel may reach another device: no remote copies, remote signals or barrier semaphores. Data moves between devices by JAX's collectives and lax.ppermute only.
A program may use at most 192 MiB of HBM per device.

```python
import math
import jax
import jax.numpy as jnp
import numpy as np
from jax import lax

D = 1024
HEADS = 16
HEAD_DIM = 64
FF = 4096
MICRO = 2
DOC_MOST = 512
BLOCK = 512
BAND = 1
SEQ_LEN = 1024
BATCH = 8


def strengthened(entries, rng, source, target, shards_of, factor):
    def block_of(axis_at):
        return (jnp.arange(entries.shape[axis_at]) // (entries.shape[axis_at] // shards_of)).reshape((-1,) + (1,) * (entries.ndim - 1 - axis_at))

    near = jax.random.permutation(rng, shards_of)[block_of(target)]
    second = (block_of(target) + shards_of // 2) % shards_of
    return jnp.where((block_of(source) == near) | (block_of(source) == second), factor * entries, entries)


def block_levels(own_key, shape, split, low, largest):
    def one(axis_at, parts):
        draws = jax.random.uniform(jax.random.fold_in(jax.random.fold_in(own_key, 6), axis_at), (parts,), jnp.float32, low / len(split), largest / len(split))
        return jnp.repeat(jnp.exp(draws), shape[axis_at] // parts).reshape((-1,) + (1,) * (len(shape) - axis_at - 1))

    gain = one(*split[0])
    for cut in split[1:]:
        gain = gain * one(*cut)
    return gain


def length_profile(count, total, reach, skew):
    portions = [(1 << 20) // math.isqrt(grade ** skew) + 1 for grade in range(2, count + 1)]
    spare, holding = total - reach - (count - 1), [1] * (count - 1)
    while spare > 0:
        free = [i for i in range(count - 1) if holding[i] < reach]
        pool, left = sum([portions[i] for i in free]), spare
        for i in free:
            extra = min(reach - holding[i], max(1, left * portions[i] // pool), spare)
            holding[i] = holding[i] + extra
            spare = spare - extra
    return np.array([reach] + holding)


def uneven_parts(own_key, count, total, limit, lean):
    if count == 2:
        one = jax.random.randint(own_key, (), max(1, total - limit), min(limit, total - 1) + 1)
        return jnp.stack([one, total - one])
    tallies = jnp.asarray(length_profile(count, total, limit, lean), jnp.int32)
    couples = (count - 1) // 2
    giver, taker = tallies[1:1 + 2 * couples:2], tallies[2:2 + 2 * couples:2]
    margin = jnp.minimum(giver - 1, limit - taker)
    moved = jax.random.randint(jax.random.fold_in(own_key, 1), (couples,), 0, 1 << 20) % (margin + 1)
    tallies = tallies.at[1:1 + 2 * couples:2].set(giver - moved).at[2:2 + 2 * couples:2].set(taker + moved)
    return tallies[jax.random.permutation(jax.random.fold_in(own_key, 2), count)]


def gaussian(own_key, dims, deviation, reach, pieces=(), kind=jnp.bfloat16):
    gain = block_levels(own_key, dims, pieces, -0.22, 0.18) if pieces else 1.0
    array = jax.random.normal(own_key, dims, jnp.float32) * deviation * gain
    return jnp.minimum(jnp.maximum(array, -reach), reach).astype(kind)


def bell_draw_with(stream_key, dims, scale, bound, shards, heavy, kind=jnp.bfloat16):
    array = scale * jax.random.normal(stream_key, dims, jnp.float32)
    if shards:
        array = array * block_levels(stream_key, dims, shards, -0.22, 0.18)
    return jnp.clip(strengthened(array, jax.random.fold_in(stream_key, 3), *heavy), -bound, bound).astype(kind)


def setup_inputs(seed: int = 0) -> dict:
    splits = jax.random.split(jax.random.key(seed), 12)
    tokens = bell_draw_with(splits[0], (MICRO, BATCH, SEQ_LEN, D), 1.0, 6.0, ((1, 8), (2, 4)), (1, 3, 8, 2.0))
    segment_ids = jax.vmap(lambda own: jnp.searchsorted(jnp.cumsum(uneven_parts(own, 4 * SEQ_LEN // DOC_MOST + 1, SEQ_LEN, DOC_MOST, 1)), jnp.arange(SEQ_LEN), side="right"))(jax.random.split(splits[1], MICRO * BATCH)).reshape((MICRO, BATCH, SEQ_LEN)).astype(jnp.int32)
    norm1_gain = jnp.clip(1.0 + 0.1 * jax.random.normal(splits[2], (D,), jnp.float32), 0.5, 1.5).astype(jnp.bfloat16)
    norm1_bias = gaussian(splits[3], (D,), 0.3, 3.0, ((0, 8),))
    w_qkv = gaussian(splits[4], (D, 3 * D), D ** -0.5, 0.1875, ((0, 8),))
    w_out = gaussian(splits[5], (D, D), (D // 64) ** -0.5, 1.5, ((0, 8),))
    norm2_gain = jnp.clip(1.0 + 0.1 * jax.random.normal(splits[6], (D,), jnp.float32), 0.5, 1.5).astype(jnp.bfloat16)
    norm2_bias = gaussian(splits[7], (D,), 0.3, 3.0, ((0, 8),))
    w_up = gaussian(splits[8], (D, FF), D ** -0.5, 0.1875, ((0, 8),))
    w_down = gaussian(splits[9], (FF, D), (FF // 2) ** -0.5, 0.125, ((0, 8),))
    cotangent = bell_draw_with(splits[10], (MICRO, BATCH, SEQ_LEN, D), 1.0, 6.0, ((1, 8), (2, 4)), (1, 3, 8, 2.0))
    return dict(tokens=tokens, segment_ids=segment_ids, norm1_gain=norm1_gain, norm1_bias=norm1_bias, w_qkv=w_qkv, w_out=w_out, norm2_gain=norm2_gain, norm2_bias=norm2_bias, w_up=w_up, w_down=w_down, cotangent=cotangent)


@jax.custom_vjp
def low(v):
    return lax.optimization_barrier(v.astype(jnp.bfloat16)).astype(jnp.float32)

@jax.custom_vjp
def low_back(v):
    return v

def low_keep(v):
    return (low(v), None)

def low_pass(kept, grad):
    return (grad,)

def back_keep(v):
    return (v, None)

def back_low(kept, grad):
    return (low(grad),)
low.defvjp(low_keep, low_pass)
low_back.defvjp(back_keep, back_low)
highest = lax.Precision.HIGHEST
epsilon = 1e-05

def normalize(values, gain_row, bias_row):
    row_mean = lax.optimization_barrier(jnp.mean(values, axis=-1, keepdims=True))
    centred = values - row_mean
    variance = lax.optimization_barrier(jnp.mean(centred * centred, axis=-1, keepdims=True))
    return centred * lax.rsqrt(variance + epsilon) * gain_row + bias_row

def attention(queries, key_rows, value_rows, segments):
    length = queries.shape[0]
    padding = BAND * BLOCK
    window = (BAND + 1) * BLOCK

    def heads_first(rows):
        return rows.reshape(length, HEADS, HEAD_DIM).transpose(1, 0, 2)
    query_heads = heads_first(queries)
    key_pad = jnp.pad(heads_first(key_rows), ((0, 0), (padding, 0), (0, 0)))
    value_pad = jnp.pad(heads_first(value_rows), ((0, 0), (padding, 0), (0, 0)))
    segments_pad = jnp.concatenate([jnp.full((padding,), -1, jnp.int32), segments.astype(jnp.int32)])

    def one_block(block_index):
        row_start = block_index * BLOCK
        query_block = lax.dynamic_slice_in_dim(query_heads, row_start, BLOCK, 1)
        key_block = lax.dynamic_slice_in_dim(key_pad, row_start, window, 1)
        value_block = lax.dynamic_slice_in_dim(value_pad, row_start, window, 1)
        query_pos = row_start + jnp.arange(BLOCK, dtype=jnp.int32)
        key_pos = row_start - padding + jnp.arange(window, dtype=jnp.int32)
        query_seg = lax.dynamic_slice_in_dim(segments_pad, row_start + padding, BLOCK, 0)
        key_seg = lax.dynamic_slice_in_dim(segments_pad, row_start, window, 0)
        allowed = (key_pos[None, :] <= query_pos[:, None]) & (key_seg[None, :] == query_seg[:, None])
        scores = low_back(jnp.einsum('hqd,hkd->hqk', query_block, key_block, precision=highest))
        scores = jnp.where(allowed[None], scores, -1e+30)
        probs = jax.nn.softmax(scores, axis=-1)
        mixed = jnp.einsum('hqk,hkd->hqd', low(probs), value_block, precision=highest)
        return low_back(low(mixed))
    blocks = lax.map(jax.checkpoint(one_block), jnp.arange(length // BLOCK, dtype=jnp.int32))
    per_head = blocks.transpose(1, 0, 2, 3).reshape(HEADS, length, HEAD_DIM)
    return per_head.transpose(1, 0, 2).reshape(length, D)

def layer(inputs, segments, params):
    gain_one, bias_one, joint_weight, output_weight, gain_two, bias_two, upward_weight, downward_weight = params
    normed = low(normalize(inputs, gain_one, bias_one))
    projected = jnp.dot(normed, joint_weight, precision=highest)
    score_scale = 1.0 / HEAD_DIM ** 0.5
    queries = low_back(low(projected[:, :D] * score_scale))
    key_rows = low_back(low(projected[:, D:2 * D]))
    value_rows = low_back(low(projected[:, 2 * D:]))
    attended = attention(queries, key_rows, value_rows, segments)
    middle = inputs + low_back(jnp.dot(attended, output_weight, precision=highest))
    normed_two = low(normalize(middle, gain_two, bias_two))
    pre_act = low_back(jnp.dot(normed_two, upward_weight, precision=highest))
    hidden = low(jax.nn.gelu(pre_act, approximate=False))
    return middle + low_back(jnp.dot(hidden, downward_weight, precision=highest))

def reference(tokens, segment_ids, norm1_gain, norm1_bias, w_qkv, w_out, norm2_gain, norm2_bias, w_up, w_down, cotangent):
    params = (norm1_gain.astype(jnp.float32), norm1_bias.astype(jnp.float32), w_qkv.astype(jnp.float32), w_out.astype(jnp.float32), norm2_gain.astype(jnp.float32), norm2_bias.astype(jnp.float32), w_up.astype(jnp.float32), w_down.astype(jnp.float32))
    flat_inputs = tokens.reshape(MICRO * BATCH, SEQ_LEN, D).astype(jnp.float32)
    flat_segments = segment_ids.reshape(MICRO * BATCH, SEQ_LEN).astype(jnp.int32)
    flat_grads = cotangent.reshape(MICRO * BATCH, SEQ_LEN, D).astype(jnp.float32)

    def one_sequence(totals, sequence):
        inputs, segments, grad_rows = sequence

        def forward(input_rows, weights):
            return layer(input_rows, segments, weights)
        result, pullback = jax.vjp(forward, inputs, params)
        grad_inputs, grad_params = pullback(grad_rows)
        return (jax.tree.map(jnp.add, totals, grad_params), (result.astype(jnp.bfloat16), grad_inputs))
    zeros = jax.tree.map(jnp.zeros_like, params)
    totals, (results, grad_inputs) = lax.scan(one_sequence, zeros, (flat_inputs, flat_segments, flat_grads))
    output = results.reshape(MICRO, BATCH, SEQ_LEN, D)
    grad_tokens = grad_inputs.reshape(MICRO, BATCH, SEQ_LEN, D)
    return (output, grad_tokens, totals[0], totals[1], totals[2], totals[3], totals[4], totals[5], totals[6], totals[7])
```

```python
import functools
import math

import jax
import jax.numpy as jnp
from jax import lax
from jax.experimental import pallas as pl
from jax.experimental.pallas import tpu as pltpu
from jax.sharding import Mesh
from jax.sharding import PartitionSpec as P

HEAD_DIM = 64
DOC_MOST = 512
TILE = 256
LANES = 128
epsilon = 1e-05
SWAP = [(0, 1), (1, 0)]
f32 = jnp.float32
bf16 = jnp.bfloat16


def dot(left, right, dims):
    return lax.dot_general(left, right, (dims, ((), ())), preferred_element_type=f32)


def mm(left, right):
    return dot(left, right, ((1,), (0,)))


def mm_rows(left, right):
    return dot(left, right, ((0,), (0,)))


def mm_cols(left, right):
    return dot(left, right, ((1,), (1,)))


def pick(array, index, axis):
    return lax.dynamic_index_in_dim(array, index, axis, keepdims=False)


def swap(value, axis):
    return lax.ppermute(value, axis, SWAP)


def ordered(own, other, index, axis):
    first = jnp.where(index == 0, own, other)
    second = jnp.where(index == 0, other, own)
    return jnp.stack([first, second], axis)


def tile_spans(rows):
    tile = min(TILE, rows)
    spans = []
    for start in range(0, rows, tile):
        low = max(0, (start - DOC_MOST + 1) // tile * tile)
        spans.append((start, low, start + tile))
    return tile, spans


def fill_bias(bias, seg_col, seg_row, spans, tile):
    for i, (start, low, high) in enumerate(spans):
        width = high - low
        query_pos = start + lax.broadcasted_iota(jnp.int32, (tile, width), 0)
        key_pos = low + lax.broadcasted_iota(jnp.int32, (tile, width), 1)
        same = seg_col[start : start + tile, :] == seg_row[:, low:high]
        allowed = (key_pos <= query_pos) & same
        bias[i, :, :width] = jnp.where(allowed, 0.0, -1e30).astype(f32)


def attend_kernel(spans, tile, q_ref, k_ref, v_ref, seg_col, seg_row, out_ref, lse_ref, bias):
    @pl.when(pl.program_id(0) == 0)
    def _():
        fill_bias(bias, seg_col, seg_row, spans, tile)

    left = lax.broadcasted_iota(jnp.int32, (tile, LANES), 1) < HEAD_DIM
    for i, (start, low, high) in enumerate(spans):
        rows = slice(start, start + tile)
        queries = q_ref[rows, :]
        keys, values = k_ref[low:high, :], v_ref[low:high, :]
        mixed, logs = [], []
        for half in (left, ~left):
            scores = mm_cols(jnp.where(half, queries, jnp.zeros_like(queries)), keys)
            scores = scores + bias[i, :, : high - low]
            top = jnp.max(scores, axis=-1, keepdims=True)
            powers = jnp.exp(scores - top)
            total = jnp.sum(powers, axis=-1, keepdims=True)
            mixed.append(mm((powers * (1.0 / total)).astype(bf16), values))
            logs.append(top + jnp.log(total))
        out_ref[rows, :] = jnp.where(left, mixed[0], mixed[1]).astype(bf16)
        lse_ref[rows, :] = jnp.where(left, logs[0], logs[1])


def attend(joint, seg_col, seg_row):
    rows, width = joint.shape[0], joint.shape[1] // 3
    pairs = width // LANES
    tile, spans = tile_spans(rows)
    widest = max(high - low for _, low, high in spans)

    def part(which):
        return pl.BlockSpec((rows, LANES), lambda p: (0, which * pairs + p))

    return pl.pallas_call(
        functools.partial(attend_kernel, spans, tile),
        grid=(pairs,),
        in_specs=[
            part(0),
            part(1),
            part(2),
            pl.BlockSpec((rows, 1), lambda p: (0, 0)),
            pl.BlockSpec((1, rows), lambda p: (0, 0)),
        ],
        out_specs=[part(0), part(0)],
        out_shape=[
            jax.ShapeDtypeStruct((rows, width), bf16),
            jax.ShapeDtypeStruct((rows, width), f32),
        ],
        scratch_shapes=[pltpu.VMEM((len(spans), tile, widest), f32)],
        compiler_params=pltpu.CompilerParams(vmem_limit_bytes=40 * 1024 * 1024),
        name="attend",
    )(joint, joint, joint, seg_col, seg_row)


def attend_back_kernel(
    spans, tile, q_ref, k_ref, v_ref, g_ref, lse_ref, seg_col, seg_row, out_ref, bias, keys_sum, values_sum
):
    @pl.when((pl.program_id(0) == 0) & (pl.program_id(1) == 0))
    def _():
        fill_bias(bias, seg_col, seg_row, spans, tile)

    @pl.when(pl.program_id(1) == 0)
    def _():
        keys_sum[...] = jnp.zeros_like(keys_sum)
        values_sum[...] = jnp.zeros_like(values_sum)
        left = lax.broadcasted_iota(jnp.int32, (tile, LANES), 1) < HEAD_DIM
        for i, (start, low, high) in enumerate(spans):
            rows = slice(start, start + tile)
            queries, grads = q_ref[rows, :], g_ref[rows, :]
            keys, values = k_ref[low:high, :], v_ref[low:high, :]
            parts = []
            for half, lane in ((left, 0), (~left, HEAD_DIM)):
                own_queries = jnp.where(half, queries, jnp.zeros_like(queries))
                own_grads = jnp.where(half, grads, jnp.zeros_like(grads))
                scores = mm_cols(own_queries, keys) + bias[i, :, : high - low]
                probs = jnp.exp(scores - lse_ref[rows, lane : lane + 1])
                grad_probs = mm_cols(own_grads, values)
                inner = jnp.sum(probs * grad_probs, axis=-1, keepdims=True)
                grad_scores = (probs * (grad_probs - inner)).astype(bf16)
                parts.append(mm(grad_scores, keys))
                keys_sum[low:high, :] += mm_rows(grad_scores, own_queries)
                values_sum[low:high, :] += mm_rows(probs.astype(bf16), own_grads)
            grad_queries = jnp.where(left, parts[0], parts[1]).astype(bf16)
            out_ref[rows, :] = grad_queries * jnp.asarray(1.0 / math.sqrt(HEAD_DIM), bf16)

    @pl.when(pl.program_id(1) == 1)
    def _():
        out_ref[...] = keys_sum[...].astype(bf16)

    @pl.when(pl.program_id(1) == 2)
    def _():
        out_ref[...] = values_sum[...].astype(bf16)


def attend_back(joint, grads, lse, seg_col, seg_row):
    rows, width = joint.shape[0], joint.shape[1] // 3
    pairs = width // LANES
    tile, spans = tile_spans(rows)
    widest = max(high - low for _, low, high in spans)

    def part(which):
        return pl.BlockSpec((rows, LANES), lambda p, j: (0, which * pairs + p))

    return pl.pallas_call(
        functools.partial(attend_back_kernel, spans, tile),
        grid=(pairs, 3),
        in_specs=[
            part(0),
            part(1),
            part(2),
            part(0),
            part(0),
            pl.BlockSpec((rows, 1), lambda p, j: (0, 0)),
            pl.BlockSpec((1, rows), lambda p, j: (0, 0)),
        ],
        out_specs=pl.BlockSpec((rows, LANES), lambda p, j: (0, j * pairs + p)),
        out_shape=jax.ShapeDtypeStruct((rows, 3 * width), bf16),
        scratch_shapes=[
            pltpu.VMEM((len(spans), tile, widest), f32),
            pltpu.VMEM((rows, LANES), f32),
            pltpu.VMEM((rows, LANES), f32),
        ],
        compiler_params=pltpu.CompilerParams(vmem_limit_bytes=48 * 1024 * 1024),
        name="attend_back",
    )(joint, joint, joint, grads, lse, seg_col, seg_row)


def gather(own, depth):
    h = lax.axis_index("hi")
    rows, columns = own.shape
    halves = own.reshape(2, rows // 2, columns)
    half = pick(halves, h, 0)
    far = [lax.ppermute(half, "fz", [(i, (i + k) % depth) for i in range(depth)]) for k in range(1, depth)]
    spots = [(0, 0, None), (0, 1, None)]
    pieces = [halves, swap(halves, "fx")]
    for k, piece in enumerate(far, 1):
        side = swap(piece, "fx")
        spots += [(k, 0, 0), (k, 0, 1), (k, 1, 0), (k, 1, 1)]
        pieces += [piece, swap(piece, "hi"), side, swap(side, "hi")]
    return spots, pieces


def load(spots, depth, place, pieces, sems, targets):
    z, x, h = place[0], place[1], place[2]
    copies = []
    for first, columns, where in targets:
        for (k, other_x, other_h), piece in zip(spots, pieces):
            shard = lax.rem(z - k + depth, depth) * 2 + (1 - x if other_x else x)
            for part in range(2) if other_h is None else (None,):
                if part is None:
                    half, source = (1 - h if other_h else h), piece
                else:
                    half, source = part, piece.at[part]
                if columns != source.shape[1]:
                    source = source.at[:, first : first + columns]
                copy = pltpu.make_async_copy(source, where(shard, half), sems.at[len(copies)])
                copy.start()
                copies.append(copy)
    return copies


def below(weight, half_rows):
    def where(shard, half):
        return weight.at[pl.ds(pl.multiple_of((shard * 2 + half) * half_rows, half_rows), half_rows), :]

    return where


def beside(weight, rows, columns):
    def where(shard, half):
        return weight.at[
            pl.ds(pl.multiple_of(shard * rows, rows), rows),
            pl.ds(pl.multiple_of(half * columns, columns), columns),
        ]

    return where


def plus(left, right):
    return (left.astype(f32) + right.astype(f32)).astype(bf16)


def reduce(full, depth):
    z, x, h = lax.axis_index("fz"), lax.axis_index("fx"), lax.axis_index("hi")
    columns = full.shape[1]
    rows = full.shape[0] // (2 * depth)
    view = full.reshape(depth, 2, 2, 2, rows // 4, columns)
    first, second = view[:, :, 0], view[:, :, 1]
    first = plus(pick(first, x, 1), swap(pick(first, 1 - x, 1), "fx"))
    second = plus(pick(second, h, 2), swap(pick(second, 1 - h, 2), "hi"))
    first = plus(pick(first, h, 1), swap(pick(first, 1 - h, 1), "hi"))
    second = plus(pick(second, x, 1), swap(pick(second, 1 - x, 1), "fx"))
    both = jnp.stack([first, second], 1)
    total = pick(both, z, 0).astype(f32)
    for k in range(1, depth):
        ring = [(i, (i + k) % depth) for i in range(depth)]
        total = total + lax.ppermute(pick(both, (z + k) % depth, 0), "fz", ring).astype(f32)
    total = total.astype(bf16)
    return ordered(total, swap(total, "hi"), h, 1).reshape(rows, columns)


def row_block(tile, width):
    return pl.BlockSpec((tile, width), lambda i: (i, 0))


def whole_block(*shape):
    return pl.BlockSpec(shape, lambda i: (0,) * len(shape))


def weight_call(name, step, tiles, place, inputs, sets, outs, scratch, copies, flops):
    pieces = [piece for _, held in sets for piece in held]
    moved = sum(math.prod(v.shape) * v.dtype.itemsize for v in pieces)
    moved += sum(math.prod(v.shape) * v.dtype.itemsize for v, _ in inputs)
    moved += sum(math.prod(v.shape) * v.dtype.itemsize for v, _ in outs)

    def kernel(place_ref, *refs):
        refs = list(refs)

        def take(count):
            taken = refs[:count]
            del refs[:count]
            return taken

        given = take(len(inputs))
        held = [take(len(one)) for _, one in sets]
        made = take(len(outs))
        step(place_ref, given, held, made, refs[:-1], refs[-1])

    return pl.pallas_call(
        kernel,
        grid=(tiles,),
        in_specs=[pl.BlockSpec(memory_space=pltpu.SMEM)]
        + [spec for _, spec in inputs]
        + [pl.BlockSpec(memory_space=pl.ANY)] * len(pieces),
        out_specs=[spec for _, spec in outs],
        out_shape=[shape for shape, _ in outs],
        scratch_shapes=list(scratch) + [pltpu.SemaphoreType.DMA(copies if isinstance(copies, tuple) else (copies,))],
        compiler_params=pltpu.CompilerParams(vmem_limit_bytes=56 * 1024 * 1024),
        cost_estimate=pl.CostEstimate(flops=flops, bytes_accessed=moved, transcendentals=0),
        name=name,
    )(place, *[v for v, _ in inputs], *pieces)


def shape_of(*shape, dtype=bf16):
    return jax.ShapeDtypeStruct(shape, dtype)


def unit_of(values):
    centred = values - jnp.mean(values, axis=-1, keepdims=True)
    variance = jnp.mean(centred * centred, axis=-1, keepdims=True)
    inverse = lax.rsqrt(variance + epsilon)
    return centred * inverse, inverse


def unit_back(grad_unit, unit_rows, inverse):
    mean_grad = jnp.mean(grad_unit, axis=-1, keepdims=True)
    mean_cross = jnp.mean(grad_unit * unit_rows, axis=-1, keepdims=True)
    return inverse * (grad_unit - mean_grad - unit_rows * mean_cross)


def bell_and_slope(values):
    size = jnp.abs(values)
    t = 1.0 / (1.0 + (0.3275911 * math.sqrt(0.5)) * size)
    bell = jnp.exp(values * values * -0.5)
    series = 0.5 * 1.061405429
    for term in (-1.453152027, 1.421413741, -0.284496736, 0.254829592):
        series = series * t + 0.5 * term
    tail = series * t * bell
    phi = jnp.where(values < 0, tail, 1.0 - tail)
    return values * phi, phi + values * bell * (1.0 / math.sqrt(2.0 * math.pi))


def body(
    group,
    depth,
    tokens,
    segment_ids,
    norm1_gain,
    norm1_bias,
    w_qkv,
    w_out,
    norm2_gain,
    norm2_bias,
    w_up,
    w_down,
    cotangent,
):
    h, lo = lax.axis_index("hi"), lax.axis_index("lo")
    z, x = lax.axis_index("fz"), lax.axis_index("fx")
    micro, _, chunk, model = tokens.shape
    shards = 2 * depth
    rows = micro * group * chunk
    own_rows = w_out.shape[0]
    inner = w_up.shape[1] // group
    split_out = (own_rows // HEAD_DIM) % group == 0
    joined = split_out and group == 2
    head_columns = model // group
    tile = min(TILE, rows)
    tiles = rows // tile

    def whole_group(value, axis):
        if group == 2:
            return ordered(value, swap(value, "lo"), lo, axis)
        return lax.all_gather(value, "lo", axis=axis)

    def sequence(array):
        kept = pick(array[:, 0], h, 0)
        came = swap(pick(array[:, 0], 1 - h, 0), "hi")
        return whole_group(ordered(kept, came, h, 0), 1).reshape(rows, model)

    def placed(array):
        came = swap(pick(array, 1 - h, 0).astype(bf16), "hi").astype(array.dtype)
        return ordered(pick(array, h, 0), came, h, 0)[:, None]

    def other_part(partial):
        if group == 2:
            return swap(partial, "lo")
        return (lax.psum(partial, "lo").astype(f32) - partial.astype(f32)).astype(bf16)

    def sum_own(partial):
        parts = partial.reshape(micro, group, chunk, model)
        if group == 2:
            came = swap(pick(parts, 1 - lo, 1), "lo").astype(f32)
            return pick(parts, lo, 1).astype(f32) + came
        return lax.psum_scatter(parts, "lo", scatter_dimension=1).astype(f32)

    def own_chunks(full):
        return pick(full.reshape(micro, group, chunk, -1), lo, 1)

    if split_out:
        qkv_part = pick(w_qkv.reshape(own_rows, 3, shards, group, -1), lo, 3).reshape(own_rows, -1)
        out_part = pick(w_out.reshape(group, own_rows // group, model), lo, 0)
    else:
        qkv_part = pick(w_qkv.reshape(own_rows, 3, group, -1), lo, 2).reshape(own_rows, -1)
        out_part = w_out
    up_part = pick(w_up.reshape(own_rows, shards, group, -1), lo, 2).reshape(own_rows, -1)
    down_part = pick(w_down.reshape(group, -1, model), lo, 0)
    out_rows, down_rows = out_part.shape[0], down_part.shape[0]

    vectors = jnp.stack([norm1_gain, norm1_bias, norm2_gain, norm2_bias], axis=1)
    parts = [qkv_part, jnp.pad(vectors, ((0, 0), (0, LANES - 4)))]
    if joined:
        parts.append(jnp.concatenate([out_part[:, : model // 2], out_part[:, model // 2 :]], axis=0))
    place = jnp.stack([z, x, h, lo]).astype(jnp.int32)
    scale_at, out_at = 3 * head_columns, 3 * head_columns + LANES

    inputs = sequence(tokens)
    first_set = gather(jnp.concatenate(parts, axis=1), depth)
    out_set = first_set if joined else gather(out_part, depth)
    up_set = gather(up_part, depth)
    down_set = gather(down_part, depth)
    grad_result = sequence(cotangent)

    segments = pick(segment_ids[:, 0], h, 0)
    seg_col, seg_row = segments[:, None], segments[None, :]
    half_rows = own_rows // 2
    copies = 4 * shards

    def load_out(place_ref, pieces, weight, sems):
        if joined:
            targets = [(out_at, model // 2, beside(weight, out_rows, model // 2))]
        else:
            targets = [(0, model, below(weight, out_rows // 2))]
        return load(out_set[0], depth, place_ref, pieces, sems, targets)

    def out_weight(weight, place_ref):
        if split_out:
            return weight[...]
        return weight[pl.ds(pl.multiple_of(place_ref[3] * head_columns, head_columns), head_columns), :]

    def project(place_ref, given, held, made, scratch, sems):
        (rows_ref,), (normed_ref, joint_ref, scales_ref) = given, made
        weight, columns = scratch

        @pl.when(pl.program_id(0) == 0)
        def _():
            targets = [
                (0, 3 * head_columns, below(weight, half_rows)),
                (scale_at, LANES, below(columns, half_rows)),
            ]
            for copy in load(first_set[0], depth, place_ref, held[0], sems, targets):
                copy.wait()
            scales_ref[...] = columns[...].astype(f32).T[:8, :]

        unit_rows, _ = unit_of(rows_ref[...].astype(f32))
        normed = (unit_rows * scales_ref[0:1, :] + scales_ref[1:2, :]).astype(bf16)
        normed_ref[...] = normed
        for at in range(0, 3 * head_columns, head_columns):
            part = mm(normed, weight[:, at : at + head_columns])
            if at == 0:
                part = part * (1.0 / math.sqrt(HEAD_DIM))
            joint_ref[:, at : at + head_columns] = part.astype(bf16)

    normed, joint, scales = weight_call(
        "project",
        project,
        tiles,
        place,
        [(inputs, row_block(tile, model))],
        [first_set],
        [
            (shape_of(rows, model), row_block(tile, model)),
            (shape_of(rows, 3 * head_columns), row_block(tile, 3 * head_columns)),
            (shape_of(8, model, dtype=f32), whole_block(8, model)),
        ],
        [pltpu.VMEM((model, 3 * head_columns), bf16), pltpu.VMEM((model, LANES), bf16)],
        copies,
        6 * rows * model * head_columns,
    )
    attended, lse = attend(joint, seg_col, seg_row)

    def leave(place_ref, given, held, made, scratch, sems):
        (rows_ref,), (out_ref,), (weight,) = given, made, scratch

        @pl.when(pl.program_id(0) == 0)
        def _():
            for copy in load_out(place_ref, held[0], weight, sems):
                copy.wait()

        out_ref[...] = mm(rows_ref[...], out_weight(weight, place_ref)).astype(bf16)

    (branch,) = weight_call(
        "leave",
        leave,
        tiles,
        place,
        [(attended, row_block(tile, head_columns))],
        [out_set],
        [(shape_of(rows, model), row_block(tile, model))],
        [pltpu.VMEM((out_rows * shards, model), bf16)],
        copies,
        2 * rows * model * head_columns,
    )
    branch_other = other_part(branch)
    wide = min(512, inner)

    def widen(place_ref, given, held, made, scratch, sems):
        rows_ref, own_ref, other_ref, scales_ref = given
        middle_ref, normed_ref, hidden_ref, slope_ref = made
        (weight,) = scratch

        @pl.when(pl.program_id(0) == 0)
        def _():
            targets = [(0, inner, below(weight, half_rows))]
            for copy in load(up_set[0], depth, place_ref, held[0], sems, targets):
                copy.wait()

        added = own_ref[...].astype(f32) + other_ref[...].astype(f32)
        middle = rows_ref[...].astype(f32) + added
        middle_ref[...] = middle
        unit_rows, _ = unit_of(middle)
        normed = (unit_rows * scales_ref[2:3, :] + scales_ref[3:4, :]).astype(bf16)
        normed_ref[...] = normed
        for at in range(0, inner, wide):
            hidden, slope = bell_and_slope(mm(normed, weight[:, at : at + wide]))
            hidden_ref[:, at : at + wide] = hidden.astype(bf16)
            slope_ref[:, at : at + wide] = slope.astype(bf16)

    middle, normed_two, hidden, slope = weight_call(
        "widen",
        widen,
        tiles,
        place,
        [
            (inputs, row_block(tile, model)),
            (branch, row_block(tile, model)),
            (branch_other, row_block(tile, model)),
            (scales, whole_block(8, model)),
        ],
        [up_set],
        [
            (shape_of(rows, model, dtype=f32), row_block(tile, model)),
            (shape_of(rows, model), row_block(tile, model)),
            (shape_of(rows, inner), row_block(tile, inner)),
            (shape_of(rows, inner), row_block(tile, inner)),
        ],
        [pltpu.VMEM((model, inner), bf16)],
        copies,
        2 * rows * model * inner,
    )
    grad_down = mm_rows(hidden, grad_result).astype(bf16)

    def narrow(place_ref, given, held, made, scratch, sems):
        hidden_ref, grad_ref, slope_ref = given
        out_ref, pre_ref, back_ref = made
        upward, downward = scratch

        @pl.when(pl.program_id(0) == 0)
        def _():
            targets = [(0, inner, below(upward, half_rows))]
            ups = load(up_set[0], depth, place_ref, held[0], sems.at[0], targets)
            targets = [(0, model, below(downward, down_rows // 2))]
            for copy in ups + load(down_set[0], depth, place_ref, held[1], sems.at[1], targets):
                copy.wait()

        out_ref[...] = mm(hidden_ref[...], downward[...]).astype(bf16)
        total = jnp.zeros(back_ref.shape, f32)
        for at in range(0, inner, wide):
            grad = mm_cols(grad_ref[...], downward[at : at + wide, :])
            grad = (grad * slope_ref[:, at : at + wide].astype(f32)).astype(bf16)
            pre_ref[:, at : at + wide] = grad
            total = total + mm_cols(grad, upward[:, at : at + wide])
        back_ref[...] = total.astype(bf16)

    result, grad_pre, back = weight_call(
        "narrow",
        narrow,
        tiles,
        place,
        [
            (hidden, row_block(tile, inner)),
            (grad_result, row_block(tile, model)),
            (slope, row_block(tile, inner)),
        ],
        [up_set, down_set],
        [
            (shape_of(rows, model), row_block(tile, model)),
            (shape_of(rows, inner), row_block(tile, inner)),
            (shape_of(rows, model), row_block(tile, model)),
        ],
        [pltpu.VMEM((model, inner), bf16), pltpu.VMEM((inner, model), bf16)],
        (2, copies),
        6 * rows * model * inner,
    )
    back_other = other_part(back)
    grad_up = mm_rows(normed_two, grad_pre).astype(bf16)

    def between(place_ref, given, held, made, scratch, sems):
        grad_ref, own_ref, other_ref, middle_ref, scales_ref = given
        middle_grad_ref, branch_ref, attended_ref, sums_ref = made
        (weight,) = scratch

        @pl.when(pl.program_id(0) == 0)
        def _():
            sums_ref[...] = jnp.zeros_like(sums_ref)
            for copy in load_out(place_ref, held[0], weight, sems):
                copy.wait()

        unit_rows, inverse = unit_of(middle_ref[...])
        back_rows = own_ref[...].astype(f32) + other_ref[...].astype(f32)
        sums_ref[0:1, :] += jnp.sum(back_rows * unit_rows, axis=0, keepdims=True)
        sums_ref[1:2, :] += jnp.sum(back_rows, axis=0, keepdims=True)
        grads = grad_ref[...].astype(f32) + unit_back(back_rows * scales_ref[2:3, :], unit_rows, inverse)
        middle_grad_ref[...] = grads
        low = grads.astype(bf16)
        branch_ref[...] = low
        attended_ref[...] = mm_cols(low, out_weight(weight, place_ref)).astype(bf16)

    grad_middle, grad_branch, grad_attended, sums_two = weight_call(
        "between",
        between,
        tiles,
        place,
        [
            (grad_result, row_block(tile, model)),
            (back, row_block(tile, model)),
            (back_other, row_block(tile, model)),
            (middle, row_block(tile, model)),
            (scales, whole_block(8, model)),
        ],
        [out_set],
        [
            (shape_of(rows, model, dtype=f32), row_block(tile, model)),
            (shape_of(rows, model), row_block(tile, model)),
            (shape_of(rows, head_columns), row_block(tile, head_columns)),
            (shape_of(8, model, dtype=f32), whole_block(8, model)),
        ],
        [pltpu.VMEM((out_rows * shards, model), bf16)],
        copies,
        2 * rows * model * head_columns,
    )
    grad_joint = attend_back(joint, grad_attended, lse, seg_col, seg_row)
    grad_out = mm_rows(attended, grad_branch).astype(bf16)

    def enter(place_ref, given, held, made, scratch, sems):
        (rows_ref,), (out_ref,), (weight,) = given, made, scratch

        @pl.when(pl.program_id(0) == 0)
        def _():
            targets = [(0, 3 * head_columns, below(weight, half_rows))]
            for copy in load(first_set[0], depth, place_ref, held[0], sems, targets):
                copy.wait()

        out_ref[...] = mm_cols(rows_ref[...], weight[...]).astype(bf16)

    (entered,) = weight_call(
        "enter",
        enter,
        tiles,
        place,
        [(grad_joint, row_block(tile, 3 * head_columns))],
        [first_set],
        [(shape_of(rows, model), row_block(tile, model))],
        [pltpu.VMEM((model, 3 * head_columns), bf16)],
        copies,
        6 * rows * model * head_columns,
    )
    grad_qkv = mm_rows(normed, grad_joint).astype(bf16)

    output = placed((own_chunks(middle) + sum_own(result)).astype(bf16))
    grad_normed = sum_own(entered)
    unit_own, inverse_own = unit_of(own_chunks(inputs).astype(f32))
    grad_gain_one = jnp.sum(grad_normed * unit_own, axis=(0, 1))
    grad_bias_one = jnp.sum(grad_normed, axis=(0, 1))
    grad_tokens = placed(own_chunks(grad_middle) + unit_back(grad_normed * scales[0], unit_own, inverse_own))

    if not split_out:
        empty = jnp.zeros((model, model), bf16)
        grad_out = lax.dynamic_update_slice_in_dim(empty, grad_out, lo * head_columns, 0)
    down_own = reduce(grad_down, depth)
    up_own = reduce(grad_up, depth)
    out_own = reduce(grad_out, depth)
    qkv_own = reduce(grad_qkv, depth)

    down_all = whole_group(down_own, 0).reshape(-1, model).astype(f32)
    up_all = whole_group(up_own.reshape(own_rows, shards, -1), 2).reshape(own_rows, -1).astype(f32)
    if split_out:
        out_all = whole_group(out_own, 0).reshape(own_rows, model).astype(f32)
        qkv_all = whole_group(qkv_own.reshape(own_rows, 3, shards, -1), 3)
    else:
        out_all = lax.psum(out_own, "lo").astype(f32)
        qkv_all = whole_group(qkv_own.reshape(own_rows, 3, -1), 2)
    qkv_all = qkv_all.reshape(own_rows, -1).astype(f32)

    once = jnp.where(lo == 0, 1.0, 0.0).astype(f32)
    sums = jnp.stack([grad_gain_one, grad_bias_one, sums_two[0] * once, sums_two[1] * once])
    sums = lax.psum(sums, ("hi", "lo", "fz", "fx")).reshape(4, shards, own_rows)
    sums = pick(sums, z * 2 + x, 1)

    return (
        output,
        grad_tokens,
        sums[0],
        sums[1],
        qkv_all,
        out_all,
        sums[2],
        sums[3],
        up_all,
        down_all,
    )


def solution(mesh):
    seq, fsdp = mesh.shape["seq"], mesh.shape["fsdp"]
    group, depth = seq // 2, fsdp // 2
    fine = Mesh(mesh.devices.reshape(2, group, depth, 2), ("hi", "lo", "fz", "fx"))
    s, f = ("hi", "lo"), ("fz", "fx")
    return jax.shard_map(
        functools.partial(body, group, depth),
        mesh=fine,
        in_specs=(
            P(None, f, s, None),
            P(None, f, None),
            P(f),
            P(f),
            P(f, None),
            P(f, None),
            P(f),
            P(f),
            P(f, None),
            P(f, None),
            P(None, f, s, None),
        ),
        out_specs=(
            P(None, f, s, None),
            P(None, f, s, None),
            P(f),
            P(f),
            P(f, None),
            P(f, None),
            P(f),
            P(f),
            P(f, None),
            P(f, None),
        ),
        check_vma=False,
    )
```

```python
import functools
import math

import jax
import jax.numpy as jnp
from jax import lax
from jax.experimental import pallas as pl
from jax.experimental.pallas import tpu as pltpu
from jax.sharding import Mesh
from jax.sharding import PartitionSpec as P

HEAD_DIM = 64
DOC_MOST = 512
TILE = 256
LANES = 128
epsilon = 1e-05
SWAP = [(0, 1), (1, 0)]
f32 = jnp.float32
bf16 = jnp.bfloat16


def dot(left, right, dims):
    return lax.dot_general(left, right, (dims, ((), ())), preferred_element_type=f32)


def mm(left, right):
    return dot(left, right, ((1,), (0,)))


def mm_rows(left, right):
    return dot(left, right, ((0,), (0,)))


def mm_cols(left, right):
    return dot(left, right, ((1,), (1,)))


def cost(micros):
    return pl.CostEstimate(flops=int(micros * 1.1e9), bytes_accessed=1, transcendentals=0)


def sync(*values):
    return lax.optimization_barrier(values)


def pick(array, index, axis):
    return lax.dynamic_index_in_dim(array, index, axis, keepdims=False)


def swap(value, axis):
    return lax.ppermute(value, axis, SWAP)


def ordered(own, other, index, axis):
    first = jnp.where(index == 0, own, other)
    second = jnp.where(index == 0, other, own)
    return jnp.stack([first, second], axis)


def tile_spans(rows):
    tile = min(TILE, rows)
    spans = []
    for start in range(0, rows, tile):
        low = max(0, (start - DOC_MOST + 1) // tile * tile)
        spans.append((start, low, start + tile))
    return tile, spans


def fill_bias(bias, seg_col, seg_row, spans, tile):
    for i, (start, low, high) in enumerate(spans):
        width = high - low
        query_pos = start + lax.broadcasted_iota(jnp.int32, (tile, width), 0)
        key_pos = low + lax.broadcasted_iota(jnp.int32, (tile, width), 1)
        same = seg_col[start : start + tile, :] == seg_row[:, low:high]
        allowed = (key_pos <= query_pos) & same
        bias[i, :, :width] = jnp.where(allowed, 0.0, -1e30).astype(f32)


def attend_kernel(spans, tile, q_ref, k_ref, v_ref, seg_col, seg_row, out_ref, lse_ref, bias):
    @pl.when(pl.program_id(0) == 0)
    def _():
        fill_bias(bias, seg_col, seg_row, spans, tile)

    left = lax.broadcasted_iota(jnp.int32, (tile, LANES), 1) < HEAD_DIM
    for i, (start, low, high) in enumerate(spans):
        rows = slice(start, start + tile)
        queries = q_ref[rows, :]
        keys, values = k_ref[low:high, :], v_ref[low:high, :]
        mixed, logs = [], []
        for half in (left, ~left):
            scores = mm_cols(jnp.where(half, queries, jnp.zeros_like(queries)), keys)
            scores = scores + bias[i, :, : high - low]
            top = jnp.max(scores, axis=-1, keepdims=True)
            powers = jnp.exp(scores - top)
            total = jnp.sum(powers, axis=-1, keepdims=True)
            mixed.append(mm((powers * (1.0 / total)).astype(bf16), values))
            logs.append(top + jnp.log(total))
        out_ref[rows, :] = jnp.where(left, mixed[0], mixed[1]).astype(bf16)
        lse_ref[rows, :] = jnp.where(left, logs[0], logs[1])


def attend(joint, seg_col, seg_row):
    rows, width = joint.shape[0], joint.shape[1] // 3
    pairs = width // LANES
    tile, spans = tile_spans(rows)
    widest = max(high - low for _, low, high in spans)

    def part(which):
        return pl.BlockSpec((rows, LANES), lambda p: (0, which * pairs + p))

    return pl.pallas_call(
        functools.partial(attend_kernel, spans, tile),
        grid=(pairs,),
        in_specs=[
            part(0),
            part(1),
            part(2),
            pl.BlockSpec((rows, 1), lambda p: (0, 0)),
            pl.BlockSpec((1, rows), lambda p: (0, 0)),
        ],
        out_specs=[part(0), part(0)],
        out_shape=[
            jax.ShapeDtypeStruct((rows, width), bf16),
            jax.ShapeDtypeStruct((rows, width), f32),
        ],
        scratch_shapes=[pltpu.VMEM((len(spans), tile, widest), f32)],
        compiler_params=pltpu.CompilerParams(vmem_limit_bytes=40 * 1024 * 1024),
        cost_estimate=cost(4.3 * pairs),
        name="attend",
    )(joint, joint, joint, seg_col, seg_row)


def attend_back_kernel(
    spans, tile, q_ref, k_ref, v_ref, g_ref, lse_ref, seg_col, seg_row, out_ref, bias, keys_sum, values_sum
):
    @pl.when((pl.program_id(0) == 0) & (pl.program_id(1) == 0))
    def _():
        fill_bias(bias, seg_col, seg_row, spans, tile)

    @pl.when(pl.program_id(1) == 0)
    def _():
        keys_sum[...] = jnp.zeros_like(keys_sum)
        values_sum[...] = jnp.zeros_like(values_sum)
        left = lax.broadcasted_iota(jnp.int32, (tile, LANES), 1) < HEAD_DIM
        for i, (start, low, high) in enumerate(spans):
            rows = slice(start, start + tile)
            queries, grads = q_ref[rows, :], g_ref[rows, :]
            keys, values = k_ref[low:high, :], v_ref[low:high, :]
            parts = []
            for half, lane in ((left, 0), (~left, HEAD_DIM)):
                own_queries = jnp.where(half, queries, jnp.zeros_like(queries))
                own_grads = jnp.where(half, grads, jnp.zeros_like(grads))
                scores = mm_cols(own_queries, keys) + bias[i, :, : high - low]
                probs = jnp.exp(scores - lse_ref[rows, lane : lane + 1])
                grad_probs = mm_cols(own_grads, values)
                inner = jnp.sum(probs * grad_probs, axis=-1, keepdims=True)
                grad_scores = (probs * (grad_probs - inner)).astype(bf16)
                parts.append(mm(grad_scores, keys))
                keys_sum[low:high, :] += mm_rows(grad_scores, own_queries)
                values_sum[low:high, :] += mm_rows(probs.astype(bf16), own_grads)
            grad_queries = jnp.where(left, parts[0], parts[1]).astype(bf16)
            out_ref[rows, :] = grad_queries * jnp.asarray(1.0 / math.sqrt(HEAD_DIM), bf16)

    @pl.when(pl.program_id(1) == 1)
    def _():
        out_ref[...] = keys_sum[...].astype(bf16)

    @pl.when(pl.program_id(1) == 2)
    def _():
        out_ref[...] = values_sum[...].astype(bf16)


def attend_back(joint, grads, lse, seg_col, seg_row, begin, count):
    rows, width = joint.shape[0], joint.shape[1] // 3
    pairs = width // LANES
    tile, spans = tile_spans(rows)
    widest = max(high - low for _, low, high in spans)

    def part(which):
        return pl.BlockSpec((rows, LANES), lambda p, j: (0, which * pairs + begin + p))

    return pl.pallas_call(
        functools.partial(attend_back_kernel, spans, tile),
        grid=(count, 3),
        in_specs=[
            part(0),
            part(1),
            part(2),
            part(0),
            part(0),
            pl.BlockSpec((rows, 1), lambda p, j: (0, 0)),
            pl.BlockSpec((1, rows), lambda p, j: (0, 0)),
        ],
        out_specs=pl.BlockSpec((rows, LANES), lambda p, j: (0, j * count + p)),
        out_shape=jax.ShapeDtypeStruct((rows, 3 * count * LANES), bf16),
        scratch_shapes=[
            pltpu.VMEM((len(spans), tile, widest), f32),
            pltpu.VMEM((rows, LANES), f32),
            pltpu.VMEM((rows, LANES), f32),
        ],
        compiler_params=pltpu.CompilerParams(vmem_limit_bytes=48 * 1024 * 1024),
        cost_estimate=cost(7.5 * count),
        name="attend_back",
    )(joint, joint, joint, grads, lse, seg_col, seg_row)


def along(value, axis, depth, step):
    return lax.ppermute(value, axis, [(i, (i + step) % depth) for i in range(depth)])


def load(depth, place, pieces, sems, targets):
    z, x, h = place[0], place[1], place[2]
    copies = []

    def put(source, shard, half):
        for first, columns, where in targets:
            taken = source if columns == source.shape[1] else source.at[:, first : first + columns]
            copies.append(pltpu.make_async_copy(taken, where(shard, half), sems.at[len(copies)]))
            copies[-1].start()

    for at_x, piece in ((x, pieces[0]), (1 - x, pieces[1])):
        for half in range(2):
            put(piece.at[half], z * 2 + at_x, half)
    for at_x, at_h, piece in ((x, h, pieces[2]), (1 - x, h, pieces[3]), (x, 1 - h, pieces[4]), (1 - x, 1 - h, pieces[5])):
        for k in range(1, depth):
            put(piece.at[k - 1], lax.rem(z - k + depth, depth) * 2 + at_x, at_h)
    return copies


def below(weight, half_rows):
    def where(shard, half):
        return weight.at[pl.ds(pl.multiple_of((shard * 2 + half) * half_rows, half_rows), half_rows), :]

    return where


def plus(left, right):
    return (left.astype(f32) + right.astype(f32)).astype(bf16)


def cut(full, depth, x, h):
    rows, columns = full.shape[0] // (2 * depth), full.shape[1]
    view = full.reshape(depth, 2, 2, 2, rows // 4, columns)
    first, second = view[:, :, 0], view[:, :, 1]
    keep = pick(first, x, 1), pick(second, h, 2)
    send = pick(first, 1 - x, 1), pick(second, 1 - h, 2)
    return keep, send


def cut_again(keep, came, x, h):
    first, second = plus(keep[0], came[0]), plus(keep[1], came[1])
    keep = pick(first, h, 1), pick(second, x, 1)
    send = pick(first, 1 - h, 1), pick(second, 1 - x, 1)
    return keep, send


def along_z(keep, came, depth, z):
    both = jnp.stack([plus(keep[0], came[0]), plus(keep[1], came[1])], 1)
    return pick(both, z, 0), [pick(both, (z + k) % depth, 0) for k in range(1, depth)]


def add_up(own, came):
    total = own.astype(f32)
    for piece in came:
        total = total + piece.astype(f32)
    return total.astype(bf16)


def row_block(tile, width):
    return pl.BlockSpec((tile, width), lambda i: (i, 0))


def whole_block(*shape):
    return pl.BlockSpec(shape, lambda i: (0,) * len(shape))


def weight_call(name, step, tiles, place, inputs, sets, outs, scratch, copies, micros):
    pieces = [piece for held in sets for piece in held]

    def kernel(place_ref, *refs):
        refs = list(refs)

        def take(count):
            taken = refs[:count]
            del refs[:count]
            return taken

        given = take(len(inputs))
        held = [take(len(one)) for one in sets]
        made = take(len(outs))
        step(place_ref, given, held, made, refs[:-1], refs[-1])

    return pl.pallas_call(
        kernel,
        grid=(tiles,),
        in_specs=[pl.BlockSpec(memory_space=pltpu.SMEM)]
        + [spec for _, spec in inputs]
        + [pl.BlockSpec(memory_space=pl.ANY)] * len(pieces),
        out_specs=[spec for _, spec in outs],
        out_shape=[shape for shape, _ in outs],
        scratch_shapes=list(scratch) + [pltpu.SemaphoreType.DMA((copies,))],
        compiler_params=pltpu.CompilerParams(vmem_limit_bytes=56 * 1024 * 1024),
        cost_estimate=cost(micros),
        name=name,
    )(place, *[v for v, _ in inputs], *pieces)


def shape_of(*shape, dtype=bf16):
    return jax.ShapeDtypeStruct(shape, dtype)


def unit_of(values):
    centred = values - jnp.mean(values, axis=-1, keepdims=True)
    variance = jnp.mean(centred * centred, axis=-1, keepdims=True)
    inverse = lax.rsqrt(variance + epsilon)
    return centred * inverse, inverse


def unit_back(grad_unit, unit_rows, inverse):
    mean_grad = jnp.mean(grad_unit, axis=-1, keepdims=True)
    mean_cross = jnp.mean(grad_unit * unit_rows, axis=-1, keepdims=True)
    return inverse * (grad_unit - mean_grad - unit_rows * mean_cross)


def bell_and_slope(values):
    size = jnp.abs(values)
    t = 1.0 / (1.0 + (0.3275911 * math.sqrt(0.5)) * size)
    bell = jnp.exp(values * values * -0.5)
    series = 0.5 * 1.061405429
    for term in (-1.453152027, 1.421413741, -0.284496736, 0.254829592):
        series = series * t + 0.5 * term
    tail = series * t * bell
    phi = jnp.where(values < 0, tail, 1.0 - tail)
    return values * phi, phi + values * bell * (1.0 / math.sqrt(2.0 * math.pi))


def body(
    group,
    depth,
    tokens,
    segment_ids,
    norm1_gain,
    norm1_bias,
    w_qkv,
    w_out,
    norm2_gain,
    norm2_bias,
    w_up,
    w_down,
    cotangent,
):
    h, lo = lax.axis_index("hi"), lax.axis_index("lo")
    z, x = lax.axis_index("fz"), lax.axis_index("fx")
    micro, _, chunk, model = tokens.shape
    shards = 2 * depth
    rows = micro * group * chunk
    own_rows = w_out.shape[0]
    inner = w_up.shape[1] // group
    split_out = (own_rows // HEAD_DIM) % group == 0
    head_columns = model // group
    half_rows = own_rows // 2
    tile = min(TILE, rows)
    tiles = rows // tile
    scale_at = 3 * head_columns
    copies = 4 * shards
    wide = min(512, inner)
    shard_axes = ("fz", "fx")

    def whole_group(value, axis):
        if group == 2:
            return ordered(value, swap(value, "lo"), lo, axis)
        return lax.all_gather(value, "lo", axis=axis)

    def other_part(partial):
        if group == 2:
            return swap(partial, "lo")
        return (lax.psum(partial, "lo").astype(f32) - partial.astype(f32)).astype(bf16)

    def own_chunks(full):
        return pick(full.reshape(micro, group, chunk, -1), lo, 1)

    def other_own(partial):
        parts = partial.reshape(micro, group, chunk, model)
        if group == 2:
            return swap(pick(parts, 1 - lo, 1), "lo")
        return plus(lax.psum_scatter(parts, "lo", scatter_dimension=1), -pick(parts, lo, 1))

    if split_out:
        qkv_part = pick(w_qkv.reshape(own_rows, 3, shards, group, -1), lo, 3).reshape(own_rows, -1)
        out_part = pick(w_out.reshape(group, own_rows // group, model), lo, 0)
    else:
        qkv_part = pick(w_qkv.reshape(own_rows, 3, group, -1), lo, 2).reshape(own_rows, -1)
        out_part = w_out
    up_part = pick(w_up.reshape(own_rows, shards, group, -1), lo, 2).reshape(own_rows, -1)
    down_part = pick(w_down.reshape(group, -1, model), lo, 0)
    vectors = jnp.stack([norm1_gain, norm1_bias, norm2_gain, norm2_bias], axis=1)
    first_part = jnp.concatenate([qkv_part, jnp.pad(vectors, ((0, 0), (0, LANES - 4)))], axis=1)
    place = jnp.stack([z, x, h, lo]).astype(jnp.int32)
    first_own = first_part.reshape(2, half_rows, -1)
    up_own = up_part.reshape(2, half_rows, -1)
    rest = range(1, depth)

    out_weight = lax.all_gather(out_part, shard_axes, axis=0, tiled=True)
    first_half = pick(first_own, h, 0)
    first_far = [along(first_half, "fz", depth, k) for k in rest]
    first_side_own = swap(first_own, "fx")
    came = swap(pick(tokens[:, 0], 1 - h, 0), "hi")
    first_far, first_side_own, came, up_own, tokens = sync(
        first_far, first_side_own, came, up_own, tokens
    )

    first_far = jnp.stack(first_far)
    first_side, first_near = swap(first_far, "fx"), swap(first_far, "hi")
    inputs = whole_group(ordered(pick(tokens[:, 0], h, 0), came, h, 0), 1).reshape(rows, model)
    up_half = pick(up_own, h, 0)
    odd = [along(up_half, "fz", depth, k) for k in rest if k % 2]
    first_side, first_near, inputs, odd, up_half, up_own, down_part = sync(
        first_side, first_near, inputs, odd, up_half, up_own, down_part
    )

    downward = lax.all_gather(down_part, shard_axes, axis=0, tiled=True)
    first_last = swap(first_side, "hi")
    up_side_own = swap(up_own, "fx")
    even = [along(up_half, "fz", depth, k) for k in rest if k % 2 == 0]
    first_last, up_side_own, even, odd, inputs = sync(first_last, up_side_own, even, odd, inputs)
    first_set = [first_own, first_side_own, first_far, first_side, first_near, first_last]
    up_far = jnp.stack([odd[k // 2] if k % 2 else even[k // 2 - 1] for k in rest])

    segments = pick(segment_ids[:, 0], h, 0)
    seg_col, seg_row = segments[:, None], segments[None, :]

    def project(place_ref, given, held, made, scratch, sems):
        (rows_ref,), (normed_ref, joint_ref, scales_ref) = given, made
        weight, columns = scratch

        @pl.when(pl.program_id(0) == 0)
        def _():
            targets = [
                (0, 3 * head_columns, below(weight, half_rows)),
                (scale_at, LANES, below(columns, half_rows)),
            ]
            for copy in load(depth, place_ref, held[0], sems, targets):
                copy.wait()
            scales_ref[...] = columns[...].astype(f32).T[:8, :]

        unit_rows, _ = unit_of(rows_ref[...].astype(f32))
        normed = (unit_rows * scales_ref[0:1, :] + scales_ref[1:2, :]).astype(bf16)
        normed_ref[...] = normed
        for at in range(0, 3 * head_columns, head_columns):
            part = mm(normed, weight[:, at : at + head_columns])
            if at == 0:
                part = part * (1.0 / math.sqrt(HEAD_DIM))
            joint_ref[:, at : at + head_columns] = part.astype(bf16)

    normed, joint, scales = weight_call(
        "project",
        project,
        tiles,
        place,
        [(inputs, row_block(tile, model))],
        [first_set],
        [
            (shape_of(rows, model), row_block(tile, model)),
            (shape_of(rows, 3 * head_columns), row_block(tile, 3 * head_columns)),
            (shape_of(8, model, dtype=f32), whole_block(8, model)),
        ],
        [pltpu.VMEM((model, 3 * head_columns), bf16), pltpu.VMEM((model, LANES), bf16)],
        copies,
        9,
    )
    attended, lse = attend(joint, seg_col, seg_row)
    up_side, up_near = swap(up_far, "fx"), swap(up_far, "hi")
    attended, up_side, up_near, cotangent = sync(attended, up_side, up_near, cotangent)

    def leave(place_ref, given, held, made, scratch, sems):
        (rows_ref, weight), (out_ref,) = given, made
        out_ref[...] = mm(rows_ref[...], own_out(weight, place_ref)).astype(bf16)

    def own_out(weight, place_ref):
        if split_out:
            return weight[...]
        return weight[pl.ds(pl.multiple_of(place_ref[3] * head_columns, head_columns), head_columns), :]

    (branch,) = weight_call(
        "leave",
        leave,
        tiles,
        place,
        [(attended, row_block(tile, head_columns)), (out_weight, whole_block(*out_weight.shape))],
        [],
        [(shape_of(rows, model), row_block(tile, model))],
        [],
        1,
        4,
    )
    branch_other = other_part(branch)
    up_last = swap(up_side, "hi")
    came = swap(pick(cotangent[:, 0], 1 - h, 0), "hi")
    branch, branch_other, up_last, cotangent = sync(branch, branch_other, up_last, cotangent)
    up_set = [up_own, up_side_own, up_far, up_side, up_near, up_last]

    grad_result = whole_group(ordered(pick(cotangent[:, 0], h, 0), came, h, 0), 1).reshape(rows, model)

    def widen(place_ref, given, held, made, scratch, sems):
        rows_ref, own_ref, other_ref, scales_ref = given
        middle_ref, normed_ref, hidden_ref, slope_ref = made
        (weight,) = scratch

        @pl.when(pl.program_id(0) == 0)
        def _():
            targets = [(0, inner, below(weight, half_rows))]
            for copy in load(depth, place_ref, held[0], sems, targets):
                copy.wait()

        added = own_ref[...].astype(f32) + other_ref[...].astype(f32)
        middle = rows_ref[...].astype(f32) + added
        middle_ref[...] = middle
        unit_rows, _ = unit_of(middle)
        normed = (unit_rows * scales_ref[2:3, :] + scales_ref[3:4, :]).astype(bf16)
        normed_ref[...] = normed
        for at in range(0, inner, wide):
            hidden, slope = bell_and_slope(mm(normed, weight[:, at : at + wide]))
            hidden_ref[:, at : at + wide] = hidden.astype(bf16)
            slope_ref[:, at : at + wide] = slope.astype(bf16)

    middle, normed_two, hidden, slope = weight_call(
        "widen",
        widen,
        tiles,
        place,
        [
            (inputs, row_block(tile, model)),
            (branch, row_block(tile, model)),
            (branch_other, row_block(tile, model)),
            (scales, whole_block(8, model)),
        ],
        [up_set],
        [
            (shape_of(rows, model, dtype=f32), row_block(tile, model)),
            (shape_of(rows, model), row_block(tile, model)),
            (shape_of(rows, inner), row_block(tile, inner)),
            (shape_of(rows, inner), row_block(tile, inner)),
        ],
        [pltpu.VMEM((model, inner), bf16)],
        copies,
        18,
    )
    hidden, slope, grad_result = sync(hidden, slope, grad_result)

    grad_down = mm_rows(hidden, grad_result).astype(bf16)
    hidden, slope, grad_down = sync(hidden, slope, grad_down)
    down_own = lax.psum_scatter(grad_down, shard_axes, scatter_dimension=0, tiled=True)

    def narrow(place_ref, given, held, made, scratch, sems):
        hidden_ref, grad_ref, slope_ref, down_ref = given
        out_ref, pre_ref, back_ref = made
        (upward,) = scratch

        @pl.when(pl.program_id(0) == 0)
        def _():
            targets = [(0, inner, below(upward, half_rows))]
            for copy in load(depth, place_ref, held[0], sems, targets):
                copy.wait()

        out_ref[...] = mm(hidden_ref[...], down_ref[...]).astype(bf16)
        total = jnp.zeros(back_ref.shape, f32)
        for at in range(0, inner, wide):
            grad = mm_cols(grad_ref[...], down_ref[at : at + wide, :])
            grad = (grad * slope_ref[:, at : at + wide].astype(f32)).astype(bf16)
            pre_ref[:, at : at + wide] = grad
            total = total + mm_cols(grad, upward[:, at : at + wide])
        back_ref[...] = total.astype(bf16)

    result, grad_pre, back = weight_call(
        "narrow",
        narrow,
        tiles,
        place,
        [
            (hidden, row_block(tile, inner)),
            (grad_result, row_block(tile, model)),
            (slope, row_block(tile, inner)),
            (downward, whole_block(inner, model)),
        ],
        [up_set],
        [
            (shape_of(rows, model), row_block(tile, model)),
            (shape_of(rows, inner), row_block(tile, inner)),
            (shape_of(rows, model), row_block(tile, model)),
        ],
        [pltpu.VMEM((model, inner), bf16)],
        copies,
        21,
    )
    result, grad_pre, back = sync(result, grad_pre, back)

    back_other = other_part(back)
    grad_up = mm_rows(normed_two, grad_pre).astype(bf16)
    up_keep, up_send = cut(grad_up, depth, x, h)
    back, back_other, up_keep, up_send, result = sync(back, back_other, up_keep, up_send, result)

    pairs = head_columns // LANES
    pieces = 2 if pairs % 2 == 0 else 1
    count = pairs // pieces

    def between(place_ref, given, held, made, scratch, sems):
        grad_ref, own_ref, other_ref, middle_ref, scales_ref, weight = given
        middle_grad_ref, branch_ref, attended_ref, sums_ref = made

        @pl.when(pl.program_id(0) == 0)
        def _():
            sums_ref[...] = jnp.zeros_like(sums_ref)

        unit_rows, inverse = unit_of(middle_ref[...])
        own_back = own_ref[...].astype(f32)
        back_rows = own_back + other_ref[...].astype(f32)
        sums_ref[0:1, :] += jnp.sum(own_back * unit_rows, axis=0, keepdims=True)
        sums_ref[1:2, :] += jnp.sum(own_back, axis=0, keepdims=True)
        grads = grad_ref[...].astype(f32) + unit_back(back_rows * scales_ref[2:3, :], unit_rows, inverse)
        middle_grad_ref[...] = grads
        low = grads.astype(bf16)
        branch_ref[...] = low
        attended_ref[...] = mm_cols(low, own_out(weight, place_ref)).astype(bf16)

    grad_middle, grad_branch, grad_attended, sums_two = weight_call(
        "between",
        between,
        tiles,
        place,
        [
            (grad_result, row_block(tile, model)),
            (back, row_block(tile, model)),
            (back_other, row_block(tile, model)),
            (middle, row_block(tile, model)),
            (scales, whole_block(8, model)),
            (out_weight, whole_block(*out_weight.shape)),
        ],
        [],
        [
            (shape_of(rows, model, dtype=f32), row_block(tile, model)),
            (shape_of(rows, model), row_block(tile, model)),
            (shape_of(rows, head_columns), row_block(tile, head_columns)),
            (shape_of(8, model, dtype=f32), whole_block(8, model)),
        ],
        [],
        1,
        10,
    )
    grad_joints = [attend_back(joint, grad_attended, lse, seg_col, seg_row, 0, count)]
    up_came = swap(up_send[0], "fx"), swap(up_send[1], "hi")
    result_other = other_own(result)
    grad_joints, grad_attended, grad_branch, up_came, result_other = sync(
        grad_joints, grad_attended, grad_branch, up_came, result_other
    )

    grad_out = mm_rows(attended, grad_branch).astype(bf16)
    if not split_out:
        empty = jnp.zeros((model, model), bf16)
        grad_out = lax.dynamic_update_slice_in_dim(empty, grad_out, lo * head_columns, 0)
    up_keep, up_send = cut_again(up_keep, up_came, x, h)
    for piece in range(1, pieces):
        grad_joints.append(
            attend_back(joint, grad_attended, lse, seg_col, seg_row, piece * count, count)
        )
    fused_out = split_out and group == 2
    parts = [mm_rows(normed, grad_joints[0]).astype(bf16)]
    if fused_out:
        halves = grad_out.reshape(shards, own_rows // group, group, model // group).transpose(0, 2, 1, 3)
        parts.append(halves.reshape(model, model // group))
    one_keep, one_send = cut(jnp.concatenate(parts, axis=1), depth, x, h)
    up_came = swap(up_send[0], "hi"), swap(up_send[1], "fx")
    grad_joints, up_came, one_keep, one_send = sync(grad_joints, up_came, one_keep, one_send)

    up_own_sum, up_send = along_z(up_keep, up_came, depth, z)
    one_came = swap(one_send[0], "fx"), swap(one_send[1], "hi")
    up_came = [along(value, "fz", depth, k) for k, value in zip(rest, up_send)]
    part_columns = count * LANES

    def enter(place_ref, given, held, made, scratch, sems):
        *parts_refs, inputs_ref = given
        (out_ref, sums_ref), (weight,) = made, scratch

        @pl.when(pl.program_id(0) == 0)
        def _():
            sums_ref[...] = jnp.zeros_like(sums_ref)
            targets = [(0, 3 * head_columns, below(weight, half_rows))]
            for copy in load(depth, place_ref, held[0], sems, targets):
                copy.wait()

        unit_rows, _ = unit_of(inputs_ref[...].astype(f32))
        grads = jnp.zeros(out_ref.shape, f32)
        for piece, part_ref in enumerate(parts_refs):
            for j in range(3):
                at = j * head_columns + piece * part_columns
                grads = grads + mm_cols(
                    part_ref[:, j * part_columns : (j + 1) * part_columns], weight[:, at : at + part_columns]
                )
        out_ref[...] = grads.astype(bf16)
        sums_ref[0:1, :] += jnp.sum(grads * unit_rows, axis=0, keepdims=True)
        sums_ref[1:2, :] += jnp.sum(grads, axis=0, keepdims=True)

    entered, sums_one = weight_call(
        "enter",
        enter,
        tiles,
        place,
        [(value, row_block(tile, 3 * part_columns)) for value in grad_joints] + [(inputs, row_block(tile, model))],
        [first_set],
        [
            (shape_of(rows, model), row_block(tile, model)),
            (shape_of(8, model, dtype=f32), whole_block(8, model)),
        ],
        [pltpu.VMEM((model, 3 * head_columns), bf16)],
        copies,
        9,
    )
    sums = jnp.stack([sums_one[0], sums_one[1], sums_two[0], sums_two[1]], axis=1).astype(bf16)
    parts = [mm_rows(normed, value).astype(bf16) for value in grad_joints[1:]]
    parts.append(jnp.pad(sums, ((0, 0), (0, LANES - 4))))
    two_keep, two_send = cut(jnp.concatenate(parts, axis=1), depth, x, h)
    entered, one_came, up_came, two_keep, two_send, down_own = sync(
        entered, one_came, up_came, two_keep, two_send, down_own
    )

    one_keep, one_send = cut_again(one_keep, one_came, x, h)
    one_came = swap(one_send[0], "hi"), swap(one_send[1], "fx")
    two_came = swap(two_send[0], "fx"), swap(two_send[1], "hi")
    up_sum = add_up(up_own_sum, up_came)
    entered_other = other_own(entered)
    output = (own_chunks(middle) + own_chunks(result).astype(f32) + result_other.astype(f32)).astype(bf16)
    entered_other, one_came, two_came, up_sum, output, down_own = sync(
        entered_other, one_came, two_came, up_sum, output, down_own
    )

    one_own_sum, one_send = along_z(one_keep, one_came, depth, z)
    one_came = [along(value, "fz", depth, k) for k, value in zip(rest, one_send)]
    two_keep, two_send = cut_again(two_keep, two_came, x, h)
    two_came = swap(two_send[0], "hi"), swap(two_send[1], "fx")
    grad_normed = own_chunks(entered).astype(f32) + entered_other.astype(f32)
    unit_own, inverse_own = unit_of(own_chunks(inputs).astype(f32))
    grad_tokens = own_chunks(grad_middle) + unit_back(grad_normed * scales[0], unit_own, inverse_own)
    one_came, two_came, grad_tokens, output, up_sum, down_own = sync(
        one_came, two_came, grad_tokens, output, up_sum, down_own
    )

    two_own_sum, two_send = along_z(two_keep, two_came, depth, z)
    two_came = [along(value, "fz", depth, k) for k, value in zip(rest, two_send)]
    one_sum = add_up(one_own_sum, one_came)
    grad_came = swap(pick(grad_tokens, 1 - h, 0).astype(bf16), "hi").astype(f32)
    output_came = swap(pick(output, 1 - h, 0), "hi")
    two_came, one_sum, grad_came, output_came, up_sum, down_own = sync(
        two_came, one_sum, grad_came, output_came, up_sum, down_own
    )
    output = ordered(pick(output, h, 0), output_came, h, 0)[:, None]
    grad_tokens = ordered(pick(grad_tokens, h, 0), grad_came, h, 0)[:, None]

    down_own = plus(down_own, swap(down_own, "hi"))
    two_sum = add_up(two_own_sum, two_came)

    def both_halves(value):
        return ordered(value, swap(value, "hi"), h, 1).reshape(own_rows, -1)

    up_own, one_own, two_own = both_halves(up_sum), both_halves(one_sum), both_halves(two_sum)
    down_all = whole_group(down_own, 0).reshape(-1, model).astype(f32)
    up_all = whole_group(up_own.reshape(own_rows, shards, -1), 2).reshape(own_rows, -1).astype(f32)
    qkv_owns = [one_own[:, : 3 * part_columns]]
    if pieces == 2:
        qkv_owns.append(two_own[:, : 3 * part_columns])
    sums_own = two_own[:, -LANES : 4 - LANES]
    sums = jnp.sum(whole_group(sums_own, 0).astype(f32), axis=0).T
    if fused_out:
        out_own = one_own[:, 3 * part_columns :].reshape(group, own_rows // group, -1)
        out_all = whole_group(out_own, 0).transpose(0, 2, 1, 3).reshape(own_rows, model).astype(f32)
    else:
        out_own = lax.psum(lax.psum_scatter(grad_out, shard_axes, scatter_dimension=0, tiled=True), "hi")
        out_all = whole_group(out_own, 0).reshape(own_rows, model) if split_out else lax.psum(out_own, "lo")
        out_all = out_all.astype(f32)
    qkv_own = jnp.concatenate([value.reshape(own_rows, 3, part_columns) for value in qkv_owns], axis=2)
    if split_out:
        qkv_all = whole_group(qkv_own.reshape(own_rows, 3, shards, -1), 3)
    else:
        qkv_all = whole_group(qkv_own, 2)
    qkv_all = qkv_all.reshape(own_rows, -1).astype(f32)

    return (
        output,
        grad_tokens,
        sums[0],
        sums[1],
        qkv_all,
        out_all,
        sums[2],
        sums[3],
        up_all,
        down_all,
    )


def solution(mesh):
    seq, fsdp = mesh.shape["seq"], mesh.shape["fsdp"]
    group, depth = seq // 2, fsdp // 2
    fine = Mesh(mesh.devices.reshape(2, group, depth, 2), ("hi", "lo", "fz", "fx"))
    s, f = ("hi", "lo"), ("fz", "fx")
    return jax.shard_map(
        functools.partial(body, group, depth),
        mesh=fine,
        in_specs=(
            P(None, f, s, None),
            P(None, f, None),
            P(f),
            P(f),
            P(f, None),
            P(f, None),
            P(f),
            P(f),
            P(f, None),
            P(f, None),
            P(None, f, s, None),
        ),
        out_specs=(
            P(None, f, s, None),
            P(None, f, s, None),
            P(f),
            P(f),
            P(f, None),
            P(f, None),
            P(f),
            P(f),
            P(f, None),
            P(f, None),
        ),
        check_vma=False,
    )
```

```python
import functools
import math

import jax
import jax.numpy as jnp
from jax import lax
from jax.experimental import pallas as pl
from jax.experimental.pallas import tpu as pltpu
from jax.sharding import Mesh
from jax.sharding import PartitionSpec as P

HEAD_DIM = 64
DOC_MOST = 512
TILE = 256
LANES = 128
epsilon = 1e-05
SWAP = [(0, 1), (1, 0)]
f32 = jnp.float32
bf16 = jnp.bfloat16


def dot(left, right, dims):
    return lax.dot_general(left, right, (dims, ((), ())), preferred_element_type=f32)


def mm(left, right):
    return dot(left, right, ((1,), (0,)))


def mm_rows(left, right):
    return dot(left, right, ((0,), (0,)))


def mm_cols(left, right):
    return dot(left, right, ((1,), (1,)))


TINY = pl.CostEstimate(flops=1000, bytes_accessed=1000, transcendentals=0)


def sync(*values):
    return lax.optimization_barrier(values)


def pick(array, index, axis):
    return lax.dynamic_index_in_dim(array, index, axis, keepdims=False)


def swap(value, axis):
    return lax.ppermute(value, axis, SWAP)


def ordered(own, other, index, axis):
    first = jnp.where(index == 0, own, other)
    second = jnp.where(index == 0, other, own)
    return jnp.stack([first, second], axis)


def tile_spans(rows):
    tile = min(TILE, rows)
    spans = []
    for start in range(0, rows, tile):
        low = max(0, (start - DOC_MOST + 1) // tile * tile)
        spans.append((start, low, start + tile))
    return tile, spans


def fill_bias(bias, seg_col, seg_row, spans, tile):
    for i, (start, low, high) in enumerate(spans):
        width = high - low
        query_pos = start + lax.broadcasted_iota(jnp.int32, (tile, width), 0)
        key_pos = low + lax.broadcasted_iota(jnp.int32, (tile, width), 1)
        same = seg_col[start : start + tile, :] == seg_row[:, low:high]
        allowed = (key_pos <= query_pos) & same
        bias[i, :, :width] = jnp.where(allowed, 0.0, -1e30).astype(f32)


def attend_kernel(spans, tile, q_ref, k_ref, v_ref, seg_col, seg_row, out_ref, lse_ref, bias):
    @pl.when(pl.program_id(0) == 0)
    def _():
        fill_bias(bias, seg_col, seg_row, spans, tile)

    left = lax.broadcasted_iota(jnp.int32, (tile, LANES), 1) < HEAD_DIM
    for i, (start, low, high) in enumerate(spans):
        rows = slice(start, start + tile)
        queries = q_ref[rows, :]
        keys, values = k_ref[low:high, :], v_ref[low:high, :]
        mixed, logs = [], []
        for half in (left, ~left):
            scores = mm_cols(jnp.where(half, queries, jnp.zeros_like(queries)), keys)
            scores = scores + bias[i, :, : high - low]
            top = jnp.max(scores, axis=-1, keepdims=True)
            powers = jnp.exp(scores - top)
            total = jnp.sum(powers, axis=-1, keepdims=True)
            mixed.append(mm((powers * (1.0 / total)).astype(bf16), values))
            logs.append(top + jnp.log(total))
        out_ref[rows, :] = jnp.where(left, mixed[0], mixed[1]).astype(bf16)
        lse_ref[rows, :] = jnp.where(left, logs[0], logs[1])


def attend(joint, seg_col, seg_row, begin, count):
    rows, width = joint.shape[0], joint.shape[1] // 3
    pairs = width // LANES
    tile, spans = tile_spans(rows)
    widest = max(high - low for _, low, high in spans)

    def part(which):
        return pl.BlockSpec((rows, LANES), lambda p: (0, which * pairs + begin + p))

    out = pl.BlockSpec((rows, LANES), lambda p: (0, p))
    return pl.pallas_call(
        functools.partial(attend_kernel, spans, tile),
        grid=(count,),
        in_specs=[
            part(0),
            part(1),
            part(2),
            pl.BlockSpec((rows, 1), lambda p: (0, 0)),
            pl.BlockSpec((1, rows), lambda p: (0, 0)),
        ],
        out_specs=[out, out],
        out_shape=[
            jax.ShapeDtypeStruct((rows, count * LANES), bf16),
            jax.ShapeDtypeStruct((rows, count * LANES), f32),
        ],
        scratch_shapes=[pltpu.VMEM((len(spans), tile, widest), f32)],
        compiler_params=pltpu.CompilerParams(vmem_limit_bytes=40 * 1024 * 1024),
        cost_estimate=TINY,
        name="attend",
    )(joint, joint, joint, seg_col, seg_row)


def attend_back_kernel(
    spans, tile, q_ref, k_ref, v_ref, g_ref, lse_ref, seg_col, seg_row, out_ref, bias, keys_sum, values_sum
):
    @pl.when((pl.program_id(0) == 0) & (pl.program_id(1) == 0))
    def _():
        fill_bias(bias, seg_col, seg_row, spans, tile)

    @pl.when(pl.program_id(1) == 0)
    def _():
        keys_sum[...] = jnp.zeros_like(keys_sum)
        values_sum[...] = jnp.zeros_like(values_sum)
        left = lax.broadcasted_iota(jnp.int32, (tile, LANES), 1) < HEAD_DIM
        for i, (start, low, high) in enumerate(spans):
            rows = slice(start, start + tile)
            queries, grads = q_ref[rows, :], g_ref[rows, :]
            keys, values = k_ref[low:high, :], v_ref[low:high, :]
            parts = []
            for half, lane in ((left, 0), (~left, HEAD_DIM)):
                own_queries = jnp.where(half, queries, jnp.zeros_like(queries))
                own_grads = jnp.where(half, grads, jnp.zeros_like(grads))
                scores = mm_cols(own_queries, keys) + bias[i, :, : high - low]
                probs = jnp.exp(scores - lse_ref[rows, lane : lane + 1])
                grad_probs = mm_cols(own_grads, values)
                inner = jnp.sum(probs * grad_probs, axis=-1, keepdims=True)
                grad_scores = (probs * (grad_probs - inner)).astype(bf16)
                parts.append(mm(grad_scores, keys))
                keys_sum[low:high, :] += mm_rows(grad_scores, own_queries)
                values_sum[low:high, :] += mm_rows(probs.astype(bf16), own_grads)
            grad_queries = jnp.where(left, parts[0], parts[1]).astype(bf16)
            out_ref[rows, :] = grad_queries * jnp.asarray(1.0 / math.sqrt(HEAD_DIM), bf16)

    @pl.when(pl.program_id(1) == 1)
    def _():
        out_ref[...] = keys_sum[...].astype(bf16)

    @pl.when(pl.program_id(1) == 2)
    def _():
        out_ref[...] = values_sum[...].astype(bf16)


def attend_back(joint, grads, lse, seg_col, seg_row, begin, count):
    rows, width = joint.shape[0], joint.shape[1] // 3
    pairs = width // LANES
    tile, spans = tile_spans(rows)
    widest = max(high - low for _, low, high in spans)

    def part(which):
        return pl.BlockSpec((rows, LANES), lambda p, j: (0, which * pairs + begin + p))

    return pl.pallas_call(
        functools.partial(attend_back_kernel, spans, tile),
        grid=(count, 3),
        in_specs=[
            part(0),
            part(1),
            part(2),
            part(0),
            pl.BlockSpec((rows, LANES), lambda p, j: (0, p)),
            pl.BlockSpec((rows, 1), lambda p, j: (0, 0)),
            pl.BlockSpec((1, rows), lambda p, j: (0, 0)),
        ],
        out_specs=pl.BlockSpec((rows, LANES), lambda p, j: (0, j * count + p)),
        out_shape=jax.ShapeDtypeStruct((rows, 3 * count * LANES), bf16),
        scratch_shapes=[
            pltpu.VMEM((len(spans), tile, widest), f32),
            pltpu.VMEM((rows, LANES), f32),
            pltpu.VMEM((rows, LANES), f32),
        ],
        compiler_params=pltpu.CompilerParams(vmem_limit_bytes=48 * 1024 * 1024),
        cost_estimate=TINY,
        name="attend_back",
    )(joint, joint, joint, grads, lse, seg_col, seg_row)


def along(value, axis, depth, step):
    return lax.ppermute(value, axis, [(i, (i + step) % depth) for i in range(depth)])


def load(depth, place, pieces, sems, targets, base=0):
    z, x, h = place[0], place[1], place[2]
    copies = []

    def put(source, shard, half, at, shift=0):
        for first, columns, where in targets:
            taken = source
            if columns != source.shape[1]:
                taken = source.at[:, shift + first : shift + first + columns]
            copies.append(pltpu.make_async_copy(taken, where(shard, half, at, source.shape[0]), sems.at[len(copies)]))
            copies[-1].start()

    own, side_own, far, side, near, last_side, last_near = pieces
    quarter = last_side.shape[1]
    for at_x, piece in ((x, own), (1 - x, side_own)):
        for half in range(2):
            put(piece.at[half], z * 2 + at_x, half, 0, base)
    for at_x, at_h, at, piece in (
        (x, h, 0, far),
        (1 - x, h, 0, side),
        (x, 1 - h, 0, near),
        (1 - x, 1 - h, 0, last_side),
        (1 - x, 1 - h, quarter, last_near),
    ):
        for k in range(1, depth):
            put(piece.at[k - 1], lax.rem(z - k + depth, depth) * 2 + at_x, at_h, at)
    return copies


def below(weight, half_rows):
    def where(shard, half, at, count):
        first = pl.multiple_of((shard * 2 + half) * half_rows + at, math.gcd(half_rows, at))
        return weight.at[pl.ds(first, count), :]

    return where


def prepare(place, shards, w_qkv, w_out, w_up, vectors):
    rows, model = w_out.shape
    half, blocks = rows // 2, w_qkv.shape[1] // LANES
    qkv_columns, wide = w_qkv.shape[1] // 2, w_up.shape[1] // 2
    scale_at = qkv_columns
    out_at = scale_at + LANES
    up_at = out_at + model // 2
    unit = wide // shards

    def kernel(place_ref, qkv_ref, out_ref, up_ref, vectors_ref, own_ref, first_ref, up_half_ref):
        lo, h = place_ref[3], place_ref[2]
        left = lax.broadcasted_iota(jnp.int32, (rows, LANES), 1) < HEAD_DIM

        def put(at, value):
            own_ref[0, :, at : at + value.shape[1]] = value[:half]
            own_ref[1, :, at : at + value.shape[1]] = value[half:]

        for block in range(0, blocks, 2):
            one = qkv_ref[:, block * LANES : (block + 1) * LANES].astype(f32)
            two = qkv_ref[:, (block + 1) * LANES : (block + 2) * LANES].astype(f32)
            even = jnp.where(left, one, pltpu.roll(two, HEAD_DIM, 1))
            odd = jnp.where(left, pltpu.roll(one, HEAD_DIM, 1), two)
            put(block // 2 * LANES, jnp.where(lo == 0, even, odd).astype(bf16))
        columns = jnp.concatenate([vectors_ref[...].astype(f32), jnp.zeros((LANES - 4, rows), f32)], axis=0)
        put(scale_at, columns.T.astype(bf16))
        outs = jnp.where(lo == 0, out_ref[:half, :], out_ref[half:, :])
        put(out_at, jnp.concatenate([outs[:, : model // 2], outs[:, model // 2 :]], axis=0))
        for shard in range(shards):
            at = shard * 2 * unit
            put(up_at + shard * unit, jnp.where(lo == 0, up_ref[:, at : at + unit], up_ref[:, at + unit : at + 2 * unit]))
        first_ref[...] = own_ref[h, :, :up_at]
        up_half_ref[...] = own_ref[h, :, up_at:]

    return pl.pallas_call(
        kernel,
        in_specs=[pl.BlockSpec(memory_space=pltpu.SMEM)] + [pl.BlockSpec(memory_space=pltpu.VMEM)] * 4,
        out_specs=[pl.BlockSpec(memory_space=pltpu.VMEM)] * 3,
        out_shape=[shape_of(2, half, up_at + wide), shape_of(half, up_at), shape_of(half, wide)],
        compiler_params=pltpu.CompilerParams(vmem_limit_bytes=40 * 1024 * 1024),
        cost_estimate=TINY,
        name="prepare",
    )(place, w_qkv, w_out, w_up, vectors)


def finish_up(place, shards, own, other):
    rows, columns = own.shape
    unit = columns // shards

    def kernel(place_ref, own_ref, other_ref, out_ref):
        lo = place_ref[3]
        for shard in range(shards):
            at, mine, theirs = shard * 2 * unit, own_ref, other_ref
            one = mine[:, shard * unit : (shard + 1) * unit].astype(f32)
            two = theirs[:, shard * unit : (shard + 1) * unit].astype(f32)
            out_ref[:, at : at + unit] = jnp.where(lo == 0, one, two)
            out_ref[:, at + unit : at + 2 * unit] = jnp.where(lo == 0, two, one)

    return pl.pallas_call(
        kernel,
        in_specs=[pl.BlockSpec(memory_space=pltpu.SMEM)] + [pl.BlockSpec(memory_space=pltpu.VMEM)] * 2,
        out_specs=pl.BlockSpec(memory_space=pltpu.VMEM),
        out_shape=shape_of(rows, 2 * columns, dtype=f32),
        cost_estimate=TINY,
        name="finish_up",
    )(place, own, other)


def finish_qkv(place, owns, others, out_own, out_other):
    rows = out_own.shape[0]
    half = rows // 2
    columns = sum(own.shape[1] for own in owns)
    model = 2 * out_own.shape[1]
    pieces = len(owns)

    def kernel(place_ref, *refs):
        lo = place_ref[3]
        owns_refs, others_refs = refs[:pieces], refs[pieces : 2 * pieces]
        out_own_ref, out_other_ref, qkv_ref, out_ref = refs[2 * pieces :]
        left = lax.broadcasted_iota(jnp.int32, (rows, LANES), 1) < HEAD_DIM
        at = 0
        for j in range(3):
            for own_ref, other_ref in zip(owns_refs, others_refs):
                third = own_ref.shape[1] // 3
                for first in range(j * third, (j + 1) * third, LANES):
                    mine = own_ref[:, first : first + LANES].astype(f32)
                    theirs = other_ref[:, first : first + LANES].astype(f32)
                    one, two = jnp.where(lo == 0, mine, theirs), jnp.where(lo == 0, theirs, mine)
                    qkv_ref[:, at : at + LANES] = jnp.where(left, one, pltpu.roll(two, HEAD_DIM, 1))
                    qkv_ref[:, at + LANES : at + 2 * LANES] = jnp.where(left, pltpu.roll(one, HEAD_DIM, 1), two)
                    at += 2 * LANES
        mine, theirs = out_own_ref[...].astype(f32), out_other_ref[...].astype(f32)
        for at, value in ((0, jnp.where(lo == 0, mine, theirs)), (half, jnp.where(lo == 0, theirs, mine))):
            out_ref[at : at + half, : model // 2] = value[:half]
            out_ref[at : at + half, model // 2 :] = value[half:]

    return pl.pallas_call(
        kernel,
        in_specs=[pl.BlockSpec(memory_space=pltpu.SMEM)] + [pl.BlockSpec(memory_space=pltpu.VMEM)] * (2 * pieces + 2),
        out_specs=[pl.BlockSpec(memory_space=pltpu.VMEM)] * 2,
        out_shape=[shape_of(rows, 2 * columns, dtype=f32), shape_of(rows, model, dtype=f32)],
        compiler_params=pltpu.CompilerParams(vmem_limit_bytes=40 * 1024 * 1024),
        cost_estimate=TINY,
        name="finish_qkv",
    )(place, *owns, *others, out_own, out_other)


def plus(left, right):
    return (left.astype(f32) + right.astype(f32)).astype(bf16)


def cut_again(keep, came, x, h):
    first, second = plus(keep[0], came[0]), plus(keep[1], came[1])
    first = first.reshape(second.shape)
    keep = pick(first, h, 1), pick(second, x, 1)
    send = pick(first, 1 - h, 1), pick(second, 1 - x, 1)
    return keep, send


def along_z(keep, came, depth, z):
    both = jnp.stack([plus(keep[0], came[0]), plus(keep[1], came[1])], 1)
    return pick(both, z, 0), [pick(both, (z + k) % depth, 0) for k in range(1, depth)]


def add_up(own, came):
    total = own.astype(f32)
    for piece in came:
        total = total + piece.astype(f32)
    return total.astype(bf16)


def row_block(tile, width):
    return pl.BlockSpec((tile, width), lambda i: (i, 0))


def whole_block(*shape):
    return pl.BlockSpec(shape, lambda i: (0,) * len(shape))


def weight_call(name, step, tiles, place, inputs, sets, outs, scratch, copies):
    pieces = [piece for held in sets for piece in held]

    def kernel(place_ref, *refs):
        refs = list(refs)

        def take(count):
            taken = refs[:count]
            del refs[:count]
            return taken

        given = take(len(inputs))
        held = [take(len(one)) for one in sets]
        made = take(len(outs))
        step(place_ref, given, held, made, refs[:-1], refs[-1])

    return pl.pallas_call(
        kernel,
        grid=(tiles,),
        in_specs=[pl.BlockSpec(memory_space=pltpu.SMEM)]
        + [spec for _, spec in inputs]
        + [pl.BlockSpec(memory_space=pl.ANY)] * len(pieces),
        out_specs=[spec for _, spec in outs],
        out_shape=[shape for shape, _ in outs],
        scratch_shapes=list(scratch) + [pltpu.SemaphoreType.DMA((copies,))],
        compiler_params=pltpu.CompilerParams(vmem_limit_bytes=56 * 1024 * 1024),
        cost_estimate=TINY,
        name=name,
    )(place, *[v for v, _ in inputs], *pieces)


def shape_of(*shape, dtype=bf16):
    return jax.ShapeDtypeStruct(shape, dtype)


def unit_of(values):
    centred = values - jnp.mean(values, axis=-1, keepdims=True)
    variance = jnp.mean(centred * centred, axis=-1, keepdims=True)
    inverse = lax.rsqrt(variance + epsilon)
    return centred * inverse, inverse


def unit_back(grad_unit, unit_rows, inverse):
    mean_grad = jnp.mean(grad_unit, axis=-1, keepdims=True)
    mean_cross = jnp.mean(grad_unit * unit_rows, axis=-1, keepdims=True)
    return inverse * (grad_unit - mean_grad - unit_rows * mean_cross)


def bell_and_slope(values):
    size = jnp.abs(values)
    base = 1.0 + (0.3275911 * math.sqrt(0.5)) * size
    t = pl.reciprocal(base, approx=True)
    t = t * (2.0 - base * t)
    bell = jnp.exp(values * values * -0.5)
    series = 0.5 * 1.061405429
    for term in (-1.453152027, 1.421413741, -0.284496736, 0.254829592):
        series = series * t + 0.5 * term
    tail = series * t * bell
    phi = jnp.where(values < 0, tail, 1.0 - tail)
    return values * phi, phi + values * bell * (1.0 / math.sqrt(2.0 * math.pi))


def outer_whole(left, right):
    rows, across = left.shape
    block = min(256, across)

    def kernel(left_ref, right_ref, out_ref):
        out_ref[...] = mm_rows(left_ref[...], right_ref[...]).astype(bf16)

    return pl.pallas_call(
        kernel,
        grid=(across // block,),
        in_specs=[pl.BlockSpec((rows, block), lambda i: (0, i)), whole_block(*right.shape)],
        out_specs=row_block(block, right.shape[1]),
        out_shape=shape_of(across, right.shape[1]),
        compiler_params=pltpu.CompilerParams(vmem_limit_bytes=56 * 1024 * 1024),
        cost_estimate=TINY,
        name="outer_whole",
    )(left, right)


def outer(place, depth, left, right, out_pair=None, sums=None):
    rows, own_rows = left.shape[0], left.shape[1] // (2 * depth)
    top, low = own_rows // 2, own_rows // 4
    columns = right.shape[1]
    given = [left, right]
    specs = [pl.BlockSpec((rows, 2 * own_rows), lambda i: (0, i)), whole_block(*right.shape)]
    if out_pair is not None:
        out_block = out_pair[0].shape[1] // depth
        given += out_pair
        specs += [pl.BlockSpec((rows, out_block), lambda i: (0, i)), whole_block(*out_pair[1].shape)]
        half = out_pair[1].shape[1] // 2
    if sums is not None:
        given += sums
        specs += [pl.BlockSpec((8, 2 * own_rows), lambda i: (0, i))] * 2
    total = columns + (half if out_pair is not None else 0) + (LANES if sums is not None else 0)

    def kernel(place_ref, *refs):
        ins, outs = list(refs[: len(given)]), refs[len(given) :]
        at_x, at_h = place_ref[1] == 0, place_ref[2] == 0
        keep_first, send_first, keep_second, send_second = outs

        def put(first, value):
            where = slice(first, first + value.shape[2])
            heads = value[:, :top].astype(bf16)
            keep_first[0, :, where] = jnp.where(at_x, heads[0], heads[1])
            send_first[0, :, where] = jnp.where(at_x, heads[1], heads[0])
            lower, upper = value[:, top : top + low].astype(bf16), value[:, top + low :].astype(bf16)
            keep_second[0, :, :, where] = jnp.where(at_h, lower, upper)
            send_second[0, :, :, where] = jnp.where(at_h, upper, lower)

        product = mm_rows(ins.pop(0)[...], ins.pop(0)[...])
        put(0, product.reshape(2, own_rows, columns))
        first = columns
        if out_pair is not None:
            product = mm_rows(ins.pop(0)[...], ins.pop(0)[...]).reshape(2, top, 2 * half)
            put(first, jnp.concatenate([product[:, :, :half], product[:, :, half:]], axis=1))
            first += half
        if sums is not None:
            stacked = jnp.concatenate([ref[0:2, :] for ref in ins], axis=0)
            stacked = jnp.concatenate([stacked, jnp.zeros((LANES - 4, 2 * own_rows), f32)], axis=0)
            put(first, stacked.T.reshape(2, own_rows, LANES))

    def spec(*block):
        return pl.BlockSpec((1, *block), lambda i: (i,) + (0,) * len(block))

    first_shape, second_shape = (top, total), (2, low, total)
    made = pl.pallas_call(
        kernel,
        grid=(depth,),
        in_specs=[pl.BlockSpec(memory_space=pltpu.SMEM)] + specs,
        out_specs=[spec(*first_shape)] * 2 + [spec(*second_shape)] * 2,
        out_shape=[shape_of(depth, *first_shape)] * 2 + [shape_of(depth, *second_shape)] * 2,
        compiler_params=pltpu.CompilerParams(vmem_limit_bytes=56 * 1024 * 1024),
        cost_estimate=TINY,
        name="outer",
    )(place, *given)
    return (made[0], made[2]), (made[1], made[3])


def body(
    group,
    depth,
    tokens,
    segment_ids,
    norm1_gain,
    norm1_bias,
    w_qkv,
    w_out,
    norm2_gain,
    norm2_bias,
    w_up,
    w_down,
    cotangent,
):
    h, lo = lax.axis_index("hi"), lax.axis_index("lo")
    z, x = lax.axis_index("fz"), lax.axis_index("fx")
    micro, _, chunk, model = tokens.shape
    shards = 2 * depth
    rows = micro * group * chunk
    own_rows = w_out.shape[0]
    inner = w_up.shape[1] // group
    split_out = (own_rows // HEAD_DIM) % group == 0
    head_columns = model // group
    half_rows = own_rows // 2
    tile = min(TILE, rows)
    tiles = rows // tile
    scale_at = 3 * head_columns
    copies = 4 * shards
    wide = min(512, inner)
    shard_axes = ("fz", "fx")

    def whole_group(value, axis):
        if group == 2:
            return ordered(value, swap(value, "lo"), lo, axis)
        return lax.all_gather(value, "lo", axis=axis)

    def other_part(partial):
        if group == 2:
            return swap(partial, "lo")
        return (lax.psum(partial, "lo").astype(f32) - partial.astype(f32)).astype(bf16)

    def own_chunks(full):
        return pick(full.reshape(micro, group, chunk, -1), lo, 1)

    def other_own(partial):
        parts = partial.reshape(micro, group, chunk, model)
        if group == 2:
            return swap(pick(parts, 1 - lo, 1), "lo")
        return plus(lax.psum_scatter(parts, "lo", scatter_dimension=1), -pick(parts, lo, 1))

    fused_out = split_out and group == 2
    out_rows, half_model = own_rows // group, model // 2
    place = jnp.stack([z, x, h, lo]).astype(jnp.int32)
    rest = range(1, depth)
    came = swap(jnp.stack([pick(tokens[:, 0], 1 - h, 0), pick(cotangent[:, 0], 1 - h, 0)]), "hi")
    vectors = jnp.stack([norm1_gain, norm1_bias, norm2_gain, norm2_bias])
    if fused_out:
        both_own, first_half, up_half = prepare(place, shards, w_qkv, w_out, w_up, vectors)
    else:
        if split_out:
            qkv_part = pick(w_qkv.reshape(own_rows, 3, shards, group, -1), lo, 3).reshape(own_rows, -1)
            out_part = pick(w_out.reshape(group, out_rows, model), lo, 0)
        else:
            qkv_part = pick(w_qkv.reshape(own_rows, 3, group, -1), lo, 2).reshape(own_rows, -1)
            out_part = w_out
        up_part = pick(w_up.reshape(own_rows, shards, group, -1), lo, 2).reshape(own_rows, -1)
        parts = [qkv_part, jnp.pad(vectors.T, ((0, 0), (0, LANES - 4)))]
        both_own = jnp.concatenate(parts + [up_part], axis=1).reshape(2, half_rows, -1)
        half = pick(both_own, h, 0)
        first_half, up_half = half[:, : scale_at + LANES], half[:, scale_at + LANES :]
        out_weight = lax.all_gather(out_part, shard_axes, axis=0, tiled=True)
    up_at = first_half.shape[1]
    down_part = pick(w_down.reshape(group, -1, model), lo, 0)
    first_far = [along(first_half, "fz", depth, k) for k in rest]
    side_own = swap(both_own, "fx")
    first_far, side_own, came, up_half = sync(first_far, side_own, came, up_half)

    def last_quarters(side, near):
        quarter = side.shape[1] // 2
        return swap(side[:, :quarter], "hi"), swap(near[:, quarter:], "fx")

    first_far = jnp.stack(first_far)
    first_side, first_near = swap(first_far, "fx"), swap(first_far, "hi")
    inputs = whole_group(ordered(pick(tokens[:, 0], h, 0), came[0], h, 0), 1).reshape(rows, model)
    odd = [along(up_half, "fz", depth, k) for k in rest if k % 2]
    first_side, first_near, inputs, odd, up_half, came = sync(first_side, first_near, inputs, odd, up_half, came)

    first_last = last_quarters(first_side, first_near)
    even = [along(up_half, "fz", depth, k) for k in rest if k % 2 == 0]
    grad_result = whole_group(ordered(pick(cotangent[:, 0], h, 0), came[1], h, 0), 1).reshape(rows, model)
    first_last, even, odd, inputs, grad_result, down_part = sync(
        first_last, even, odd, inputs, grad_result, down_part
    )
    downward = lax.all_gather(down_part, shard_axes, axis=0, tiled=True)
    first_set = [both_own, side_own, first_far, first_side, first_near, *first_last]
    up_far = jnp.stack([odd[k // 2] if k % 2 else even[k // 2 - 1] for k in rest])

    segments = pick(segment_ids[:, 0], h, 0)
    seg_col, seg_row = segments[:, None], segments[None, :]

    def project(place_ref, given, held, made, scratch, sems):
        (rows_ref,), (normed_ref, joint_ref, scales_ref, *outs) = given, made
        weight, columns, *beside = scratch

        @pl.when(pl.program_id(0) == 0)
        def _():
            targets = [
                (0, 3 * head_columns, below(weight, half_rows)),
                (scale_at, LANES, below(columns, half_rows)),
            ]
            if fused_out:
                targets.append((scale_at + LANES, half_model, below(beside[0], half_rows)))
            for copy in load(depth, place_ref, held[0], sems, targets):
                copy.wait()
            scales_ref[...] = columns[...].astype(f32).T[:8, :]
            for shard in range(shards if fused_out else 0):
                for part in range(2):
                    at = shard * own_rows + part * out_rows
                    outs[0][
                        shard * out_rows : (shard + 1) * out_rows, part * half_model : (part + 1) * half_model
                    ] = beside[0][at : at + out_rows, :]

        unit_rows, _ = unit_of(rows_ref[...].astype(f32))
        normed = (unit_rows * scales_ref[0:1, :] + scales_ref[1:2, :]).astype(bf16)
        normed_ref[...] = normed
        for at in range(0, 3 * head_columns, head_columns):
            part = mm(normed, weight[:, at : at + head_columns])
            if at == 0:
                part = part * (1.0 / math.sqrt(HEAD_DIM))
            joint_ref[:, at : at + head_columns] = part.astype(bf16)

    out_shapes, out_scratch = [], []
    if fused_out:
        out_shapes = [(shape_of(head_columns, model), whole_block(head_columns, model))]
        out_scratch = [pltpu.VMEM((model, half_model), bf16)]
    normed, joint, scales, *outs = weight_call(
        "project",
        project,
        tiles,
        place,
        [(inputs, row_block(tile, model))],
        [first_set],
        [
            (shape_of(rows, model), row_block(tile, model)),
            (shape_of(rows, 3 * head_columns), row_block(tile, 3 * head_columns)),
            (shape_of(8, model, dtype=f32), whole_block(8, model)),
        ]
        + out_shapes,
        [pltpu.VMEM((model, 3 * head_columns), bf16), pltpu.VMEM((model, LANES), bf16)] + out_scratch,
        3 * copies,
    )
    if fused_out:
        (out_weight,) = outs
    pairs = head_columns // LANES
    pieces = 2 if pairs % 2 == 0 else 1
    count = pairs // pieces
    part_columns = count * LANES
    mixed = [attend(joint, seg_col, seg_row, 0, count)]
    up_side, up_near = swap(up_far, "fx"), swap(up_far, "hi")
    mixed, joint, up_side, up_near, scales, out_weight = sync(mixed, joint, up_side, up_near, scales, out_weight)

    up_last = last_quarters(up_side, up_near)
    for piece in range(1, pieces):
        mixed.append(attend(joint, seg_col, seg_row, piece * count, count))
    mixed, up_last, out_weight = sync(mixed, up_last, out_weight)
    up_set = [both_own, side_own, up_far, up_side, up_near, *up_last]
    lses = [lse for _, lse in mixed]

    def leave(place_ref, given, held, made, scratch, sems):
        *parts_refs, weight = given
        out_ref, attended_ref = made
        weight = own_out(weight, place_ref)
        total = jnp.zeros(out_ref.shape, f32)
        for piece, part_ref in enumerate(parts_refs):
            at = slice(piece * part_columns, (piece + 1) * part_columns)
            attended_ref[:, at] = part_ref[...]
            total = total + mm(part_ref[...], weight[at, :])
        out_ref[...] = total.astype(bf16)

    def own_out(weight, place_ref):
        if split_out:
            return weight[...]
        return weight[pl.ds(pl.multiple_of(place_ref[3] * head_columns, head_columns), head_columns), :]

    branch, attended = weight_call(
        "leave",
        leave,
        tiles,
        place,
        [(value, row_block(tile, part_columns)) for value, _ in mixed]
        + [(out_weight, whole_block(*out_weight.shape))],
        [],
        [
            (shape_of(rows, model), row_block(tile, model)),
            (shape_of(rows, head_columns), row_block(tile, head_columns)),
        ],
        [],
        1,
    )
    branch_other = other_part(branch)
    def widen(place_ref, given, held, made, scratch, sems):
        rows_ref, own_ref, other_ref, scales_ref = given
        middle_ref, normed_ref, hidden_ref, slope_ref = made
        (weight,) = scratch

        @pl.when(pl.program_id(0) == 0)
        def _():
            targets = [(0, inner, below(weight, half_rows))]
            for copy in load(depth, place_ref, held[0], sems, targets, up_at):
                copy.wait()

        added = own_ref[...].astype(f32) + other_ref[...].astype(f32)
        middle = rows_ref[...].astype(f32) + added
        middle_ref[...] = middle
        unit_rows, _ = unit_of(middle)
        normed = (unit_rows * scales_ref[2:3, :] + scales_ref[3:4, :]).astype(bf16)
        normed_ref[...] = normed
        for at in range(0, inner, wide):
            hidden, slope = bell_and_slope(mm(normed, weight[:, at : at + wide]))
            hidden_ref[:, at : at + wide] = hidden.astype(bf16)
            slope_ref[:, at : at + wide] = slope.astype(bf16)

    middle, normed_two, hidden, slope = weight_call(
        "widen",
        widen,
        tiles,
        place,
        [
            (inputs, row_block(tile, model)),
            (branch, row_block(tile, model)),
            (branch_other, row_block(tile, model)),
            (scales, whole_block(8, model)),
        ],
        [up_set],
        [
            (shape_of(rows, model, dtype=f32), row_block(tile, model)),
            (shape_of(rows, model), row_block(tile, model)),
            (shape_of(rows, inner), row_block(tile, inner)),
            (shape_of(rows, inner), row_block(tile, inner)),
        ],
        [pltpu.VMEM((model, inner), bf16)],
        copies,
    )

    grad_down = outer_whole(hidden, grad_result)
    hidden, slope, grad_down, normed_two = sync(hidden, slope, grad_down, normed_two)
    down_own = lax.psum_scatter(grad_down, shard_axes, scatter_dimension=0, tiled=True)

    def narrow(place_ref, given, held, made, scratch, sems):
        hidden_ref, grad_ref, slope_ref, down_ref = given
        out_ref, pre_ref, back_ref = made
        (upward,) = scratch

        @pl.when(pl.program_id(0) == 0)
        def _():
            targets = [(0, inner, below(upward, half_rows))]
            for copy in load(depth, place_ref, held[0], sems, targets, up_at):
                copy.wait()

        for at in range(0, inner, wide):
            grad = mm_cols(grad_ref[...], down_ref[at : at + wide, :])
            pre_ref[:, at : at + wide] = (grad * slope_ref[:, at : at + wide].astype(f32)).astype(bf16)
        back_ref[...] = mm_cols(pre_ref[...], upward[...]).astype(bf16)
        out_ref[...] = mm(hidden_ref[...], down_ref[...]).astype(bf16)

    result, grad_pre, back = weight_call(
        "narrow",
        narrow,
        tiles,
        place,
        [
            (hidden, row_block(tile, inner)),
            (grad_result, row_block(tile, model)),
            (slope, row_block(tile, inner)),
            (downward, whole_block(inner, model)),
        ],
        [up_set],
        [
            (shape_of(rows, model), row_block(tile, model)),
            (shape_of(rows, inner), row_block(tile, inner)),
            (shape_of(rows, model), row_block(tile, model)),
        ],
        [pltpu.VMEM((model, inner), bf16)],
        copies,
    )
    result, grad_pre, back, normed_two = sync(result, grad_pre, back, normed_two)

    back_other = other_part(back)
    result_other = other_own(result)
    up_keep, up_send = outer(place, depth, normed_two, grad_pre)
    back, back_other, up_keep, up_send, result_other = sync(back, back_other, up_keep, up_send, result_other)

    def between(place_ref, given, held, made, scratch, sems):
        grad_ref, own_ref, other_ref, middle_ref, scales_ref, weight = given
        middle_grad_ref, branch_ref, attended_ref, sums_ref = made

        @pl.when(pl.program_id(0) == 0)
        def _():
            sums_ref[...] = jnp.zeros_like(sums_ref)

        unit_rows, inverse = unit_of(middle_ref[...])
        own_back = own_ref[...].astype(f32)
        back_rows = own_back + other_ref[...].astype(f32)
        sums_ref[0:1, :] += jnp.sum(own_back * unit_rows, axis=0, keepdims=True)
        sums_ref[1:2, :] += jnp.sum(own_back, axis=0, keepdims=True)
        grads = grad_ref[...].astype(f32) + unit_back(back_rows * scales_ref[2:3, :], unit_rows, inverse)
        middle_grad_ref[...] = grads
        low = grads.astype(bf16)
        branch_ref[...] = low
        attended_ref[...] = mm_cols(low, own_out(weight, place_ref)).astype(bf16)

    grad_middle, grad_branch, grad_attended, sums_two = weight_call(
        "between",
        between,
        tiles,
        place,
        [
            (grad_result, row_block(tile, model)),
            (back, row_block(tile, model)),
            (back_other, row_block(tile, model)),
            (middle, row_block(tile, model)),
            (scales, whole_block(8, model)),
            (out_weight, whole_block(*out_weight.shape)),
        ],
        [],
        [
            (shape_of(rows, model, dtype=f32), row_block(tile, model)),
            (shape_of(rows, model), row_block(tile, model)),
            (shape_of(rows, head_columns), row_block(tile, head_columns)),
            (shape_of(8, model, dtype=f32), whole_block(8, model)),
        ],
        [],
        1,
    )
    grad_joints = [attend_back(joint, grad_attended, lses[0], seg_col, seg_row, 0, count)]
    up_came = swap(up_send[0], "fx"), swap(up_send[1], "hi")
    grad_joints, grad_attended, grad_branch, up_came = sync(grad_joints, grad_attended, grad_branch, up_came)

    up_keep, up_send = cut_again(up_keep, up_came, x, h)
    up_came = swap(up_send[0], "hi"), swap(up_send[1], "fx")
    one_keep, one_send = outer(
        place, depth, normed, grad_joints[0], out_pair=[attended, grad_branch] if fused_out else None
    )
    output = (own_chunks(middle) + own_chunks(result).astype(f32) + result_other.astype(f32)).astype(bf16)
    up_came, one_keep, one_send, grad_attended, output = sync(up_came, one_keep, one_send, grad_attended, output)

    up_own_sum, up_send = along_z(up_keep, up_came, depth, z)
    up_send = dict(zip(rest, up_send))
    for piece in range(1, pieces):
        grad_joints.append(
            attend_back(joint, grad_attended, lses[piece], seg_col, seg_row, piece * count, count)
        )
    one_came = swap(one_send[0], "fx"), swap(one_send[1], "hi")
    odd = [along(up_send[k], "fz", depth, k) for k in rest if k % 2]
    output_came = swap(pick(output, 1 - h, 0), "hi")
    grad_joints, odd, up_send, one_keep, one_came, output_came = sync(
        grad_joints, odd, up_send, one_keep, one_came, output_came
    )

    if pieces == 2:
        two_keep, two_send = outer(place, depth, normed, grad_joints[1])
        two_keep, two_send, grad_joints, one_keep, one_came, up_send = sync(
            two_keep, two_send, grad_joints, one_keep, one_came, up_send
        )
        two_came = swap(two_send[0], "fx"), swap(two_send[1], "hi")
    else:
        two_keep, two_came = one_keep, one_came
    one_keep, one_send = cut_again(one_keep, one_came, x, h)
    one_came = swap(one_send[0], "hi"), swap(one_send[1], "fx")
    even = [along(up_send[k], "fz", depth, k) for k in rest if k % 2 == 0]

    def enter(place_ref, given, held, made, scratch, sems):
        *parts_refs, inputs_ref = given
        (out_ref, sums_ref), (weight,) = made, scratch

        @pl.when(pl.program_id(0) == 0)
        def _():
            sums_ref[...] = jnp.zeros_like(sums_ref)
            targets = [(0, 3 * head_columns, below(weight, half_rows))]
            for copy in load(depth, place_ref, held[0], sems, targets):
                copy.wait()

        unit_rows, _ = unit_of(inputs_ref[...].astype(f32))
        grads = jnp.zeros(out_ref.shape, f32)
        for piece, part_ref in enumerate(parts_refs):
            for j in range(3):
                at = j * head_columns + piece * part_columns
                grads = grads + mm_cols(
                    part_ref[:, j * part_columns : (j + 1) * part_columns], weight[:, at : at + part_columns]
                )
        out_ref[...] = grads.astype(bf16)
        sums_ref[0:1, :] += jnp.sum(grads * unit_rows, axis=0, keepdims=True)
        sums_ref[1:2, :] += jnp.sum(grads, axis=0, keepdims=True)

    entered, sums_one = weight_call(
        "enter",
        enter,
        tiles,
        place,
        [(value, row_block(tile, 3 * part_columns)) for value in grad_joints] + [(inputs, row_block(tile, model))],
        [first_set],
        [
            (shape_of(rows, model), row_block(tile, model)),
            (shape_of(8, model, dtype=f32), whole_block(8, model)),
        ],
        [pltpu.VMEM((model, 3 * head_columns), bf16)],
        copies,
    )
    sums = jnp.concatenate([sums_one[:2], sums_two[:2]]).reshape(4, depth, 2, own_rows)
    two_came, one_came, even, entered, sums, down_own = sync(two_came, one_came, even, entered, sums, down_own)

    def both_halves(value):
        return ordered(value, swap(value, "hi"), h, 1).reshape(own_rows, -1)

    two_keep, two_send = cut_again(two_keep, two_came, x, h)
    two_came = swap(two_send[0], "hi"), swap(two_send[1], "fx")
    one_own_sum, one_send = along_z(one_keep, one_came, depth, z)
    one_came = [along(value, "fz", depth, k) for k, value in zip(rest, one_send)]
    entered_other = other_own(entered)
    down_own = plus(down_own, swap(down_own, "hi"))
    sums = pick(sums, x, 2) + swap(pick(sums, 1 - x, 2), "fx")
    two_came, one_came, entered_other, sums, odd, even, down_own = sync(
        two_came, one_came, entered_other, sums, odd, even, down_own
    )

    two_own_sum, two_send = along_z(two_keep, two_came, depth, z)
    two_came = [along(value, "fz", depth, k) for k, value in zip(rest, two_send)]
    up_own = both_halves(add_up(up_own_sum, odd + even))
    grad_normed = own_chunks(entered).astype(f32) + entered_other.astype(f32)
    unit_own, inverse_own = unit_of(own_chunks(inputs).astype(f32))
    grad_tokens = own_chunks(grad_middle) + unit_back(grad_normed * scales[0], unit_own, inverse_own)
    grad_came = swap(pick(grad_tokens, 1 - h, 0).astype(bf16), "hi")
    sums = sums + swap(sums, "hi")
    two_came, up_own, grad_tokens, grad_came, sums, one_came, down_own = sync(
        two_came, up_own, grad_tokens, grad_came, sums, one_came, down_own
    )

    one_own = both_halves(add_up(one_own_sum, one_came))
    two_own = both_halves(add_up(two_own_sum, two_came))
    sums_came = [along(pick(sums, (z + k) % depth, 1), "fz", depth, k) for k in rest]
    sums = pick(sums, z, 1)
    for piece in sums_came:
        sums = sums + piece
    output = ordered(pick(output, h, 0), output_came, h, 0)[:, None]
    grad_tokens = ordered(pick(grad_tokens, h, 0), grad_came.astype(f32), h, 0)[:, None]

    down_all = whole_group(down_own, 0).reshape(-1, model).astype(f32)
    sums = jnp.sum(whole_group(sums, 0), axis=0)
    if fused_out:
        up_all = finish_up(place, shards, up_own, swap(up_own, "lo"))
        owns = [value[:, : 3 * part_columns] for value in ((one_own, two_own) if pieces == 2 else (one_own,))]
        one_other = swap(one_own, "lo")
        others = [one_other[:, : 3 * part_columns]]
        if pieces == 2:
            others.append(swap(two_own, "lo"))
        out_own, out_other = one_own[:, 3 * part_columns :], one_other[:, 3 * part_columns :]
        qkv_all, out_all = finish_qkv(place, owns, others, out_own, out_other)
    else:
        up_all = whole_group(up_own.reshape(own_rows, shards, -1), 2).reshape(own_rows, -1).astype(f32)
        qkv_owns = [one_own] + ([two_own] if pieces == 2 else [])
        qkv_own = jnp.concatenate([value.reshape(own_rows, 3, part_columns) for value in qkv_owns], axis=2)
        if split_out:
            qkv_all = whole_group(qkv_own.reshape(own_rows, 3, shards, -1), 3)
        else:
            qkv_all = whole_group(qkv_own, 2)
        qkv_all = qkv_all.reshape(own_rows, -1).astype(f32)
        grad_out = outer_whole(attended, grad_branch)
        if not split_out:
            empty = jnp.zeros((model, model), bf16)
            grad_out = lax.dynamic_update_slice_in_dim(empty, grad_out, lo * head_columns, 0)
        out_own = lax.psum(lax.psum_scatter(grad_out, shard_axes, scatter_dimension=0, tiled=True), "hi")
        out_all = whole_group(out_own, 0).reshape(own_rows, model) if split_out else lax.psum(out_own, "lo")
        out_all = out_all.astype(f32)

    return (
        output,
        grad_tokens,
        sums[0],
        sums[1],
        qkv_all,
        out_all,
        sums[2],
        sums[3],
        up_all,
        down_all,
    )


def solution(mesh):
    seq, fsdp = mesh.shape["seq"], mesh.shape["fsdp"]
    group, depth = seq // 2, fsdp // 2
    fine = Mesh(mesh.devices.reshape(2, group, depth, 2), ("hi", "lo", "fz", "fx"))
    s, f = ("hi", "lo"), ("fz", "fx")
    return jax.shard_map(
        functools.partial(body, group, depth),
        mesh=fine,
        in_specs=(
            P(None, f, s, None),
            P(None, f, None),
            P(f),
            P(f),
            P(f, None),
            P(f, None),
            P(f),
            P(f),
            P(f, None),
            P(f, None),
            P(None, f, s, None),
        ),
        out_specs=(
            P(None, f, s, None),
            P(None, f, s, None),
            P(f),
            P(f),
            P(f, None),
            P(f, None),
            P(f),
            P(f),
            P(f, None),
            P(f, None),
        ),
        check_vma=False,
    )
```

```python
import functools
import math

import jax
import jax.numpy as jnp
from jax import lax
from jax.experimental import pallas as pl
from jax.experimental.pallas import tpu as pltpu
from jax.sharding import Mesh
from jax.sharding import PartitionSpec as P

HEAD_DIM = 64
DOC_MOST = 512
TILE = 256
LANES = 128
VMEM = 30 * 1024 * 1024
epsilon = 1e-05
SWAP = [(0, 1), (1, 0)]
f32 = jnp.float32
bf16 = jnp.bfloat16


def dot(left, right, dims):
    return lax.dot_general(left, right, (dims, ((), ())), preferred_element_type=f32)


def mm(left, right):
    return dot(left, right, ((1,), (0,)))


def mm_rows(left, right):
    return dot(left, right, ((0,), (0,)))


def mm_cols(left, right):
    return dot(left, right, ((1,), (1,)))


def cost(micros):
    return pl.CostEstimate(flops=int(micros * 1.1e9), bytes_accessed=1000, transcendentals=0)


def far(array):
    return pltpu.with_memory_space_constraint(array, pltpu.HBM)


def sync(*values):
    return lax.optimization_barrier(values)


def pick(array, index, axis):
    return lax.dynamic_index_in_dim(array, index, axis, keepdims=False)


def swap(value, axis):
    return lax.ppermute(value, axis, SWAP)


def ordered(own, other, index, axis):
    first = jnp.where(index == 0, own, other)
    second = jnp.where(index == 0, other, own)
    return jnp.stack([first, second], axis)


def tile_spans(rows):
    tile = min(TILE, rows)
    spans = []
    for start in range(0, rows, tile):
        low = max(0, (start - DOC_MOST + 1) // tile * tile)
        spans.append((start, low, start + tile))
    return tile, spans


def fill_bias(bias, seg_col, seg_row, spans, tile):
    for i, (start, low, high) in enumerate(spans):
        width = high - low
        query_pos = start + lax.broadcasted_iota(jnp.int32, (tile, width), 0)
        key_pos = low + lax.broadcasted_iota(jnp.int32, (tile, width), 1)
        same = seg_col[start : start + tile, :] == seg_row[:, low:high]
        allowed = (key_pos <= query_pos) & same
        bias[i, :, :width] = jnp.where(allowed, 0.0, -1e30).astype(f32)


def attend_kernel(spans, tile, q_ref, k_ref, v_ref, seg_col, seg_row, out_ref, lse_ref, bias):
    @pl.when(pl.program_id(0) == 0)
    def _():
        fill_bias(bias, seg_col, seg_row, spans, tile)

    left = lax.broadcasted_iota(jnp.int32, (tile, LANES), 1) < HEAD_DIM
    for i, (start, low, high) in enumerate(spans):
        rows = slice(start, start + tile)
        queries = q_ref[rows, :]
        keys, values = k_ref[low:high, :], v_ref[low:high, :]
        mixed, logs = [], []
        for half in (left, ~left):
            scores = mm_cols(jnp.where(half, queries, jnp.zeros_like(queries)), keys)
            scores = scores + bias[i, :, : high - low]
            top = jnp.max(scores, axis=-1, keepdims=True)
            powers = jnp.exp(scores - top)
            total = jnp.sum(powers, axis=-1, keepdims=True)
            mixed.append(mm((powers * (1.0 / total)).astype(bf16), values))
            logs.append(top + jnp.log(total))
        out_ref[rows, :] = jnp.where(left, mixed[0], mixed[1]).astype(bf16)
        lse_ref[rows, :] = jnp.where(left, logs[0], logs[1])


def attend(joint, seg_col, seg_row, begin, count):
    rows, width = joint.shape[0], joint.shape[1] // 3
    pairs = width // LANES
    tile, spans = tile_spans(rows)
    widest = max(high - low for _, low, high in spans)

    def part(which):
        return pl.BlockSpec((rows, LANES), lambda p: (0, which * pairs + begin + p))

    out = pl.BlockSpec((rows, LANES), lambda p: (0, p))
    return pl.pallas_call(
        functools.partial(attend_kernel, spans, tile),
        grid=(count,),
        in_specs=[
            part(0),
            part(1),
            part(2),
            pl.BlockSpec((rows, 1), lambda p: (0, 0)),
            pl.BlockSpec((1, rows), lambda p: (0, 0)),
        ],
        out_specs=[out, out],
        out_shape=[
            jax.ShapeDtypeStruct((rows, count * LANES), bf16),
            jax.ShapeDtypeStruct((rows, count * LANES), f32),
        ],
        scratch_shapes=[pltpu.VMEM((len(spans), tile, widest), f32)],
        compiler_params=pltpu.CompilerParams(vmem_limit_bytes=VMEM),
        cost_estimate=cost(4 * count),
        name="attend",
    )(far(joint), far(joint), far(joint), seg_col, seg_row)


def attend_back_kernel(
    spans, tile, q_ref, k_ref, v_ref, g_ref, lse_ref, seg_col, seg_row, out_ref, bias, keys_sum, values_sum
):
    @pl.when((pl.program_id(0) == 0) & (pl.program_id(1) == 0))
    def _():
        fill_bias(bias, seg_col, seg_row, spans, tile)

    @pl.when(pl.program_id(1) == 0)
    def _():
        keys_sum[...] = jnp.zeros_like(keys_sum)
        values_sum[...] = jnp.zeros_like(values_sum)
        left = lax.broadcasted_iota(jnp.int32, (tile, LANES), 1) < HEAD_DIM
        for i, (start, low, high) in enumerate(spans):
            rows = slice(start, start + tile)
            queries, grads = q_ref[rows, :], g_ref[rows, :]
            keys, values = k_ref[low:high, :], v_ref[low:high, :]
            parts = []
            for half, lane in ((left, 0), (~left, HEAD_DIM)):
                own_queries = jnp.where(half, queries, jnp.zeros_like(queries))
                own_grads = jnp.where(half, grads, jnp.zeros_like(grads))
                scores = mm_cols(own_queries, keys) + bias[i, :, : high - low]
                probs = jnp.exp(scores - lse_ref[rows, lane : lane + 1])
                grad_probs = mm_cols(own_grads, values)
                inner = jnp.sum(probs * grad_probs, axis=-1, keepdims=True)
                grad_scores = (probs * (grad_probs - inner)).astype(bf16)
                parts.append(mm(grad_scores, keys))
                keys_sum[low:high, :] += mm_rows(grad_scores, own_queries)
                values_sum[low:high, :] += mm_rows(probs.astype(bf16), own_grads)
            grad_queries = jnp.where(left, parts[0], parts[1]).astype(bf16)
            out_ref[rows, :] = grad_queries * jnp.asarray(1.0 / math.sqrt(HEAD_DIM), bf16)

    @pl.when(pl.program_id(1) == 1)
    def _():
        out_ref[...] = keys_sum[...].astype(bf16)

    @pl.when(pl.program_id(1) == 2)
    def _():
        out_ref[...] = values_sum[...].astype(bf16)


def attend_back(joint, grads, lse, seg_col, seg_row, begin, count):
    rows, width = joint.shape[0], joint.shape[1] // 3
    pairs = width // LANES
    tile, spans = tile_spans(rows)
    widest = max(high - low for _, low, high in spans)

    def part(which):
        return pl.BlockSpec((rows, LANES), lambda p, j: (0, which * pairs + begin + p))

    return pl.pallas_call(
        functools.partial(attend_back_kernel, spans, tile),
        grid=(count, 3),
        in_specs=[
            part(0),
            part(1),
            part(2),
            part(0),
            pl.BlockSpec((rows, LANES), lambda p, j: (0, p)),
            pl.BlockSpec((rows, 1), lambda p, j: (0, 0)),
            pl.BlockSpec((1, rows), lambda p, j: (0, 0)),
        ],
        out_specs=pl.BlockSpec((rows, LANES), lambda p, j: (0, j * count + p)),
        out_shape=jax.ShapeDtypeStruct((rows, 3 * count * LANES), bf16),
        scratch_shapes=[
            pltpu.VMEM((len(spans), tile, widest), f32),
            pltpu.VMEM((rows, LANES), f32),
            pltpu.VMEM((rows, LANES), f32),
        ],
        compiler_params=pltpu.CompilerParams(vmem_limit_bytes=VMEM),
        cost_estimate=cost(6 * count),
        name="attend_back",
    )(far(joint), far(joint), far(joint), grads, lse, seg_col, seg_row)


def along(value, axis, depth, step):
    return lax.ppermute(value, axis, [(i, (i + step) % depth) for i in range(depth)])


def load(depth, place, pieces, sems, targets, base=0, sem=0):
    z, x, h = place[0], place[1], place[2]
    copies = []

    def put(source, shard, half, at, shift=0):
        for first, columns, where in targets:
            taken = source
            if columns != source.shape[1]:
                taken = source.at[:, shift + first : shift + first + columns]
            copies.append(pltpu.make_async_copy(taken, where(shard, half, at, source.shape[0]), sems.at[sem + len(copies)]))
            copies[-1].start()

    own, side_own, far, side, near, last_side, last_near = pieces
    quarter = last_side.shape[1]
    for at_x, piece in ((x, own), (1 - x, side_own)):
        for half in range(2):
            put(piece.at[half], z * 2 + at_x, half, 0, base)
    for at_x, at_h, at, piece in (
        (x, h, 0, far),
        (1 - x, h, 0, side),
        (x, 1 - h, 0, near),
        (1 - x, 1 - h, 0, last_side),
        (1 - x, 1 - h, quarter, last_near),
    ):
        for k in range(1, depth):
            put(piece.at[k - 1], lax.rem(z - k + depth, depth) * 2 + at_x, at_h, at)
    return copies


def below(weight, half_rows):
    def where(shard, half, at, count):
        first = pl.multiple_of((shard * 2 + half) * half_rows + at, math.gcd(half_rows, at))
        return weight.at[pl.ds(first, count), :]

    return where


def halve(side, near):
    count, rows, columns = side.shape
    half = rows // 2

    def kernel(side_ref, near_ref, one_ref, two_ref):
        one_ref[...] = side_ref[:, :half, :]
        two_ref[...] = near_ref[:, half:, :]

    return pl.pallas_call(
        kernel,
        in_specs=[pl.BlockSpec(memory_space=pltpu.VMEM)] * 2,
        out_specs=[pl.BlockSpec(memory_space=pltpu.VMEM)] * 2,
        out_shape=[shape_of(count, half, columns)] * 2,
        compiler_params=pltpu.CompilerParams(vmem_limit_bytes=VMEM),
        cost_estimate=cost(1),
        name="halve",
    )(side, near)


def prepare(place, shards, w_qkv, w_out, w_up, vectors):
    rows, model = w_out.shape
    half, blocks = rows // 2, w_qkv.shape[1] // LANES
    qkv_columns, wide = w_qkv.shape[1] // 2, w_up.shape[1] // 2
    scale_at = qkv_columns
    out_at = scale_at + LANES
    up_at = out_at + model // 2
    unit = wide // shards

    def kernel(place_ref, qkv_ref, out_ref, up_ref, vectors_ref, own_ref, first_ref, up_half_ref):
        lo, h = place_ref[3], place_ref[2]
        left = lax.broadcasted_iota(jnp.int32, (rows, LANES), 1) < HEAD_DIM

        def put(at, value):
            own_ref[0, :, at : at + value.shape[1]] = value[:half]
            own_ref[1, :, at : at + value.shape[1]] = value[half:]

        for block in range(0, blocks, 2):
            one = qkv_ref[:, block * LANES : (block + 1) * LANES].astype(f32)
            two = qkv_ref[:, (block + 1) * LANES : (block + 2) * LANES].astype(f32)
            even = jnp.where(left, one, pltpu.roll(two, HEAD_DIM, 1))
            odd = jnp.where(left, pltpu.roll(one, HEAD_DIM, 1), two)
            put(block // 2 * LANES, jnp.where(lo == 0, even, odd).astype(bf16))
        columns = jnp.concatenate([vectors_ref[...].astype(f32), jnp.zeros((LANES - 4, rows), f32)], axis=0)
        put(scale_at, columns.T.astype(bf16))
        outs = jnp.where(lo == 0, out_ref[:half, :], out_ref[half:, :])
        put(out_at, jnp.concatenate([outs[:, : model // 2], outs[:, model // 2 :]], axis=0))
        for shard in range(shards):
            at = shard * 2 * unit
            put(up_at + shard * unit, jnp.where(lo == 0, up_ref[:, at : at + unit], up_ref[:, at + unit : at + 2 * unit]))
        first_ref[...] = own_ref[h, :, :up_at]
        up_half_ref[...] = own_ref[h, :, up_at:]

    return pl.pallas_call(
        kernel,
        in_specs=[pl.BlockSpec(memory_space=pltpu.SMEM)] + [pl.BlockSpec(memory_space=pltpu.VMEM)] * 4,
        out_specs=[pl.BlockSpec(memory_space=pltpu.VMEM)] * 3,
        out_shape=[shape_of(2, half, up_at + wide), shape_of(half, up_at), shape_of(half, wide)],
        compiler_params=pltpu.CompilerParams(vmem_limit_bytes=VMEM),
        cost_estimate=cost(2),
        name="prepare",
    )(place, far(w_qkv), far(w_out), far(w_up), vectors)


def finish_up(place, shards, own, other):
    rows, columns = own.shape
    unit = columns // shards

    def kernel(place_ref, own_ref, other_ref, out_ref):
        lo = place_ref[3]
        for shard in range(shards):
            at, mine, theirs = shard * 2 * unit, own_ref, other_ref
            one = mine[:, shard * unit : (shard + 1) * unit].astype(f32)
            two = theirs[:, shard * unit : (shard + 1) * unit].astype(f32)
            out_ref[:, at : at + unit] = jnp.where(lo == 0, one, two)
            out_ref[:, at + unit : at + 2 * unit] = jnp.where(lo == 0, two, one)

    return pl.pallas_call(
        kernel,
        in_specs=[pl.BlockSpec(memory_space=pltpu.SMEM)] + [pl.BlockSpec(memory_space=pltpu.VMEM)] * 2,
        out_specs=pl.BlockSpec(memory_space=pltpu.VMEM),
        out_shape=shape_of(rows, 2 * columns, dtype=f32),
        cost_estimate=cost(2),
        name="finish_up",
    )(place, own, other)


def finish_qkv(place, owns, others):
    rows = owns[0].shape[0]
    half, pieces = rows // 2, len(owns)
    columns = owns[-1].shape[1] - LANES
    third = columns // 3
    model = 2 * (owns[0].shape[1] - columns - LANES)

    def kernel(place_ref, *refs):
        lo = place_ref[3]
        owns_refs, others_refs = refs[:pieces], refs[pieces : 2 * pieces]
        qkv_ref, out_ref, sums_ref = refs[2 * pieces :]
        left = lax.broadcasted_iota(jnp.int32, (rows, LANES), 1) < HEAD_DIM
        at = 0
        for j in range(3):
            for own_ref, other_ref in zip(owns_refs, others_refs):
                for first in range(j * third, (j + 1) * third, LANES):
                    mine = own_ref[:, first : first + LANES].astype(f32)
                    theirs = other_ref[:, first : first + LANES].astype(f32)
                    one, two = jnp.where(lo == 0, mine, theirs), jnp.where(lo == 0, theirs, mine)
                    qkv_ref[:, at : at + LANES] = jnp.where(left, one, pltpu.roll(two, HEAD_DIM, 1))
                    qkv_ref[:, at + LANES : at + 2 * LANES] = jnp.where(left, pltpu.roll(one, HEAD_DIM, 1), two)
                    at += 2 * LANES
        sums = jnp.zeros((rows, LANES), f32)
        for ref in refs[: 2 * pieces]:
            sums = sums + ref[:, columns : columns + LANES].astype(f32)
        sums_ref[...] = sums.T[:8, :]
        mine, theirs = (ref[:, columns + LANES :].astype(f32) for ref in (owns_refs[0], others_refs[0]))
        for at, value in ((0, jnp.where(lo == 0, mine, theirs)), (half, jnp.where(lo == 0, theirs, mine))):
            out_ref[at : at + half, : model // 2] = value[:half]
            out_ref[at : at + half, model // 2 :] = value[half:]

    return pl.pallas_call(
        kernel,
        in_specs=[pl.BlockSpec(memory_space=pltpu.SMEM)] + [pl.BlockSpec(memory_space=pltpu.VMEM)] * (2 * pieces),
        out_specs=[pl.BlockSpec(memory_space=pltpu.VMEM)] * 3,
        out_shape=[
            shape_of(rows, 2 * pieces * columns, dtype=f32),
            shape_of(rows, model, dtype=f32),
            shape_of(8, rows, dtype=f32),
        ],
        compiler_params=pltpu.CompilerParams(vmem_limit_bytes=VMEM),
        cost_estimate=cost(2),
        name="finish_qkv",
    )(place, *owns, *others)


def plus(left, right):
    return (left.astype(f32) + right.astype(f32)).astype(bf16)


def fold_one(place, keep, came):
    depth, top, columns = keep[0].shape
    low = top // 2

    def kernel(place_ref, keep_one, keep_two, came_one, came_two, kept_ref, send_one, send_two):
        at_x, at_h = place_ref[1] == 0, place_ref[2] == 0
        one, two = plus(keep_one[0], came_one[0]), plus(keep_two[0], came_two[0])
        kept_ref[0, 0] = jnp.where(at_h, one[:low], one[low:])
        send_one[0] = jnp.where(at_h, one[low:], one[:low])
        kept_ref[1, 0] = jnp.where(at_x, two[0], two[1])
        send_two[0] = jnp.where(at_x, two[1], two[0])

    one = pl.BlockSpec((1, top, columns), lambda i: (i, 0, 0))
    two = pl.BlockSpec((1, 2, low, columns), lambda i: (i, 0, 0, 0))
    send = pl.BlockSpec((1, low, columns), lambda i: (i, 0, 0))
    kept, *sends = pl.pallas_call(
        kernel,
        grid=(depth,),
        in_specs=[pl.BlockSpec(memory_space=pltpu.SMEM), one, two, one, two],
        out_specs=[pl.BlockSpec((2, 1, low, columns), lambda i: (0, i, 0, 0)), send, send],
        out_shape=[shape_of(2, depth, low, columns)] + [shape_of(depth, low, columns)] * 2,
        compiler_params=pltpu.CompilerParams(vmem_limit_bytes=VMEM),
        cost_estimate=cost(1),
        name="fold_one",
    )(place, *keep, *came)
    return kept, sends


def fold_two(place, kept, came):
    _, depth, low, columns = kept.shape

    def kernel(place_ref, kept_ref, came_one, came_two, *refs):
        *outs, sums = refs
        for half, came_ref in enumerate((came_one, came_two)):
            for at in range(depth):
                sums[at, half] = plus(kept_ref[half, at], came_ref[at])
        for k, out in enumerate(outs):
            out[...] = sums[lax.rem(place_ref[0] + k, depth)]

    own, *sends = pl.pallas_call(
        kernel,
        in_specs=[pl.BlockSpec(memory_space=pltpu.SMEM)] + [pl.BlockSpec(memory_space=pltpu.VMEM)] * 3,
        out_specs=[pl.BlockSpec(memory_space=pltpu.VMEM)] * depth,
        out_shape=[shape_of(2, low, columns)] * depth,
        scratch_shapes=[pltpu.VMEM((depth, 2, low, columns), bf16)],
        compiler_params=pltpu.CompilerParams(vmem_limit_bytes=VMEM),
        cost_estimate=cost(1),
        name="fold_two",
    )(place, kept, *came)
    return own, sends


def add_up(own, came):
    total = own.astype(f32)
    for piece in came:
        total = total + piece.astype(f32)
    return total.astype(bf16)


def row_block(tile, width):
    return pl.BlockSpec((tile, width), lambda i: (i, 0))


def whole_block(*shape):
    return pl.BlockSpec(shape, lambda i: (0,) * len(shape))


def weight_call(name, step, tiles, place, inputs, sets, outs, scratch, copies, micros):
    pieces = [piece for held in sets for piece in held]

    def kernel(place_ref, *refs):
        refs = list(refs)

        def take(count):
            taken = refs[:count]
            del refs[:count]
            return taken

        given = take(len(inputs))
        held = [take(len(one)) for one in sets]
        made = take(len(outs))
        step(place_ref, given, held, made, refs[:-1], refs[-1])

    return pl.pallas_call(
        kernel,
        grid=(tiles,),
        in_specs=[pl.BlockSpec(memory_space=pltpu.SMEM)]
        + [spec for _, spec in inputs]
        + [pl.BlockSpec(memory_space=pltpu.HBM)] * len(pieces),
        out_specs=[spec for _, spec in outs],
        out_shape=[shape for shape, _ in outs],
        scratch_shapes=list(scratch) + [pltpu.SemaphoreType.DMA((copies,))],
        compiler_params=pltpu.CompilerParams(vmem_limit_bytes=VMEM),
        cost_estimate=cost(micros),
        name=name,
    )(place, *[v for v, _ in inputs], *[far(piece) for piece in pieces])


def shape_of(*shape, dtype=bf16):
    return jax.ShapeDtypeStruct(shape, dtype)


def far_shape(*shape, dtype=bf16):
    return pltpu.HBM(shape, dtype)


def unit_of(values):
    centred = values - jnp.mean(values, axis=-1, keepdims=True)
    variance = jnp.mean(centred * centred, axis=-1, keepdims=True)
    inverse = lax.rsqrt(variance + epsilon)
    return centred * inverse, inverse


def unit_back(grad_unit, unit_rows, inverse):
    mean_grad = jnp.mean(grad_unit, axis=-1, keepdims=True)
    mean_cross = jnp.mean(grad_unit * unit_rows, axis=-1, keepdims=True)
    return inverse * (grad_unit - mean_grad - unit_rows * mean_cross)


def bell_and_slope(values):
    phi = 0.5 + 0.5 * lax.erf(values * math.sqrt(0.5))
    density = jnp.exp(values * values * -0.5) * (1.0 / math.sqrt(2.0 * math.pi))
    return values * phi, phi + values * density


def outer_whole(left, right):
    rows, across = left.shape
    block = min(256, across)

    def kernel(left_ref, right_ref, out_ref):
        out_ref[...] = mm_rows(left_ref[...], right_ref[...]).astype(bf16)

    return pl.pallas_call(
        kernel,
        grid=(across // block,),
        in_specs=[pl.BlockSpec((rows, block), lambda i: (0, i)), whole_block(*right.shape)],
        out_specs=row_block(block, right.shape[1]),
        out_shape=shape_of(across, right.shape[1]),
        compiler_params=pltpu.CompilerParams(vmem_limit_bytes=VMEM),
        cost_estimate=cost(7),
        name="outer_whole",
    )(left, right)


def outer(place, depth, left, right, out_pair=None, weight=None, scales=None, piece=0, sums=None):
    rows, own_rows = left.shape[0], left.shape[1] // (2 * depth)
    top, low = own_rows // 2, own_rows // 4
    columns = right.shape[1]
    given = [left, right]
    specs = [pl.BlockSpec((rows, 2 * own_rows), lambda i: (0, i)), whole_block(*right.shape)]
    total = columns
    if weight is not None:
        given += [weight, scales, sums]
        specs += [pl.BlockSpec((2 * own_rows, part.shape[1]), lambda i: (i, 0)) for part in (weight, scales)]
        specs.append(pl.BlockSpec((8, 2 * own_rows), lambda i: (0, i)))
        total += LANES
        third, width = columns // 3, weight.shape[1] // 3
    if out_pair is not None:
        out_block = out_pair[0].shape[1] // depth
        given += out_pair
        specs += [pl.BlockSpec((rows, out_block), lambda i: (0, i)), whole_block(*out_pair[1].shape)]
        half = out_pair[1].shape[1] // 2
        total += half

    def kernel(place_ref, *refs):
        ins, outs = list(refs[: len(given)]), refs[len(given) :]
        at_x, at_h = place_ref[1] == 0, place_ref[2] == 0
        keep_first, send_first, keep_second, send_second = outs

        def put(first, value):
            where = slice(first, first + value.shape[2])
            heads = value[:, :top].astype(bf16)
            keep_first[0, :, where] = jnp.where(at_x, heads[0], heads[1])
            send_first[0, :, where] = jnp.where(at_x, heads[1], heads[0])
            lower, upper = value[:, top : top + low].astype(bf16), value[:, top + low :].astype(bf16)
            keep_second[0, :, :, where] = jnp.where(at_h, lower, upper)
            send_second[0, :, :, where] = jnp.where(at_h, upper, lower)

        left_ref, right_ref = ins.pop(0), ins.pop(0)
        product = mm_rows(left_ref[...], right_ref[...])
        put(0, product.reshape(2, own_rows, columns))
        first = columns
        if weight is not None:
            weight_ref, scales_ref, sums_ref = ins.pop(0), ins.pop(0), ins.pop(0)
            column_sums = jnp.sum(right_ref[...].astype(f32), axis=0, keepdims=True)
            bias_sum = cross = 0.0
            for j in range(3):
                at, to = j * width + piece * third, slice(j * third, (j + 1) * third)
                part = weight_ref[:, at : at + third].astype(f32)
                bias_sum = bias_sum + jnp.sum(part * column_sums[:, to], axis=1, keepdims=True)
                cross = cross + jnp.sum(part * product[:, to], axis=1, keepdims=True)
            gain, bias = scales_ref[:, 0:1].astype(f32), scales_ref[:, 1:2].astype(f32)
            gain_sum = (cross - bias * bias_sum) / gain
            kept = jnp.concatenate(
                [jnp.zeros((2, 2 * own_rows), f32), sums_ref[0:2, :], jnp.zeros((LANES - 4, 2 * own_rows), f32)], axis=0
            ).T
            lane = lax.broadcasted_iota(jnp.int32, kept.shape, 1)
            kept = jnp.where(lane == 0, gain_sum, jnp.where(lane == 1, bias_sum, kept))
            put(first, kept.reshape(2, own_rows, LANES))
            first += LANES
        if out_pair is not None:
            product = mm_rows(ins.pop(0)[...], ins.pop(0)[...]).reshape(2, top, 2 * half)
            put(first, jnp.concatenate([product[:, :, :half], product[:, :, half:]], axis=1))

    def spec(*block):
        return pl.BlockSpec((1, *block), lambda i: (i,) + (0,) * len(block))

    first_shape, second_shape = (top, total), (2, low, total)
    made = pl.pallas_call(
        kernel,
        grid=(depth,),
        in_specs=[pl.BlockSpec(memory_space=pltpu.SMEM)] + specs,
        out_specs=[spec(*first_shape)] * 2 + [spec(*second_shape)] * 2,
        out_shape=[shape_of(depth, *first_shape)] * 2 + [shape_of(depth, *second_shape)] * 2,
        compiler_params=pltpu.CompilerParams(vmem_limit_bytes=VMEM),
        cost_estimate=cost(6),
        name="outer",
    )(place, *given)
    return (made[0], made[2]), (made[1], made[3])


def body(
    group,
    depth,
    tokens,
    segment_ids,
    norm1_gain,
    norm1_bias,
    w_qkv,
    w_out,
    norm2_gain,
    norm2_bias,
    w_up,
    w_down,
    cotangent,
):
    h, lo = lax.axis_index("hi"), lax.axis_index("lo")
    z, x = lax.axis_index("fz"), lax.axis_index("fx")
    micro, _, chunk, model = tokens.shape
    shards = 2 * depth
    rows = micro * group * chunk
    own_rows = w_out.shape[0]
    inner = w_up.shape[1] // group
    split_out = (own_rows // HEAD_DIM) % group == 0
    head_columns = model // group
    half_rows = own_rows // 2
    tile = min(TILE, rows)
    tiles = rows // tile
    scale_at = 3 * head_columns
    copies = 4 * shards
    wide = min(512, inner)
    shard_axes = ("fz", "fx")

    def whole_group(value, axis):
        if group == 2:
            return ordered(value, swap(value, "lo"), lo, axis)
        return lax.all_gather(value, "lo", axis=axis)

    def other_part(partial):
        if group == 2:
            return swap(partial, "lo")
        return (lax.psum(partial, "lo").astype(f32) - partial.astype(f32)).astype(bf16)

    def own_chunks(full):
        return pick(full.reshape(micro, group, chunk, -1), lo, 1)

    def other_own(partial):
        parts = partial.reshape(micro, group, chunk, model)
        if group == 2:
            return swap(pick(parts, 1 - lo, 1), "lo")
        return plus(lax.psum_scatter(parts, "lo", scatter_dimension=1), -pick(parts, lo, 1))

    fused_out = split_out and group == 2
    out_rows, half_model = own_rows // group, model // 2
    place = jnp.stack([z, x, h, lo]).astype(jnp.int32)
    rest = range(1, depth)
    came = swap(jnp.stack([pick(tokens[:, 0], 1 - h, 0), pick(cotangent[:, 0], 1 - h, 0)]), "hi")
    vectors = jnp.stack([norm1_gain, norm1_bias, norm2_gain, norm2_bias])
    if fused_out:
        both_own, first_half, up_half = prepare(place, shards, w_qkv, w_out, w_up, vectors)
    else:
        if split_out:
            qkv_part = pick(w_qkv.reshape(own_rows, 3, shards, group, -1), lo, 3).reshape(own_rows, -1)
            out_part = pick(w_out.reshape(group, out_rows, model), lo, 0)
        else:
            qkv_part = pick(w_qkv.reshape(own_rows, 3, group, -1), lo, 2).reshape(own_rows, -1)
            out_part = w_out
        up_part = pick(w_up.reshape(own_rows, shards, group, -1), lo, 2).reshape(own_rows, -1)
        parts = [qkv_part, jnp.pad(vectors.T, ((0, 0), (0, LANES - 4)))]
        both_own = jnp.concatenate(parts + [up_part], axis=1).reshape(2, half_rows, -1)
        half = pick(both_own, h, 0)
        first_half, up_half = half[:, : scale_at + LANES], half[:, scale_at + LANES :]
        out_weight = lax.all_gather(out_part, shard_axes, axis=0, tiled=True)
    up_at = first_half.shape[1]
    down_rows = inner // shards
    fine_down = down_rows % 64 == 0
    down_part = pick(w_down.reshape(group, 2, down_rows // 2, model), lo, 0)
    first_far = [along(first_half, "fz", depth, k) for k in rest]
    side_own = swap(both_own, "fx")
    first_far, side_own, came, up_half = sync(first_far, side_own, came, up_half)

    def last_quarters(side_part, near_part):
        return swap(side_part, "hi"), swap(near_part, "fx")

    first_far = jnp.stack(first_far)
    first_side, first_near = swap(first_far, "fx"), swap(first_far, "hi")
    up_far = [along(up_half, "fz", depth, k) for k in rest]
    first_side, first_near, up_far, came, down_part = sync(first_side, first_near, up_far, came, down_part)

    cuts, came, tokens, up_far = sync(halve(first_side, first_near), came, tokens, up_far)
    first_last = last_quarters(*cuts)
    down_half = pick(down_part, h, 0)
    if not fine_down:
        downward = lax.all_gather(down_part.reshape(down_rows, model), shard_axes, axis=0, tiled=True)
    inputs = whole_group(ordered(pick(tokens[:, 0], h, 0), came[0], h, 0), 1).reshape(rows, model)
    up_far = jnp.stack(up_far)
    first_last, inputs, up_far, came, down_half, down_part = sync(
        first_last, inputs, up_far, came, down_half, down_part
    )
    first_set = [both_own, side_own, first_far, first_side, first_near, *first_last]

    segments = pick(segment_ids[:, 0], h, 0)
    seg_col, seg_row = segments[:, None], segments[None, :]

    def project(place_ref, given, held, made, scratch, sems):
        (rows_ref,), (normed_ref, joint_ref, scales_ref, weight, columns, *outs) = given, made

        @pl.when(pl.program_id(0) == 0)
        def _():
            targets = [
                (0, 3 * head_columns, below(weight, half_rows)),
                (scale_at, LANES, below(columns, half_rows)),
            ]
            if fused_out:
                targets.append((scale_at + LANES, half_model, below(scratch[0], half_rows)))
            for copy in load(depth, place_ref, held[0], sems, targets):
                copy.wait()
            scales_ref[...] = columns[...].astype(f32).T[:8, :]
            for shard in range(shards if fused_out else 0):
                for part in range(2):
                    at = shard * own_rows + part * out_rows
                    outs[0][
                        shard * out_rows : (shard + 1) * out_rows, part * half_model : (part + 1) * half_model
                    ] = scratch[0][at : at + out_rows, :]

        unit_rows, _ = unit_of(rows_ref[...].astype(f32))
        normed = (unit_rows * scales_ref[0:1, :] + scales_ref[1:2, :]).astype(bf16)
        normed_ref[...] = normed
        for at in range(0, 3 * head_columns, head_columns):
            part = mm(normed, weight[:, at : at + head_columns])
            if at == 0:
                part = part * (1.0 / math.sqrt(HEAD_DIM))
            joint_ref[:, at : at + head_columns] = part.astype(bf16)

    wholes = [(8, model, f32), (model, 3 * head_columns, bf16), (model, LANES, bf16)]
    if fused_out:
        wholes.append((head_columns, model, bf16))
    normed, joint, scales, joint_weight, scale_columns, *outs = weight_call(
        "project",
        project,
        tiles,
        place,
        [(inputs, row_block(tile, model))],
        [first_set],
        [
            (far_shape(rows, model), row_block(tile, model)),
            (far_shape(rows, 3 * head_columns), row_block(tile, 3 * head_columns)),
        ]
        + [(shape_of(*shape, dtype=dtype), whole_block(*shape)) for *shape, dtype in wholes],
        [pltpu.VMEM((model, half_model), bf16)] if fused_out else [],
        3 * copies,
        8,
    )
    if fused_out:
        (out_weight,) = outs
    pairs = head_columns // LANES
    pieces = 2 if pairs % 2 == 0 else 1
    count = pairs // pieces
    part_columns = count * LANES
    mixed = [attend(joint, seg_col, seg_row, 0, count)]
    up_side, up_near = swap(up_far, "fx"), swap(up_far, "hi")
    down_odd = down_even = down_side_own = None
    if fine_down:
        down_odd = [along(down_half, "fz", depth, k) for k in rest if k % 2]
        down_side_own = swap(down_part, "fx")
    mixed, joint, up_side, up_near, scales, out_weight, came, down_odd, down_side_own, down_half = sync(
        mixed, joint, up_side, up_near, scales, out_weight, came, down_odd, down_side_own, down_half
    )

    cuts, joint, came, down_half = sync(halve(up_side, up_near), joint, came, down_half)
    up_last = last_quarters(*cuts)
    for piece in range(1, pieces):
        mixed.append(attend(joint, seg_col, seg_row, piece * count, count))
    grad_result = whole_group(ordered(pick(cotangent[:, 0], h, 0), came[1], h, 0), 1).reshape(rows, model)
    if fine_down:
        down_even = [along(down_half, "fz", depth, k) for k in rest if k % 2 == 0]
    mixed, up_last, out_weight, grad_result, down_even = sync(mixed, up_last, out_weight, grad_result, down_even)
    up_set = [both_own, side_own, up_far, up_side, up_near, *up_last]
    lses = [lse for _, lse in mixed]

    def leave(place_ref, given, held, made, scratch, sems):
        *parts_refs, weight = given
        out_ref, attended_ref = made
        weight = own_out(weight, place_ref)
        total = jnp.zeros(out_ref.shape, f32)
        for piece, part_ref in enumerate(parts_refs):
            at = slice(piece * part_columns, (piece + 1) * part_columns)
            attended_ref[:, at] = part_ref[...]
            total = total + mm(part_ref[...], weight[at, :])
        out_ref[...] = total.astype(bf16)

    def own_out(weight, place_ref):
        if split_out:
            return weight[...]
        return weight[pl.ds(pl.multiple_of(place_ref[3] * head_columns, head_columns), head_columns), :]

    branch, attended = weight_call(
        "leave",
        leave,
        tiles,
        place,
        [(value, row_block(tile, part_columns)) for value, _ in mixed]
        + [(out_weight, whole_block(*out_weight.shape))],
        [],
        [
            (shape_of(rows, model), row_block(tile, model)),
            (shape_of(rows, head_columns), row_block(tile, head_columns)),
        ],
        [],
        1,
        3,
    )
    branch_other = other_part(branch)

    if fine_down:
        down_far = jnp.stack([down_odd[k // 2] if k % 2 else down_even[k // 2 - 1] for k in rest])
        down_side, down_near = swap(down_far, "fx"), swap(down_far, "hi")

    def widen(place_ref, given, held, made, scratch, sems):
        rows_ref, own_ref, other_ref, scales_ref = given
        middle_ref, normed_ref, hidden_ref, slope_ref = made
        (weight,) = scratch

        @pl.when(pl.program_id(0) == 0)
        def _():
            targets = [(0, inner, below(weight, half_rows))]
            for copy in load(depth, place_ref, held[0], sems, targets, up_at):
                copy.wait()

        added = own_ref[...].astype(f32) + other_ref[...].astype(f32)
        middle = rows_ref[...].astype(f32) + added
        middle_ref[...] = middle
        unit_rows, _ = unit_of(middle)
        normed = (unit_rows * scales_ref[2:3, :] + scales_ref[3:4, :]).astype(bf16)
        normed_ref[...] = normed
        for at in range(0, inner, wide):
            hidden, slope = bell_and_slope(mm(normed, weight[:, at : at + wide]))
            hidden_ref[:, at : at + wide] = hidden.astype(bf16)
            slope_ref[:, at : at + wide] = slope.astype(bf16)

    middle, normed_two, hidden, slope = weight_call(
        "widen",
        widen,
        tiles,
        place,
        [
            (inputs, row_block(tile, model)),
            (branch, row_block(tile, model)),
            (branch_other, row_block(tile, model)),
            (scales, whole_block(8, model)),
        ],
        [up_set],
        [
            (far_shape(rows, model, dtype=f32), row_block(tile, model)),
            (far_shape(rows, model), row_block(tile, model)),
            (far_shape(rows, inner), row_block(tile, inner)),
            (far_shape(rows, inner), row_block(tile, inner)),
        ],
        [pltpu.VMEM((model, inner), bf16)],
        copies,
        13,
    )

    if fine_down:
        hidden, slope, normed_two, down_side, down_near = sync(hidden, slope, normed_two, down_side, down_near)
        cuts, hidden = sync(halve(down_side, down_near), hidden)
        down_last = last_quarters(*cuts)
        down_keep, down_send = outer(place, depth, hidden, grad_result)
        hidden, slope, down_keep, down_send, normed_two, down_last = sync(
            hidden, slope, down_keep, down_send, normed_two, down_last
        )
        down_set = [down_part, down_side_own, down_far, down_side, down_near, *down_last]
        down_came = swap(down_send[0], "fx"), swap(down_send[1], "hi")
    else:
        down_keep = down_came = outer_whole(hidden, grad_result)

    def narrow(place_ref, given, held, made, scratch, sems):
        hidden_ref, grad_ref, slope_ref, *downs = given
        out_ref, pre_ref, back_ref = made
        upward = scratch[0]
        down_ref = scratch[1] if fine_down else downs[0]

        @pl.when(pl.program_id(0) == 0)
        def _():
            started = []
            if fine_down:
                targets = [(0, model, below(down_ref, down_rows // 2))]
                started = load(depth, place_ref, held[1], sems, targets, sem=copies)
            targets = [(0, inner, below(upward, half_rows))]
            for copy in started + load(depth, place_ref, held[0], sems, targets, up_at):
                copy.wait()

        for at in range(0, inner, wide):
            grad = mm_cols(grad_ref[...], down_ref[at : at + wide, :])
            pre_ref[:, at : at + wide] = (grad * slope_ref[:, at : at + wide].astype(f32)).astype(bf16)
        back_ref[...] = mm_cols(pre_ref[...], upward[...]).astype(bf16)
        out_ref[...] = mm(hidden_ref[...], down_ref[...]).astype(bf16)

    result, grad_pre, back = weight_call(
        "narrow",
        narrow,
        tiles,
        place,
        [
            (far(hidden), row_block(tile, inner)),
            (far(grad_result), row_block(tile, model)),
            (far(slope), row_block(tile, inner)),
        ]
        + ([] if fine_down else [(far(downward), whole_block(inner, model))]),
        [up_set, down_set] if fine_down else [up_set],
        [
            (far_shape(rows, model), row_block(tile, model)),
            (far_shape(rows, inner), row_block(tile, inner)),
            (far_shape(rows, model), row_block(tile, model)),
        ],
        [pltpu.VMEM((model, inner), bf16), pltpu.VMEM((inner, model), bf16)],
        2 * copies,
        18,
    )
    result, grad_pre, back, normed_two, down_keep, down_came = sync(
        result, grad_pre, back, normed_two, down_keep, down_came
    )

    back_other = other_part(back)
    result_other = other_own(result)
    if fine_down:
        down_kept, down_send = fold_one(place, down_keep, down_came)
        down_kept, down_send, normed_two, grad_pre = sync(down_kept, down_send, normed_two, grad_pre)
        down_came = swap(down_send[0], "hi"), swap(down_send[1], "fx")
    up_keep, up_send = outer(place, depth, far(normed_two), far(grad_pre))
    back, back_other, up_keep, up_send, result_other, down_came = sync(
        back, back_other, up_keep, up_send, result_other, down_came
    )
    if fine_down:
        down_sum, down_send = fold_two(place, down_kept, down_came)
        down_send, back, back_other, up_send = sync(down_send, back, back_other, up_send)
        down_came = [along(value, "fz", depth, k) for k, value in zip(rest, down_send)]

    def between(place_ref, given, held, made, scratch, sems):
        grad_ref, own_ref, other_ref, middle_ref, scales_ref, weight = given
        middle_grad_ref, branch_ref, attended_ref, sums_ref = made

        @pl.when(pl.program_id(0) == 0)
        def _():
            sums_ref[...] = jnp.zeros_like(sums_ref)

        unit_rows, inverse = unit_of(middle_ref[...])
        own_back = own_ref[...].astype(f32)
        back_rows = own_back + other_ref[...].astype(f32)
        sums_ref[0:1, :] += jnp.sum(own_back * unit_rows, axis=0, keepdims=True)
        sums_ref[1:2, :] += jnp.sum(own_back, axis=0, keepdims=True)
        grads = grad_ref[...].astype(f32) + unit_back(back_rows * scales_ref[2:3, :], unit_rows, inverse)
        middle_grad_ref[...] = grads
        low = grads.astype(bf16)
        branch_ref[...] = low
        attended_ref[...] = mm_cols(low, own_out(weight, place_ref)).astype(bf16)

    grad_middle, grad_branch, grad_attended, sums_two = weight_call(
        "between",
        between,
        tiles,
        place,
        [
            (grad_result, row_block(tile, model)),
            (back, row_block(tile, model)),
            (back_other, row_block(tile, model)),
            (far(middle), row_block(tile, model)),
            (scales, whole_block(8, model)),
            (out_weight, whole_block(*out_weight.shape)),
        ],
        [],
        [
            (far_shape(rows, model, dtype=f32), row_block(tile, model)),
            (far_shape(rows, model), row_block(tile, model)),
            (shape_of(rows, head_columns), row_block(tile, head_columns)),
            (shape_of(8, model, dtype=f32), whole_block(8, model)),
        ],
        [],
        1,
        8,
    )
    grad_joints = [attend_back(joint, grad_attended, lses[0], seg_col, seg_row, 0, count)]
    up_came = swap(up_send[0], "fx"), swap(up_send[1], "hi")
    output = (own_chunks(middle) + own_chunks(result).astype(f32) + result_other.astype(f32)).astype(bf16)
    grad_joints, grad_attended, grad_branch, up_came, output, down_came = sync(
        grad_joints, grad_attended, grad_branch, up_came, output, down_came
    )

    def both_halves(value):
        return ordered(value, swap(value, "hi"), h, 1).reshape(-1, value.shape[2])

    norm_parts = dict(weight=joint_weight, scales=scale_columns)
    up_kept, up_send = fold_one(place, up_keep, up_came)
    up_kept, up_send, grad_joints, output = sync(up_kept, up_send, grad_joints, output)
    up_came = swap(up_send[0], "hi"), swap(up_send[1], "fx")
    if fine_down:
        down_own = both_halves(add_up(down_sum, down_came))
    else:
        down_own = lax.psum(lax.psum_scatter(down_came, shard_axes, scatter_dimension=0, tiled=True), "hi")
    one_keep, one_send = outer(
        place,
        depth,
        normed,
        grad_joints[0],
        out_pair=[attended, grad_branch] if fused_out else None,
        sums=sums_two,
        **norm_parts,
    )
    up_came, one_keep, one_send, grad_attended, output, down_own = sync(
        up_came, one_keep, one_send, grad_attended, output, down_own
    )

    up_sum, up_send = fold_two(place, up_kept, up_came)
    up_sum, up_send, grad_attended, one_send = sync(up_sum, up_send, grad_attended, one_send)
    for piece in range(1, pieces):
        grad_joints.append(
            attend_back(joint, grad_attended, lses[piece], seg_col, seg_row, piece * count, count)
        )
    one_came = swap(one_send[0], "fx"), swap(one_send[1], "hi")
    up_came = [along(value, "fz", depth, k) for k, value in zip(rest, up_send)]
    grad_joints, up_came, one_keep, one_came, up_sum, down_own, output = sync(
        grad_joints, up_came, one_keep, one_came, up_sum, down_own, output
    )

    one_kept, one_send = fold_one(place, one_keep, one_came)
    two_came = None
    if pieces == 2:
        two_keep, two_send = outer(
            place, depth, normed, grad_joints[1], piece=1, sums=jnp.zeros_like(sums_two), **norm_parts
        )
        two_send, grad_joints, one_send = sync(two_send, grad_joints, one_send)
        two_came = swap(two_send[0], "fx"), swap(two_send[1], "hi")
    one_came = swap(one_send[0], "hi"), swap(one_send[1], "fx")

    def enter(place_ref, given, held, made, scratch, sems):
        *parts_refs, weight = given
        (out_ref,) = made
        grads = jnp.zeros(out_ref.shape, f32)
        for piece, part_ref in enumerate(parts_refs):
            for j in range(3):
                at = j * head_columns + piece * part_columns
                grads = grads + mm_cols(
                    part_ref[:, j * part_columns : (j + 1) * part_columns], weight[:, at : at + part_columns]
                )
        out_ref[...] = grads.astype(bf16)

    (entered,) = weight_call(
        "enter",
        enter,
        tiles,
        place,
        [(value, row_block(tile, 3 * part_columns)) for value in grad_joints]
        + [(joint_weight, whole_block(*joint_weight.shape))],
        [],
        [(shape_of(rows, model), row_block(tile, model))],
        [],
        1,
        14,
    )
    two_came, one_came, entered, output, up_sum, up_came, down_own = sync(
        two_came, one_came, entered, output, up_sum, up_came, down_own
    )

    if pieces == 2:
        two_kept, two_send = fold_one(place, two_keep, two_came)
        two_came = swap(two_send[0], "hi"), swap(two_send[1], "fx")
    one_sum, one_send = fold_two(place, one_kept, one_came)
    one_came = [along(value, "fz", depth, k) for k, value in zip(rest, one_send)]
    output_came = swap(pick(output, 1 - h, 0), "hi")
    entered_other = other_own(entered)
    grad_normed = own_chunks(entered).astype(f32) + entered_other.astype(f32)
    unit_own, inverse_own = unit_of(own_chunks(inputs).astype(f32))
    grad_tokens = own_chunks(grad_middle) + unit_back(grad_normed * scales[0], unit_own, inverse_own)
    two_came, one_came, output_came, grad_tokens, up_sum, up_came, down_own = sync(
        two_came, one_came, output_came, grad_tokens, up_sum, up_came, down_own
    )

    if pieces == 2:
        two_sum, two_send = fold_two(place, two_kept, two_came)
        two_came = [along(value, "fz", depth, k) for k, value in zip(rest, two_send)]
    up_own = both_halves(add_up(up_sum, up_came))
    grad_came = swap(pick(grad_tokens, 1 - h, 0).astype(bf16), "hi")
    down_all = whole_group(down_own, 0).reshape(-1, model).astype(f32)
    two_came, grad_tokens, grad_came, one_came, up_own = sync(two_came, grad_tokens, grad_came, one_came, up_own)

    owns = [both_halves(add_up(one_sum, one_came))]
    if pieces == 2:
        owns.append(both_halves(add_up(two_sum, two_came)))
    output = ordered(pick(output, h, 0), output_came, h, 0)[:, None]
    grad_tokens = ordered(pick(grad_tokens, h, 0), grad_came.astype(f32), h, 0)[:, None]
    if fused_out:
        up_all = finish_up(place, shards, up_own, swap(up_own, "lo"))
        qkv_all, out_all, sums = finish_qkv(place, owns, [swap(own, "lo") for own in owns])
    else:
        up_all = whole_group(up_own.reshape(own_rows, shards, -1), 2).reshape(own_rows, -1).astype(f32)
        columns = 3 * part_columns
        qkv_own = jnp.concatenate([own[:, :columns].reshape(own_rows, 3, part_columns) for own in owns], axis=2)
        if split_out:
            qkv_all = whole_group(qkv_own.reshape(own_rows, 3, shards, -1), 3)
        else:
            qkv_all = whole_group(qkv_own, 2)
        qkv_all = qkv_all.reshape(own_rows, -1).astype(f32)
        sums = sum(own[:, columns : columns + 4].astype(f32) for own in owns)
        sums = jnp.sum(whole_group(sums, 0), axis=0).T
        grad_out = outer_whole(attended, grad_branch)
        if not split_out:
            empty = jnp.zeros((model, model), bf16)
            grad_out = lax.dynamic_update_slice_in_dim(empty, grad_out, lo * head_columns, 0)
        out_own = lax.psum(lax.psum_scatter(grad_out, shard_axes, scatter_dimension=0, tiled=True), "hi")
        out_all = whole_group(out_own, 0).reshape(own_rows, model) if split_out else lax.psum(out_own, "lo")
        out_all = out_all.astype(f32)

    return (
        output,
        grad_tokens,
        sums[0],
        sums[1],
        qkv_all,
        out_all,
        sums[2],
        sums[3],
        up_all,
        down_all,
    )


def solution(mesh):
    seq, fsdp = mesh.shape["seq"], mesh.shape["fsdp"]
    group, depth = seq // 2, fsdp // 2
    fine = Mesh(mesh.devices.reshape(2, group, depth, 2), ("hi", "lo", "fz", "fx"))
    s, f = ("hi", "lo"), ("fz", "fx")
    return jax.shard_map(
        functools.partial(body, group, depth),
        mesh=fine,
        in_specs=(
            P(None, f, s, None),
            P(None, f, None),
            P(f),
            P(f),
            P(f, None),
            P(f, None),
            P(f),
            P(f),
            P(f, None),
            P(f, None),
            P(None, f, s, None),
        ),
        out_specs=(
            P(None, f, s, None),
            P(None, f, s, None),
            P(f),
            P(f),
            P(f, None),
            P(f, None),
            P(f),
            P(f),
            P(f, None),
            P(f, None),
        ),
        check_vma=False,
    )
```

```python
import functools
import math

import jax
import jax.numpy as jnp
from jax import lax
from jax.experimental import pallas as pl
from jax.experimental.pallas import tpu as pltpu
from jax.sharding import Mesh
from jax.sharding import PartitionSpec as P

HEAD_DIM = 64
DOC_MOST = 512
TILE = 256
LANES = 128
VMEM = 26 * 1024 * 1024
epsilon = 1e-05
SWAP = [(0, 1), (1, 0)]
f32 = jnp.float32
bf16 = jnp.bfloat16


def dot(left, right, dims):
    return lax.dot_general(left, right, (dims, ((), ())), preferred_element_type=f32)


def mm(left, right):
    return dot(left, right, ((1,), (0,)))


def mm_rows(left, right):
    return dot(left, right, ((0,), (0,)))


def mm_cols(left, right):
    return dot(left, right, ((1,), (1,)))


def cost(micros):
    return pl.CostEstimate(flops=int(micros * 1.1e9), bytes_accessed=1000, transcendentals=0)


def far(array):
    return pltpu.with_memory_space_constraint(array, pltpu.HBM)


def sync(*values):
    return lax.optimization_barrier(values)


def pick(array, index, axis):
    return lax.dynamic_index_in_dim(array, index, axis, keepdims=False)


def swap(value, axis):
    return lax.ppermute(value, axis, SWAP)


def ordered(own, other, index, axis):
    first = jnp.where(index == 0, own, other)
    second = jnp.where(index == 0, other, own)
    return jnp.stack([first, second], axis)


def tile_spans(rows):
    tile = min(TILE, rows)
    spans = []
    for start in range(0, rows, tile):
        low = max(0, (start - DOC_MOST + 1) // tile * tile)
        spans.append((start, low, start + tile))
    return tile, spans


def fill_bias(bias, seg_col, seg_row, spans, tile):
    for i, (start, low, high) in enumerate(spans):
        width = high - low
        query_pos = start + lax.broadcasted_iota(jnp.int32, (tile, width), 0)
        key_pos = low + lax.broadcasted_iota(jnp.int32, (tile, width), 1)
        same = seg_col[start : start + tile, :] == seg_row[:, low:high]
        allowed = (key_pos <= query_pos) & same
        bias[i, :, :width] = jnp.where(allowed, 0.0, -1e30).astype(f32)


def pipelined(count, first, second, third):
    current, waiting = first(0), None
    for block in range(count):
        following = first(block + 1) if block + 1 < count else None
        middle = second(block, current)
        if waiting is not None:
            third(*waiting)
        waiting = (block, current, middle)
        current = following
    third(*waiting)


def own_half(left, head, rows):
    return jnp.where(left if head == 0 else ~left, rows, jnp.zeros_like(rows))


def attend_kernel(spans, tile, q_ref, k_ref, v_ref, seg_col, seg_row, out_ref, lse_ref, bias):
    @pl.when(pl.program_id(0) == 0)
    def _():
        fill_bias(bias, seg_col, seg_row, spans, tile)

    left = lax.broadcasted_iota(jnp.int32, (tile, LANES), 1) < HEAD_DIM
    done = {}

    def scores(block):
        (start, low, high), head = spans[block // 2], block % 2
        return mm_cols(own_half(left, head, q_ref[start : start + tile, :]), k_ref[low:high, :])

    def softmax(block, values):
        _, low, high = spans[block // 2]
        values = values + bias[block // 2, :, : high - low]
        top = jnp.max(values, axis=-1, keepdims=True)
        powers = jnp.exp(values - top)
        total = jnp.sum(powers, axis=-1, keepdims=True)
        return powers.astype(bf16), total, top + jnp.log(total)

    def mix(block, _, held):
        (start, low, high), head = spans[block // 2], block % 2
        powers, total, logs = held
        done[head] = mm(powers, v_ref[low:high, :]) * (1.0 / total), logs
        if head == 1:
            rows = slice(start, start + tile)
            out_ref[rows, :] = jnp.where(left, done[0][0], done[1][0]).astype(bf16)
            lse_ref[rows, :] = jnp.where(left, done[0][1], done[1][1])

    pipelined(2 * len(spans), scores, softmax, mix)


def attend(joint, seg_col, seg_row, begin, count):
    rows, width = joint.shape[0], joint.shape[1] // 3
    pairs = width // LANES
    tile, spans = tile_spans(rows)
    widest = max(high - low for _, low, high in spans)

    def part(which):
        return pl.BlockSpec((rows, LANES), lambda p: (0, which * pairs + begin + p))

    out = pl.BlockSpec((rows, LANES), lambda p: (0, p))
    return pl.pallas_call(
        functools.partial(attend_kernel, spans, tile),
        grid=(count,),
        in_specs=[
            part(0),
            part(1),
            part(2),
            pl.BlockSpec((rows, 1), lambda p: (0, 0)),
            pl.BlockSpec((1, rows), lambda p: (0, 0)),
        ],
        out_specs=[out, out],
        out_shape=[
            jax.ShapeDtypeStruct((rows, count * LANES), bf16),
            jax.ShapeDtypeStruct((rows, count * LANES), f32),
        ],
        scratch_shapes=[pltpu.VMEM((len(spans), tile, widest), f32)],
        compiler_params=pltpu.CompilerParams(vmem_limit_bytes=VMEM),
        cost_estimate=cost(4 * count),
        name="attend",
    )(far(joint), far(joint), far(joint), seg_col, seg_row)


def attend_back_kernel(
    spans, tile, q_ref, k_ref, v_ref, g_ref, lse_ref, seg_col, seg_row, out_ref, bias, keys_sum, values_sum
):
    @pl.when(pl.program_id(0) == 0)
    def _():
        fill_bias(bias, seg_col, seg_row, spans, tile)

    keys_sum[...] = jnp.zeros_like(keys_sum)
    values_sum[...] = jnp.zeros_like(values_sum)
    left = lax.broadcasted_iota(jnp.int32, (tile, LANES), 1) < HEAD_DIM
    done = {}

    def products(block):
        (start, low, high), head = spans[block // 2], block % 2
        rows = slice(start, start + tile)
        queries, grads = own_half(left, head, q_ref[rows, :]), own_half(left, head, g_ref[rows, :])
        return queries, grads, mm_cols(queries, k_ref[low:high, :]), mm_cols(grads, v_ref[low:high, :])

    def softmax_back(block, held):
        (start, low, high), lane = spans[block // 2], block % 2 * HEAD_DIM
        _, _, scores, grad_probs = held
        logs = lse_ref[start : start + tile, lane : lane + 1]
        probs = jnp.exp(scores + bias[block // 2, :, : high - low] - logs)
        both = probs * grad_probs
        inner = jnp.sum(both, axis=-1, keepdims=True)
        return (both - probs * inner).astype(bf16), probs.astype(bf16)

    def gather_up(block, held, middle):
        (start, low, high), head = spans[block // 2], block % 2
        queries, grads, _, _ = held
        grad_scores, probs = middle
        done[head] = mm(grad_scores, k_ref[low:high, :])
        keys_sum[low:high, :] += mm_rows(grad_scores, queries)
        values_sum[low:high, :] += mm_rows(probs, grads)
        if head == 1:
            grad_queries = jnp.where(left, done[0], done[1]).astype(bf16)
            out_ref[0, start : start + tile, :] = grad_queries * jnp.asarray(1.0 / math.sqrt(HEAD_DIM), bf16)

    pipelined(2 * len(spans), products, softmax_back, gather_up)
    out_ref[1] = keys_sum[...].astype(bf16)
    out_ref[2] = values_sum[...].astype(bf16)


def attend_back(joint, grads, lse, seg_col, seg_row, begin, count):
    rows, width = joint.shape[0], joint.shape[1] // 3
    pairs = width // LANES
    tile, spans = tile_spans(rows)
    widest = max(high - low for _, low, high in spans)

    def part(which):
        return pl.BlockSpec((rows, LANES), lambda p: (0, which * pairs + begin + p))

    return pl.pallas_call(
        functools.partial(attend_back_kernel, spans, tile),
        grid=(count,),
        in_specs=[
            part(0),
            part(1),
            part(2),
            part(0),
            pl.BlockSpec((rows, LANES), lambda p: (0, p)),
            pl.BlockSpec((rows, 1), lambda p: (0, 0)),
            pl.BlockSpec((1, rows), lambda p: (0, 0)),
        ],
        out_specs=pl.BlockSpec((3, rows, LANES), lambda p: (0, 0, p)),
        out_shape=jax.ShapeDtypeStruct((3, rows, count * LANES), bf16),
        scratch_shapes=[
            pltpu.VMEM((len(spans), tile, widest), f32),
            pltpu.VMEM((rows, LANES), f32),
            pltpu.VMEM((rows, LANES), f32),
        ],
        compiler_params=pltpu.CompilerParams(vmem_limit_bytes=VMEM),
        cost_estimate=cost(6 * count),
        name="attend_back",
    )(far(joint), far(joint), far(joint), grads, lse, seg_col, seg_row)


def shape_of(*shape, dtype=bf16):
    return jax.ShapeDtypeStruct(shape, dtype)


def far_shape(*shape, dtype=bf16):
    return pltpu.HBM(shape, dtype)


def along(value, axis, depth, step):
    return lax.ppermute(value, axis, [(i, (i + step) % depth) for i in range(depth)])


def load(depth, place, pieces, sems, targets, base=0, sem=0):
    z, x, h = place[0], place[1], place[2]
    copies = []

    def put(source, shard, half, at, shift=0):
        for first, columns, where in targets:
            taken = source
            if columns != source.shape[1]:
                taken = source.at[:, shift + first : shift + first + columns]
            copies.append(pltpu.make_async_copy(taken, where(shard, half, at, source.shape[0]), sems.at[sem + len(copies)]))
            copies[-1].start()

    own, side_own, far, side, near, last_side, last_near = pieces
    quarter = last_side.shape[1]
    for at_x, piece in ((x, own), (1 - x, side_own)):
        for half in range(2):
            put(piece.at[half], z * 2 + at_x, half, 0, base)
    for at_x, at_h, at, piece in (
        (x, h, 0, far),
        (1 - x, h, 0, side),
        (x, 1 - h, 0, near),
        (1 - x, 1 - h, 0, last_side),
        (1 - x, 1 - h, quarter, last_near),
    ):
        for k in range(1, depth):
            put(piece.at[k - 1], lax.rem(z - k + depth, depth) * 2 + at_x, at_h, at)
    return copies


def below(weight, half_rows):
    def where(shard, half, at, count):
        first = pl.multiple_of((shard * 2 + half) * half_rows + at, math.gcd(half_rows, at))
        return weight.at[pl.ds(first, count), :]

    return where


def halve(side, near):
    count, rows, columns = side.shape
    half = rows // 2

    def kernel(side_ref, near_ref, one_ref, two_ref):
        one_ref[...] = side_ref[:, :half, :]
        two_ref[...] = near_ref[:, half:, :]

    return pl.pallas_call(
        kernel,
        in_specs=[pl.BlockSpec(memory_space=pltpu.VMEM)] * 2,
        out_specs=[pl.BlockSpec(memory_space=pltpu.VMEM)] * 2,
        out_shape=[shape_of(count, half, columns)] * 2,
        compiler_params=pltpu.CompilerParams(vmem_limit_bytes=VMEM),
        cost_estimate=cost(1),
        name="halve",
    )(side, near)


def prepare(place, shards, w_qkv, w_out, w_up, vectors):
    rows, model = w_out.shape
    half, blocks = rows // 2, w_qkv.shape[1] // LANES
    qkv_columns, wide = w_qkv.shape[1] // 2, w_up.shape[1] // 2
    scale_at = qkv_columns
    out_at = scale_at + LANES
    up_at = out_at + model // 2
    unit = wide // shards

    def kernel(place_ref, qkv_ref, out_ref, up_ref, vectors_ref, own_ref, first_ref, up_half_ref):
        lo, h = place_ref[3], place_ref[2]
        left = lax.broadcasted_iota(jnp.int32, (rows, LANES), 1) < HEAD_DIM

        def put(at, value):
            own_ref[0, :, at : at + value.shape[1]] = value[:half]
            own_ref[1, :, at : at + value.shape[1]] = value[half:]

        for block in range(0, blocks, 2):
            one = qkv_ref[:, block * LANES : (block + 1) * LANES].astype(f32)
            two = qkv_ref[:, (block + 1) * LANES : (block + 2) * LANES].astype(f32)
            even = jnp.where(left, one, pltpu.roll(two, HEAD_DIM, 1))
            odd = jnp.where(left, pltpu.roll(one, HEAD_DIM, 1), two)
            put(block // 2 * LANES, jnp.where(lo == 0, even, odd).astype(bf16))
        columns = jnp.concatenate([vectors_ref[...].astype(f32), jnp.zeros((LANES - 4, rows), f32)], axis=0)
        put(scale_at, columns.T.astype(bf16))
        outs = jnp.where(lo == 0, out_ref[:half, :], out_ref[half:, :])
        put(out_at, jnp.concatenate([outs[:, : model // 2], outs[:, model // 2 :]], axis=0))
        for shard in range(shards):
            at = shard * 2 * unit
            put(up_at + shard * unit, jnp.where(lo == 0, up_ref[:, at : at + unit], up_ref[:, at + unit : at + 2 * unit]))
        first_ref[...] = own_ref[h, :, :up_at]
        up_half_ref[...] = own_ref[h, :, up_at:]

    return pl.pallas_call(
        kernel,
        in_specs=[pl.BlockSpec(memory_space=pltpu.SMEM)] + [pl.BlockSpec(memory_space=pltpu.VMEM)] * 4,
        out_specs=[pl.BlockSpec(memory_space=pltpu.VMEM)] * 3,
        out_shape=[shape_of(2, half, up_at + wide), shape_of(half, up_at), shape_of(half, wide)],
        compiler_params=pltpu.CompilerParams(vmem_limit_bytes=VMEM),
        cost_estimate=cost(2),
        name="prepare",
    )(place, far(w_qkv), far(w_out), far(w_up), vectors)


def finish_up(place, shards, own, other):
    rows, columns = own.shape
    unit = columns // shards

    def kernel(place_ref, own_ref, other_ref, out_ref):
        lo = place_ref[3]
        for shard in range(shards):
            at, mine, theirs = shard * 2 * unit, own_ref, other_ref
            one = mine[:, shard * unit : (shard + 1) * unit].astype(f32)
            two = theirs[:, shard * unit : (shard + 1) * unit].astype(f32)
            out_ref[:, at : at + unit] = jnp.where(lo == 0, one, two)
            out_ref[:, at + unit : at + 2 * unit] = jnp.where(lo == 0, two, one)

    return pl.pallas_call(
        kernel,
        in_specs=[pl.BlockSpec(memory_space=pltpu.SMEM)] + [pl.BlockSpec(memory_space=pltpu.VMEM)] * 2,
        out_specs=pl.BlockSpec(memory_space=pltpu.VMEM),
        out_shape=shape_of(rows, 2 * columns, dtype=f32),
        cost_estimate=cost(2),
        name="finish_up",
    )(place, own, other)


def finish_qkv(place, columns, owns, others):
    rows = owns[0].shape[0]
    half, pieces = rows // 2, len(owns)
    third = columns // 3
    model = 2 * (owns[0].shape[1] - columns - LANES)

    def kernel(place_ref, *refs):
        lo = place_ref[3]
        owns_refs, others_refs = refs[:pieces], refs[pieces : 2 * pieces]
        qkv_ref, out_ref, sums_ref = refs[2 * pieces :]
        left = lax.broadcasted_iota(jnp.int32, (rows, LANES), 1) < HEAD_DIM
        at = 0
        for j in range(3):
            for own_ref, other_ref in zip(owns_refs, others_refs):
                for first in range(j * third, (j + 1) * third, LANES):
                    mine = own_ref[:, first : first + LANES].astype(f32)
                    theirs = other_ref[:, first : first + LANES].astype(f32)
                    one, two = jnp.where(lo == 0, mine, theirs), jnp.where(lo == 0, theirs, mine)
                    qkv_ref[:, at : at + LANES] = jnp.where(left, one, pltpu.roll(two, HEAD_DIM, 1))
                    qkv_ref[:, at + LANES : at + 2 * LANES] = jnp.where(left, pltpu.roll(one, HEAD_DIM, 1), two)
                    at += 2 * LANES
        sums = jnp.zeros((rows, LANES), f32)
        for ref in refs[: 2 * pieces]:
            sums = sums + ref[:, columns : columns + LANES].astype(f32)
        sums_ref[...] = sums.T[:8, :]
        mine, theirs = (ref[:, columns + LANES :].astype(f32) for ref in (owns_refs[0], others_refs[0]))
        for at, value in ((0, jnp.where(lo == 0, mine, theirs)), (half, jnp.where(lo == 0, theirs, mine))):
            out_ref[at : at + half, : model // 2] = value[:half]
            out_ref[at : at + half, model // 2 :] = value[half:]

    return pl.pallas_call(
        kernel,
        in_specs=[pl.BlockSpec(memory_space=pltpu.SMEM)] + [pl.BlockSpec(memory_space=pltpu.VMEM)] * (2 * pieces),
        out_specs=[pl.BlockSpec(memory_space=pltpu.VMEM)] * 3,
        out_shape=[
            shape_of(rows, 2 * pieces * columns, dtype=f32),
            shape_of(rows, model, dtype=f32),
            shape_of(8, rows, dtype=f32),
        ],
        compiler_params=pltpu.CompilerParams(vmem_limit_bytes=VMEM),
        cost_estimate=cost(2),
        name="finish_qkv",
    )(place, *owns, *others)


def plus(left, right):
    return (left.astype(f32) + right.astype(f32)).astype(bf16)


def fold_one(place, keep, came, shape=shape_of):
    depth, top, columns = keep[0].shape
    low = top // 2

    def kernel(place_ref, keep_one, keep_two, came_one, came_two, kept_ref, send_one, send_two):
        at_x, at_h = place_ref[1] == 0, place_ref[2] == 0
        one, two = plus(keep_one[0], came_one[0]), plus(keep_two[0], came_two[0])
        kept_ref[0, 0] = jnp.where(at_h, one[:low], one[low:])
        send_one[0] = jnp.where(at_h, one[low:], one[:low])
        kept_ref[1, 0] = jnp.where(at_x, two[0], two[1])
        send_two[0] = jnp.where(at_x, two[1], two[0])

    one = pl.BlockSpec((1, top, columns), lambda i: (i, 0, 0))
    two = pl.BlockSpec((1, 2, low, columns), lambda i: (i, 0, 0, 0))
    send = pl.BlockSpec((1, low, columns), lambda i: (i, 0, 0))
    kept, *sends = pl.pallas_call(
        kernel,
        grid=(depth,),
        in_specs=[pl.BlockSpec(memory_space=pltpu.SMEM), one, two, one, two],
        out_specs=[pl.BlockSpec((2, 1, low, columns), lambda i: (0, i, 0, 0)), send, send],
        out_shape=[shape(2, depth, low, columns)] + [shape(depth, low, columns)] * 2,
        compiler_params=pltpu.CompilerParams(vmem_limit_bytes=VMEM),
        cost_estimate=cost(1),
        name="fold_one",
    )(place, *keep, *came)
    return kept, sends


def fold_two(place, kept, came):
    _, depth, low, columns = kept.shape

    def kernel(place_ref, kept_ref, came_one, came_two, *refs):
        *outs, sums = refs
        for half, came_ref in enumerate((came_one, came_two)):
            for at in range(depth):
                sums[at, half] = plus(kept_ref[half, at], came_ref[at])
        for k, out in enumerate(outs):
            out[...] = sums[lax.rem(place_ref[0] + k, depth)]

    own, *sends = pl.pallas_call(
        kernel,
        in_specs=[pl.BlockSpec(memory_space=pltpu.SMEM)] + [pl.BlockSpec(memory_space=pltpu.VMEM)] * 3,
        out_specs=[pl.BlockSpec(memory_space=pltpu.VMEM)] * depth,
        out_shape=[shape_of(2, low, columns)] * depth,
        scratch_shapes=[pltpu.VMEM((depth, 2, low, columns), bf16)],
        compiler_params=pltpu.CompilerParams(vmem_limit_bytes=VMEM),
        cost_estimate=cost(1),
        name="fold_two",
    )(place, kept, *came)
    return own, sends


def add_up(own, came):
    total = own.astype(f32)
    for piece in came:
        total = total + piece.astype(f32)
    return total.astype(bf16)


def row_block(tile, width):
    return pl.BlockSpec((tile, width), lambda i: (i, 0))


def whole_block(*shape):
    return pl.BlockSpec(shape, lambda i: (0,) * len(shape))


def weight_call(name, step, tiles, place, inputs, sets, outs, scratch, copies, micros):
    pieces = [piece for held in sets for piece in held]

    def kernel(place_ref, *refs):
        refs = list(refs)

        def take(count):
            taken = refs[:count]
            del refs[:count]
            return taken

        given = take(len(inputs))
        held = [take(len(one)) for one in sets]
        made = take(len(outs))
        step(place_ref, given, held, made, refs[:-1], refs[-1])

    return pl.pallas_call(
        kernel,
        grid=(tiles,),
        in_specs=[pl.BlockSpec(memory_space=pltpu.SMEM)]
        + [spec for _, spec in inputs]
        + [pl.BlockSpec(memory_space=pltpu.HBM)] * len(pieces),
        out_specs=[spec for _, spec in outs],
        out_shape=[shape for shape, _ in outs],
        scratch_shapes=list(scratch) + [pltpu.SemaphoreType.DMA((copies,))],
        compiler_params=pltpu.CompilerParams(vmem_limit_bytes=VMEM),
        cost_estimate=cost(micros),
        name=name,
    )(place, *[v for v, _ in inputs], *[far(piece) for piece in pieces])


def unit_of(values):
    centred = values - jnp.mean(values, axis=-1, keepdims=True)
    variance = jnp.mean(centred * centred, axis=-1, keepdims=True)
    inverse = lax.rsqrt(variance + epsilon)
    return centred * inverse, inverse


def unit_back(grad_unit, unit_rows, inverse):
    mean_grad = jnp.mean(grad_unit, axis=-1, keepdims=True)
    mean_cross = jnp.mean(grad_unit * unit_rows, axis=-1, keepdims=True)
    return inverse * (grad_unit - mean_grad - unit_rows * mean_cross)


def bell_and_slope(values):
    phi = 0.5 + 0.5 * lax.erf(values * math.sqrt(0.5))
    density = jnp.exp(values * values * -0.5) * (1.0 / math.sqrt(2.0 * math.pi))
    return values * phi, phi + values * density


def outer_whole(left, right):
    rows, across = left.shape
    block = min(256, across)

    def kernel(left_ref, right_ref, out_ref):
        out_ref[...] = mm_rows(left_ref[...], right_ref[...]).astype(bf16)

    return pl.pallas_call(
        kernel,
        grid=(across // block,),
        in_specs=[pl.BlockSpec((rows, block), lambda i: (0, i)), whole_block(*right.shape)],
        out_specs=row_block(block, right.shape[1]),
        out_shape=shape_of(across, right.shape[1]),
        compiler_params=pltpu.CompilerParams(vmem_limit_bytes=VMEM),
        cost_estimate=cost(7),
        name="outer_whole",
    )(left, right)


def outer(place, depth, left, right, out_pair=None, weight=None, scales=None, piece=0, sums=None):
    rows, own_rows = left.shape[0], left.shape[1] // (2 * depth)
    top, low = own_rows // 2, own_rows // 4
    parts = right.shape[0] if right.ndim == 3 else 1
    third = right.shape[-1]
    columns = parts * third
    given = [left, right]
    specs = [pl.BlockSpec((rows, 2 * own_rows), lambda i: (0, i)), whole_block(*right.shape)]
    total = columns
    if weight is not None:
        given += [weight, scales, sums]
        specs += [pl.BlockSpec((2 * own_rows, part.shape[1]), lambda i: (i, 0)) for part in (weight, scales)]
        specs.append(pl.BlockSpec((8, 2 * own_rows), lambda i: (0, i)))
        total += LANES
        width = weight.shape[1] // 3
    if out_pair is not None:
        out_block = out_pair[0].shape[1] // depth
        given += out_pair
        specs += [pl.BlockSpec((rows, out_block), lambda i: (0, i)), whole_block(*out_pair[1].shape)]
        half = out_pair[1].shape[1] // 2
        total += half

    def kernel(place_ref, *refs):
        ins, outs = list(refs[: len(given)]), refs[len(given) :]
        at_x, at_h = place_ref[1] == 0, place_ref[2] == 0
        keep_first, send_first, keep_second, send_second = outs

        def put(first, value):
            where = slice(first, first + value.shape[2])
            heads = value[:, :top].astype(bf16)
            keep_first[0, :, where] = jnp.where(at_x, heads[0], heads[1])
            send_first[0, :, where] = jnp.where(at_x, heads[1], heads[0])
            lower, upper = value[:, top : top + low].astype(bf16), value[:, top + low :].astype(bf16)
            keep_second[0, :, :, where] = jnp.where(at_h, lower, upper)
            send_second[0, :, :, where] = jnp.where(at_h, upper, lower)

        left_ref, right_ref = ins.pop(0), ins.pop(0)
        rights = [right_ref.at[j] for j in range(parts)] if parts > 1 else [right_ref]
        products = [mm_rows(left_ref[...], ref[...]) for ref in rights]
        for j, product in enumerate(products):
            put(j * third, product.reshape(2, own_rows, third))
        first = columns
        if weight is not None:
            weight_ref, scales_ref, sums_ref = ins.pop(0), ins.pop(0), ins.pop(0)
            bias_sum = cross = 0.0
            for j, product in enumerate(products):
                at = j * width + piece * third
                part = weight_ref[:, at : at + third].astype(f32)
                column_sums = jnp.sum(rights[j][...].astype(f32), axis=0, keepdims=True)
                bias_sum = bias_sum + jnp.sum(part * column_sums, axis=1, keepdims=True)
                cross = cross + jnp.sum(part * product, axis=1, keepdims=True)
            gain, bias = scales_ref[:, 0:1].astype(f32), scales_ref[:, 1:2].astype(f32)
            gain_sum = (cross - bias * bias_sum) / gain
            kept = jnp.concatenate(
                [jnp.zeros((2, 2 * own_rows), f32), sums_ref[0:2, :], jnp.zeros((LANES - 4, 2 * own_rows), f32)], axis=0
            ).T
            lane = lax.broadcasted_iota(jnp.int32, kept.shape, 1)
            kept = jnp.where(lane == 0, gain_sum, jnp.where(lane == 1, bias_sum, kept))
            put(first, kept.reshape(2, own_rows, LANES))
            first += LANES
        if out_pair is not None:
            product = mm_rows(ins.pop(0)[...], ins.pop(0)[...]).reshape(2, top, 2 * half)
            put(first, jnp.concatenate([product[:, :, :half], product[:, :, half:]], axis=1))

    def spec(*block):
        return pl.BlockSpec((1, *block), lambda i: (i,) + (0,) * len(block))

    first_shape, second_shape = (top, total), (2, low, total)
    made = pl.pallas_call(
        kernel,
        grid=(depth,),
        in_specs=[pl.BlockSpec(memory_space=pltpu.SMEM)] + specs,
        out_specs=[spec(*first_shape)] * 2 + [spec(*second_shape)] * 2,
        out_shape=[shape_of(depth, *first_shape)] * 2 + [shape_of(depth, *second_shape)] * 2,
        compiler_params=pltpu.CompilerParams(vmem_limit_bytes=VMEM),
        cost_estimate=cost(6),
        name="outer",
    )(place, *given)
    return (made[0], made[2]), (made[1], made[3])


def body(
    group,
    depth,
    tokens,
    segment_ids,
    norm1_gain,
    norm1_bias,
    w_qkv,
    w_out,
    norm2_gain,
    norm2_bias,
    w_up,
    w_down,
    cotangent,
):
    h, lo = lax.axis_index("hi"), lax.axis_index("lo")
    z, x = lax.axis_index("fz"), lax.axis_index("fx")
    micro, _, chunk, model = tokens.shape
    shards = 2 * depth
    rows = micro * group * chunk
    own_rows = w_out.shape[0]
    inner = w_up.shape[1] // group
    split_out = (own_rows // HEAD_DIM) % group == 0
    head_columns = model // group
    half_rows = own_rows // 2
    tile = min(TILE, rows)
    tiles = rows // tile
    scale_at = 3 * head_columns
    copies = 4 * shards
    wide = min(512, inner)
    shard_axes = ("fz", "fx")

    rest = range(1, depth)

    def whole_group(value, axis):
        if group == 2:
            return ordered(value, swap(value, "lo"), lo, axis)
        return lax.all_gather(value, "lo", axis=axis)

    def other_part(partial):
        if group == 2:
            return swap(partial, "lo")
        return (lax.psum(partial, "lo").astype(f32) - partial.astype(f32)).astype(bf16)

    def own_chunks(full):
        return pick(full.reshape(micro, group, chunk, -1), lo, 1)

    def other_own(partial):
        parts = partial.reshape(micro, group, chunk, model)
        if group == 2:
            return swap(pick(parts, 1 - lo, 1), "lo")
        return plus(lax.psum_scatter(parts, "lo", scatter_dimension=1), -pick(parts, lo, 1))

    def hop(values, parity):
        return [along(value, "fz", depth, k) for k, value in zip(rest, values) if k % 2 == parity]

    fused_out = split_out and group == 2
    out_rows, half_model = own_rows // group, model // 2
    place = jnp.stack([z, x, h, lo]).astype(jnp.int32)
    came = swap(jnp.stack([pick(tokens[:, 0], 1 - h, 0), pick(cotangent[:, 0], 1 - h, 0)]), "hi")
    vectors = jnp.stack([norm1_gain, norm1_bias, norm2_gain, norm2_bias])
    if fused_out:
        both_own, first_half, up_half = prepare(place, shards, w_qkv, w_out, w_up, vectors)
    else:
        if split_out:
            qkv_part = pick(w_qkv.reshape(own_rows, 3, shards, group, -1), lo, 3).reshape(own_rows, -1)
            out_part = pick(w_out.reshape(group, out_rows, model), lo, 0)
        else:
            qkv_part = pick(w_qkv.reshape(own_rows, 3, group, -1), lo, 2).reshape(own_rows, -1)
            out_part = w_out
        up_part = pick(w_up.reshape(own_rows, shards, group, -1), lo, 2).reshape(own_rows, -1)
        parts = [qkv_part, jnp.pad(vectors.T, ((0, 0), (0, LANES - 4)))]
        both_own = jnp.concatenate(parts + [up_part], axis=1).reshape(2, half_rows, -1)
        half = pick(both_own, h, 0)
        first_half, up_half = half[:, : scale_at + LANES], half[:, scale_at + LANES :]
        out_weight = lax.all_gather(out_part, shard_axes, axis=0, tiled=True)
    up_at = first_half.shape[1]
    down_rows = inner // shards
    fine_down = down_rows % 64 == 0
    down_part = pick(w_down.reshape(group, 2, down_rows // 2, model), lo, 0)
    first_far = [along(first_half, "fz", depth, k) for k in rest]
    side_own = swap(both_own, "fx")
    first_far, side_own, came, up_half = sync(first_far, side_own, came, up_half)

    def last_quarters(side_part, near_part):
        return swap(side_part, "hi"), swap(near_part, "fx")

    first_far = jnp.stack(first_far)
    first_side, first_near = swap(first_far, "fx"), swap(first_far, "hi")
    up_far = [along(up_half, "fz", depth, k) for k in rest]
    first_side, first_near, up_far, came, down_part = sync(first_side, first_near, up_far, came, down_part)

    cuts, came, tokens, up_far = sync(halve(first_side, first_near), came, tokens, up_far)
    first_last = last_quarters(*cuts)
    down_half = pick(down_part, h, 0)
    if not fine_down:
        downward = lax.all_gather(down_part.reshape(down_rows, model), shard_axes, axis=0, tiled=True)
    inputs = whole_group(ordered(pick(tokens[:, 0], h, 0), came[0], h, 0), 1).reshape(rows, model)
    up_far = jnp.stack(up_far)
    first_last, inputs, up_far, came, down_half, down_part = sync(
        first_last, inputs, up_far, came, down_half, down_part
    )
    first_set = [both_own, side_own, first_far, first_side, first_near, *first_last]

    segments = pick(segment_ids[:, 0], h, 0)
    seg_col, seg_row = segments[:, None], segments[None, :]

    def project(place_ref, given, held, made, scratch, sems):
        (rows_ref,), (normed_ref, joint_ref, scales_ref, weight, columns, *outs) = given, made

        @pl.when(pl.program_id(0) == 0)
        def _():
            targets = [
                (0, 3 * head_columns, below(weight, half_rows)),
                (scale_at, LANES, below(columns, half_rows)),
            ]
            if fused_out:
                targets.append((scale_at + LANES, half_model, below(scratch[0], half_rows)))
            for copy in load(depth, place_ref, held[0], sems, targets):
                copy.wait()
            scales_ref[...] = columns[...].astype(f32).T[:8, :]
            for shard in range(shards if fused_out else 0):
                for part in range(2):
                    at = shard * own_rows + part * out_rows
                    outs[0][
                        shard * out_rows : (shard + 1) * out_rows, part * half_model : (part + 1) * half_model
                    ] = scratch[0][at : at + out_rows, :]

        unit_rows, _ = unit_of(rows_ref[...].astype(f32))
        normed = (unit_rows * scales_ref[0:1, :] + scales_ref[1:2, :]).astype(bf16)
        normed_ref[...] = normed
        for at in range(0, 3 * head_columns, head_columns):
            part = mm(normed, weight[:, at : at + head_columns])
            if at == 0:
                part = part * (1.0 / math.sqrt(HEAD_DIM))
            joint_ref[:, at : at + head_columns] = part.astype(bf16)

    wholes = [(8, model, f32), (model, 3 * head_columns, bf16), (model, LANES, bf16)]
    if fused_out:
        wholes.append((head_columns, model, bf16))
    normed, joint, scales, joint_weight, scale_columns, *outs = weight_call(
        "project",
        project,
        tiles,
        place,
        [(inputs, row_block(tile, model))],
        [first_set],
        [
            (far_shape(rows, model), row_block(tile, model)),
            (far_shape(rows, 3 * head_columns), row_block(tile, 3 * head_columns)),
        ]
        + [(shape_of(*shape, dtype=dtype), whole_block(*shape)) for *shape, dtype in wholes],
        [pltpu.VMEM((model, half_model), bf16)] if fused_out else [],
        3 * copies,
        8,
    )
    if fused_out:
        (out_weight,) = outs
    pairs = head_columns // LANES
    pieces = 2 if pairs % 2 == 0 else 1
    count = pairs // pieces
    part_columns = count * LANES
    mixed = [attend(joint, seg_col, seg_row, 0, count)]
    up_side, up_near = swap(up_far, "fx"), swap(up_far, "hi")
    down_odd = down_even = down_side_own = None
    if fine_down:
        down_odd = [along(down_half, "fz", depth, k) for k in rest if k % 2]
        down_side_own = swap(down_part, "fx")
    mixed, joint, up_side, up_near, scales, out_weight, came, down_odd, down_side_own, down_half = sync(
        mixed, joint, up_side, up_near, scales, out_weight, came, down_odd, down_side_own, down_half
    )

    cuts, joint, came, down_half = sync(halve(up_side, up_near), joint, came, down_half)
    up_last = last_quarters(*cuts)
    for piece in range(1, pieces):
        mixed.append(attend(joint, seg_col, seg_row, piece * count, count))
    grad_result = whole_group(ordered(pick(cotangent[:, 0], h, 0), came[1], h, 0), 1).reshape(rows, model)
    if fine_down:
        down_even = [along(down_half, "fz", depth, k) for k in rest if k % 2 == 0]
    mixed, up_last, out_weight, grad_result, down_even = sync(mixed, up_last, out_weight, grad_result, down_even)
    up_set = [both_own, side_own, up_far, up_side, up_near, *up_last]
    lse = mixed[0][1] if pieces == 1 else jnp.concatenate([part for _, part in mixed], axis=1)

    def leave(place_ref, given, held, made, scratch, sems):
        *parts_refs, weight = given
        out_ref, attended_ref = made
        weight = own_out(weight, place_ref)
        total = jnp.zeros(out_ref.shape, f32)
        for piece, part_ref in enumerate(parts_refs):
            at = slice(piece * part_columns, (piece + 1) * part_columns)
            attended_ref[:, at] = part_ref[...]
            total = total + mm(part_ref[...], weight[at, :])
        out_ref[...] = total.astype(bf16)

    def own_out(weight, place_ref):
        if split_out:
            return weight[...]
        return weight[pl.ds(pl.multiple_of(place_ref[3] * head_columns, head_columns), head_columns), :]

    branch, attended = weight_call(
        "leave",
        leave,
        tiles,
        place,
        [(value, row_block(tile, part_columns)) for value, _ in mixed]
        + [(out_weight, whole_block(*out_weight.shape))],
        [],
        [
            (shape_of(rows, model), row_block(tile, model)),
            (shape_of(rows, head_columns), row_block(tile, head_columns)),
        ],
        [],
        1,
        3,
    )
    branch_other = other_part(branch)

    if fine_down:
        down_far = jnp.stack([down_odd[k // 2] if k % 2 else down_even[k // 2 - 1] for k in rest])
        down_side, down_near = swap(down_far, "fx"), swap(down_far, "hi")

    def widen(place_ref, given, held, made, scratch, sems):
        rows_ref, own_ref, other_ref, scales_ref = given
        middle_ref, normed_ref, hidden_ref, slope_ref = made
        (weight,) = scratch

        @pl.when(pl.program_id(0) == 0)
        def _():
            targets = [(0, inner, below(weight, half_rows))]
            for copy in load(depth, place_ref, held[0], sems, targets, up_at):
                copy.wait()

        added = own_ref[...].astype(f32) + other_ref[...].astype(f32)
        middle = rows_ref[...].astype(f32) + added
        middle_ref[...] = middle
        unit_rows, _ = unit_of(middle)
        normed = (unit_rows * scales_ref[2:3, :] + scales_ref[3:4, :]).astype(bf16)
        normed_ref[...] = normed
        for at in range(0, inner, wide):
            hidden, slope = bell_and_slope(mm(normed, weight[:, at : at + wide]))
            hidden_ref[:, at : at + wide] = hidden.astype(bf16)
            slope_ref[:, at : at + wide] = slope.astype(bf16)

    middle, normed_two, hidden, slope = weight_call(
        "widen",
        widen,
        tiles,
        place,
        [
            (inputs, row_block(tile, model)),
            (branch, row_block(tile, model)),
            (branch_other, row_block(tile, model)),
            (scales, whole_block(8, model)),
        ],
        [up_set],
        [
            (far_shape(rows, model, dtype=f32), row_block(tile, model)),
            (far_shape(rows, model), row_block(tile, model)),
            (far_shape(rows, inner), row_block(tile, inner)),
            (far_shape(rows, inner), row_block(tile, inner)),
        ],
        [pltpu.VMEM((model, inner), bf16)],
        copies,
        13,
    )

    if fine_down:
        hidden, slope, normed_two, down_side, down_near = sync(hidden, slope, normed_two, down_side, down_near)
        cuts, hidden = sync(halve(down_side, down_near), hidden)
        down_last = last_quarters(*cuts)
        down_keep, down_send = outer(place, depth, far(hidden), grad_result)
        hidden, slope, down_keep, down_send, normed_two, down_last = sync(
            hidden, slope, down_keep, down_send, normed_two, down_last
        )
        down_set = [down_part, down_side_own, down_far, down_side, down_near, *down_last]
        down_came = swap(down_send[0], "fx"), swap(down_send[1], "hi")
    else:
        down_keep = down_came = outer_whole(hidden, grad_result)
        down_send = None

    def narrow(place_ref, given, held, made, scratch, sems):
        hidden_ref, grad_ref, slope_ref, *downs = given
        out_ref, pre_ref, back_ref = made
        upward = scratch[0]
        down_ref = scratch[1] if fine_down else downs[0]

        @pl.when(pl.program_id(0) == 0)
        def _():
            started = []
            if fine_down:
                targets = [(0, model, below(down_ref, down_rows // 2))]
                started = load(depth, place_ref, held[1], sems, targets, sem=copies)
            targets = [(0, inner, below(upward, half_rows))]
            for copy in started + load(depth, place_ref, held[0], sems, targets, up_at):
                copy.wait()

        for at in range(0, inner, wide):
            grad = mm_cols(grad_ref[...], down_ref[at : at + wide, :])
            pre_ref[:, at : at + wide] = (grad * slope_ref[:, at : at + wide].astype(f32)).astype(bf16)
        back_ref[...] = mm_cols(pre_ref[...], upward[...]).astype(bf16)
        out_ref[...] = mm(hidden_ref[...], down_ref[...]).astype(bf16)

    result, grad_pre, back = weight_call(
        "narrow",
        narrow,
        tiles,
        place,
        [
            (far(hidden), row_block(tile, inner)),
            (far(grad_result), row_block(tile, model)),
            (far(slope), row_block(tile, inner)),
        ]
        + ([] if fine_down else [(far(downward), whole_block(inner, model))]),
        [up_set, down_set] if fine_down else [up_set],
        [
            (far_shape(rows, model), row_block(tile, model)),
            (far_shape(rows, inner), row_block(tile, inner)),
            (far_shape(rows, model), row_block(tile, model)),
        ],
        [pltpu.VMEM((model, inner), bf16), pltpu.VMEM((inner, model), bf16)],
        2 * copies,
        18,
    )
    down_kept = None
    if fine_down:
        down_kept, down_send = fold_one(place, down_keep, down_came, far_shape)
    result, grad_pre, back, normed_two, down_kept, down_send, down_came = sync(
        result, grad_pre, back, normed_two, down_kept, down_send, down_came
    )

    back_other = other_part(back)
    result_other = other_own(result)
    if fine_down:
        down_came = swap(down_send[0], "hi"), swap(down_send[1], "fx")
    up_keep, up_send = outer(place, depth, far(normed_two), far(grad_pre))
    output = (own_chunks(middle) + own_chunks(result).astype(f32) + result_other.astype(f32)).astype(bf16)
    back, back_other, up_keep, up_send, down_came, output = sync(
        back, back_other, up_keep, up_send, down_came, output
    )
    if fine_down:
        down_sum, down_send = fold_two(place, down_kept, down_came)
        down_send, back, back_other, up_send = sync(down_send, back, back_other, up_send)
        down_came = hop(down_send, 1)

    def between(place_ref, given, held, made, scratch, sems):
        grad_ref, own_ref, other_ref, middle_ref, scales_ref, weight = given
        middle_grad_ref, branch_ref, attended_ref, sums_ref = made

        @pl.when(pl.program_id(0) == 0)
        def _():
            sums_ref[...] = jnp.zeros_like(sums_ref)

        unit_rows, inverse = unit_of(middle_ref[...])
        own_back = own_ref[...].astype(f32)
        back_rows = own_back + other_ref[...].astype(f32)
        sums_ref[0:1, :] += jnp.sum(own_back * unit_rows, axis=0, keepdims=True)
        sums_ref[1:2, :] += jnp.sum(own_back, axis=0, keepdims=True)
        grads = grad_ref[...].astype(f32) + unit_back(back_rows * scales_ref[2:3, :], unit_rows, inverse)
        middle_grad_ref[...] = grads
        low = grads.astype(bf16)
        branch_ref[...] = low
        attended_ref[...] = mm_cols(low, own_out(weight, place_ref)).astype(bf16)

    grad_middle, grad_branch, grad_attended, sums_two = weight_call(
        "between",
        between,
        tiles,
        place,
        [
            (grad_result, row_block(tile, model)),
            (back, row_block(tile, model)),
            (back_other, row_block(tile, model)),
            (far(middle), row_block(tile, model)),
            (scales, whole_block(8, model)),
            (out_weight, whole_block(*out_weight.shape)),
        ],
        [],
        [
            (far_shape(rows, model, dtype=f32), row_block(tile, model)),
            (far_shape(rows, model), row_block(tile, model)),
            (shape_of(rows, head_columns), row_block(tile, head_columns)),
            (shape_of(8, model, dtype=f32), whole_block(8, model)),
        ],
        [],
        1,
        8,
    )
    if fine_down:
        grad_attended, down_came, down_send = sync(grad_attended, down_came, down_send)
        down_came = down_came + hop(down_send, 0)
    grad_joint = attend_back(joint, grad_attended, lse, seg_col, seg_row, 0, pairs)
    up_came = swap(up_send[0], "fx"), swap(up_send[1], "hi")
    output_came = swap(pick(output, 1 - h, 0), "hi")
    if fine_down:
        down_came = add_up(down_sum, down_came)
    grad_joint, grad_branch, up_came, output_came, down_came = sync(
        grad_joint, grad_branch, up_came, output_came, down_came
    )

    def both_halves(value):
        return ordered(value, swap(value, "hi"), h, 1).reshape(-1, value.shape[2])

    up_kept, up_send = fold_one(place, up_keep, up_came)
    up_kept, up_send, grad_joint = sync(up_kept, up_send, grad_joint)
    up_came = swap(up_send[0], "hi"), swap(up_send[1], "fx")
    if fine_down:
        down_own = both_halves(down_came)
    else:
        down_own = lax.psum(lax.psum_scatter(down_came, shard_axes, scatter_dimension=0, tiled=True), "hi")
    last_keep, last_send = outer(
        place,
        depth,
        normed,
        grad_joint,
        out_pair=[attended, grad_branch] if fused_out else None,
        weight=joint_weight,
        scales=scale_columns,
        sums=sums_two,
    )
    up_came, last_keep, last_send, down_own, grad_joint = sync(
        up_came, last_keep, last_send, down_own, grad_joint
    )

    up_sum, up_send = fold_two(place, up_kept, up_came)
    up_sum, up_send, last_send, grad_joint = sync(up_sum, up_send, last_send, grad_joint)
    last_came = swap(last_send[0], "fx"), swap(last_send[1], "hi")
    up_came = [along(value, "fz", depth, k) for k, value in zip(rest, up_send)]

    def enter(place_ref, given, held, made, scratch, sems):
        part_ref, weight = given
        (out_ref,) = made
        grads = jnp.zeros(out_ref.shape, f32)
        for j in range(3):
            grads = grads + mm_cols(part_ref[j], weight[:, j * head_columns : (j + 1) * head_columns])
        out_ref[...] = grads.astype(bf16)

    (entered,) = weight_call(
        "enter",
        enter,
        tiles,
        place,
        [
            (grad_joint, pl.BlockSpec((3, tile, head_columns), lambda i: (0, i, 0))),
            (joint_weight, whole_block(*joint_weight.shape)),
        ],
        [],
        [(shape_of(rows, model), row_block(tile, model))],
        [],
        1,
        14,
    )
    output = ordered(pick(output, h, 0), output_came, h, 0)[:, None]
    last_came, entered, up_sum, up_came, down_own, output = sync(
        last_came, entered, up_sum, up_came, down_own, output
    )

    last_kept, last_send = fold_one(place, last_keep, last_came)
    up_own = add_up(up_sum, up_came)
    last_kept, last_send, entered, up_own, down_own = sync(last_kept, last_send, entered, up_own, down_own)
    last_came = swap(last_send[0], "hi"), swap(last_send[1], "fx")
    entered_other = other_own(entered)
    grad_normed = own_chunks(entered).astype(f32) + entered_other.astype(f32)
    unit_own, inverse_own = unit_of(own_chunks(inputs).astype(f32))
    grad_tokens = own_chunks(grad_middle) + unit_back(grad_normed * scales[0], unit_own, inverse_own)
    grad_sent = pick(grad_tokens, 1 - h, 0).astype(bf16)
    last_came, grad_tokens, grad_sent, up_own, down_own = sync(last_came, grad_tokens, grad_sent, up_own, down_own)

    last_sum, last_send = fold_two(place, last_kept, last_came)
    last_came = [along(value, "fz", depth, k) for k, value in zip(rest, last_send)]
    grad_came = swap(grad_sent, "hi")
    up_own = both_halves(up_own)
    down_all = whole_group(down_own, 0).reshape(-1, model).astype(f32)
    up_all = None
    if fused_out:
        up_all = finish_up(place, shards, up_own, swap(up_own, "lo"))
    last_came, grad_came, grad_tokens, up_own, up_all, down_all = sync(
        last_came, grad_came, grad_tokens, up_own, up_all, down_all
    )

    last_own = both_halves(add_up(last_sum, last_came))
    grad_tokens = ordered(pick(grad_tokens, h, 0), grad_came.astype(f32), h, 0)[:, None]
    if fused_out:
        qkv_all, out_all, sums = finish_qkv(place, 3 * head_columns, [last_own], [swap(last_own, "lo")])
    else:
        up_all = whole_group(up_own.reshape(own_rows, shards, -1), 2).reshape(own_rows, -1).astype(f32)
        columns = 3 * head_columns
        qkv_own = last_own[:, :columns]
        if split_out:
            qkv_all = whole_group(qkv_own.reshape(own_rows, 3, shards, -1), 3)
        else:
            qkv_all = whole_group(qkv_own.reshape(own_rows, 3, -1), 2)
        qkv_all = qkv_all.reshape(own_rows, -1).astype(f32)
        sums = jnp.sum(whole_group(last_own[:, columns : columns + 4].astype(f32), 0), axis=0).T
        grad_out = outer_whole(attended, grad_branch)
        if not split_out:
            empty = jnp.zeros((model, model), bf16)
            grad_out = lax.dynamic_update_slice_in_dim(empty, grad_out, lo * head_columns, 0)
        out_own = lax.psum(lax.psum_scatter(grad_out, shard_axes, scatter_dimension=0, tiled=True), "hi")
        out_all = whole_group(out_own, 0).reshape(own_rows, model) if split_out else lax.psum(out_own, "lo")
        out_all = out_all.astype(f32)

    return (
        output,
        grad_tokens,
        sums[0],
        sums[1],
        qkv_all,
        out_all,
        sums[2],
        sums[3],
        up_all,
        down_all,
    )


def solution(mesh):
    seq, fsdp = mesh.shape["seq"], mesh.shape["fsdp"]
    group, depth = seq // 2, fsdp // 2
    fine = Mesh(mesh.devices.reshape(2, group, depth, 2), ("hi", "lo", "fz", "fx"))
    s, f = ("hi", "lo"), ("fz", "fx")
    return jax.shard_map(
        functools.partial(body, group, depth),
        mesh=fine,
        in_specs=(
            P(None, f, s, None),
            P(None, f, None),
            P(f),
            P(f),
            P(f, None),
            P(f, None),
            P(f),
            P(f),
            P(f, None),
            P(f, None),
            P(None, f, s, None),
        ),
        out_specs=(
            P(None, f, s, None),
            P(None, f, s, None),
            P(f),
            P(f),
            P(f, None),
            P(f, None),
            P(f),
            P(f),
            P(f, None),
            P(f, None),
        ),
        check_vma=False,
    )
```

```python
import functools
import math

import jax
import jax.numpy as jnp
from jax import lax
from jax.experimental import pallas as pl
from jax.experimental.pallas import tpu as pltpu
from jax.sharding import Mesh
from jax.sharding import PartitionSpec as P

HEAD_DIM = 64
DOC_MOST = 512
TILE = 256
LANES = 128
VMEM = 26 * 1024 * 1024
epsilon = 1e-05
SWAP = [(0, 1), (1, 0)]
f32 = jnp.float32
bf16 = jnp.bfloat16


def dot(left, right, dims):
    return lax.dot_general(left, right, (dims, ((), ())), preferred_element_type=f32)


def mm(left, right):
    return dot(left, right, ((1,), (0,)))


def mm_rows(left, right):
    return dot(left, right, ((0,), (0,)))


def mm_cols(left, right):
    return dot(left, right, ((1,), (1,)))


def cost(micros):
    return pl.CostEstimate(flops=int(micros * 1.1e9), bytes_accessed=1000, transcendentals=0)


def far(array):
    return pltpu.with_memory_space_constraint(array, pltpu.HBM)


def sync(*values):
    return lax.optimization_barrier(values)


def pick(array, index, axis):
    return lax.dynamic_index_in_dim(array, index, axis, keepdims=False)


def swap(value, axis):
    return lax.ppermute(value, axis, SWAP)


def ordered(own, other, index, axis):
    first = jnp.where(index == 0, own, other)
    second = jnp.where(index == 0, other, own)
    return jnp.stack([first, second], axis)


def tile_spans(rows):
    tile = min(TILE, rows)
    spans = []
    for start in range(0, rows, tile):
        low = max(0, (start - DOC_MOST + 1) // tile * tile)
        spans.append((start, low, start + tile))
    return tile, spans


def fill_bias(bias, seg_col, seg_row, spans, tile):
    for i, (start, low, high) in enumerate(spans):
        width = high - low
        query_pos = start + lax.broadcasted_iota(jnp.int32, (tile, width), 0)
        key_pos = low + lax.broadcasted_iota(jnp.int32, (tile, width), 1)
        same = seg_col[start : start + tile, :] == seg_row[:, low:high]
        allowed = (key_pos <= query_pos) & same
        bias[i, :, :width] = jnp.where(allowed, 0.0, -1e30).astype(f32)


def pipelined(count, first, second, third):
    current, waiting = first(0), None
    for block in range(count):
        following = first(block + 1) if block + 1 < count else None
        middle = second(block, current)
        if waiting is not None:
            third(*waiting)
        waiting = (block, current, middle)
        current = following
    third(*waiting)


def own_half(left, head, rows):
    return jnp.where(left if head == 0 else ~left, rows, jnp.zeros_like(rows))


def attend_kernel(spans, tile, q_ref, k_ref, v_ref, seg_col, seg_row, out_ref, lse_ref, bias):
    @pl.when(pl.program_id(0) == 0)
    def _():
        fill_bias(bias, seg_col, seg_row, spans, tile)

    left = lax.broadcasted_iota(jnp.int32, (tile, LANES), 1) < HEAD_DIM
    done = {}

    def scores(block):
        (start, low, high), head = spans[block // 2], block % 2
        return mm_cols(own_half(left, head, q_ref[start : start + tile, :]), k_ref[low:high, :])

    def softmax(block, values):
        _, low, high = spans[block // 2]
        values = values + bias[block // 2, :, : high - low]
        top = jnp.max(values, axis=-1, keepdims=True)
        powers = jnp.exp(values - top)
        total = jnp.sum(powers, axis=-1, keepdims=True)
        return powers.astype(bf16), total, top + jnp.log(total)

    def mix(block, _, held):
        (start, low, high), head = spans[block // 2], block % 2
        powers, total, logs = held
        done[head] = mm(powers, v_ref[low:high, :]) * (1.0 / total), logs
        if head == 1:
            rows = slice(start, start + tile)
            out_ref[rows, :] = jnp.where(left, done[0][0], done[1][0]).astype(bf16)
            lse_ref[rows, :] = jnp.where(left, done[0][1], done[1][1])

    pipelined(2 * len(spans), scores, softmax, mix)


def attend(joint, seg_col, seg_row, begin, count):
    rows, width = joint.shape[0], joint.shape[1] // 3
    pairs = width // LANES
    tile, spans = tile_spans(rows)
    widest = max(high - low for _, low, high in spans)

    def part(which):
        return pl.BlockSpec((rows, LANES), lambda p: (0, which * pairs + begin + p))

    out = pl.BlockSpec((rows, LANES), lambda p: (0, p))
    return pl.pallas_call(
        functools.partial(attend_kernel, spans, tile),
        grid=(count,),
        in_specs=[
            part(0),
            part(1),
            part(2),
            pl.BlockSpec((rows, 1), lambda p: (0, 0)),
            pl.BlockSpec((1, rows), lambda p: (0, 0)),
        ],
        out_specs=[out, out],
        out_shape=[
            jax.ShapeDtypeStruct((rows, count * LANES), bf16),
            pltpu.HBM((rows, count * LANES), f32),
        ],
        scratch_shapes=[pltpu.VMEM((len(spans), tile, widest), f32)],
        compiler_params=pltpu.CompilerParams(vmem_limit_bytes=VMEM),
        cost_estimate=cost(4 * count),
        name="attend",
    )(far(joint), far(joint), far(joint), seg_col, seg_row)


def attend_back_kernel(
    spans, tile, q_ref, k_ref, v_ref, g_ref, lse_ref, seg_col, seg_row, out_ref, bias, keys_sum, values_sum
):
    @pl.when(pl.program_id(0) == 0)
    def _():
        fill_bias(bias, seg_col, seg_row, spans, tile)

    keys_sum[...] = jnp.zeros_like(keys_sum)
    values_sum[...] = jnp.zeros_like(values_sum)
    left = lax.broadcasted_iota(jnp.int32, (tile, LANES), 1) < HEAD_DIM
    done = {}

    def products(block):
        (start, low, high), head = spans[block // 2], block % 2
        rows = slice(start, start + tile)
        queries, grads = own_half(left, head, q_ref[rows, :]), own_half(left, head, g_ref[rows, :])
        return queries, grads, mm_cols(queries, k_ref[low:high, :]), mm_cols(grads, v_ref[low:high, :])

    def softmax_back(block, held):
        (start, low, high), lane = spans[block // 2], block % 2 * HEAD_DIM
        _, _, scores, grad_probs = held
        logs = lse_ref[start : start + tile, lane : lane + 1]
        probs = jnp.exp(scores + bias[block // 2, :, : high - low] - logs)
        both = probs * grad_probs
        inner = jnp.sum(both, axis=-1, keepdims=True)
        return (both - probs * inner).astype(bf16), probs.astype(bf16)

    def gather_up(block, held, middle):
        (start, low, high), head = spans[block // 2], block % 2
        queries, grads, _, _ = held
        grad_scores, probs = middle
        done[head] = mm(grad_scores, k_ref[low:high, :])
        keys_sum[low:high, :] += mm_rows(grad_scores, queries)
        values_sum[low:high, :] += mm_rows(probs, grads)
        if head == 1:
            grad_queries = jnp.where(left, done[0], done[1]).astype(bf16)
            out_ref[0, start : start + tile, :] = grad_queries * jnp.asarray(1.0 / math.sqrt(HEAD_DIM), bf16)

    pipelined(2 * len(spans), products, softmax_back, gather_up)
    out_ref[1] = keys_sum[...].astype(bf16)
    out_ref[2] = values_sum[...].astype(bf16)


def attend_back(joint, grads, lse, seg_col, seg_row, begin, count):
    rows, width = joint.shape[0], joint.shape[1] // 3
    pairs = width // LANES
    tile, spans = tile_spans(rows)
    widest = max(high - low for _, low, high in spans)

    def part(which):
        return pl.BlockSpec((rows, LANES), lambda p: (0, which * pairs + begin + p))

    return pl.pallas_call(
        functools.partial(attend_back_kernel, spans, tile),
        grid=(count,),
        in_specs=[
            part(0),
            part(1),
            part(2),
            part(0),
            pl.BlockSpec((rows, LANES), lambda p: (0, p)),
            pl.BlockSpec((rows, 1), lambda p: (0, 0)),
            pl.BlockSpec((1, rows), lambda p: (0, 0)),
        ],
        out_specs=pl.BlockSpec((3, rows, LANES), lambda p: (0, 0, p)),
        out_shape=jax.ShapeDtypeStruct((3, rows, count * LANES), bf16),
        scratch_shapes=[
            pltpu.VMEM((len(spans), tile, widest), f32),
            pltpu.VMEM((rows, LANES), f32),
            pltpu.VMEM((rows, LANES), f32),
        ],
        compiler_params=pltpu.CompilerParams(vmem_limit_bytes=VMEM),
        cost_estimate=cost(6 * count),
        name="attend_back",
    )(far(joint), far(joint), far(joint), grads, far(lse), seg_col, seg_row)


def shape_of(*shape, dtype=bf16):
    return jax.ShapeDtypeStruct(shape, dtype)


def far_shape(*shape, dtype=bf16):
    return pltpu.HBM(shape, dtype)


def along(value, axis, depth, step):
    return lax.ppermute(value, axis, [(i, (i + step) % depth) for i in range(depth)])


def load(depth, place, pieces, sems, targets, base=0, sem=0):
    z, x, h = place[0], place[1], place[2]
    copies = []

    def put(source, shard, half, at, shift=0):
        for first, columns, where in targets:
            taken = source
            if columns != source.shape[1]:
                taken = source.at[:, shift + first : shift + first + columns]
            copies.append(pltpu.make_async_copy(taken, where(shard, half, at, source.shape[0]), sems.at[sem + len(copies)]))
            copies[-1].start()

    own, side_own, far, side, near, last_side, last_near = pieces
    quarter = last_side.shape[1]
    for at_x, piece in ((x, own), (1 - x, side_own)):
        for half in range(2):
            put(piece.at[half], z * 2 + at_x, half, 0, base)
    for at_x, at_h, at, piece in (
        (x, h, 0, far),
        (1 - x, h, 0, side),
        (x, 1 - h, 0, near),
        (1 - x, 1 - h, 0, last_side),
        (1 - x, 1 - h, quarter, last_near),
    ):
        for k in range(1, depth):
            put(piece.at[k - 1], lax.rem(z - k + depth, depth) * 2 + at_x, at_h, at)
    return copies


def below(weight, half_rows):
    def where(shard, half, at, count):
        first = pl.multiple_of((shard * 2 + half) * half_rows + at, math.gcd(half_rows, at))
        return weight.at[pl.ds(first, count), :]

    return where


def halve(side, near):
    count, rows, columns = side.shape
    half = rows // 2

    def kernel(side_ref, near_ref, one_ref, two_ref):
        one_ref[...] = side_ref[:, :half, :]
        two_ref[...] = near_ref[:, half:, :]

    return pl.pallas_call(
        kernel,
        in_specs=[pl.BlockSpec(memory_space=pltpu.VMEM)] * 2,
        out_specs=[pl.BlockSpec(memory_space=pltpu.VMEM)] * 2,
        out_shape=[shape_of(count, half, columns)] * 2,
        compiler_params=pltpu.CompilerParams(vmem_limit_bytes=VMEM),
        cost_estimate=cost(1),
        name="halve",
    )(far(side), far(near))


def prepare(place, shards, w_qkv, w_out, w_up, vectors):
    rows, model = w_out.shape
    half, blocks = rows // 2, w_qkv.shape[1] // LANES
    qkv_columns, wide = w_qkv.shape[1] // 2, w_up.shape[1] // 2
    scale_at = qkv_columns
    out_at = scale_at + LANES
    up_at = out_at + model // 2
    unit = wide // shards

    def kernel(place_ref, qkv_ref, out_ref, up_ref, vectors_ref, own_ref, first_ref, up_half_ref):
        lo, h = place_ref[3], place_ref[2]
        left = lax.broadcasted_iota(jnp.int32, (rows, LANES), 1) < HEAD_DIM

        def put(at, value):
            own_ref[0, :, at : at + value.shape[1]] = value[:half]
            own_ref[1, :, at : at + value.shape[1]] = value[half:]

        for block in range(0, blocks, 2):
            one = qkv_ref[:, block * LANES : (block + 1) * LANES].astype(f32)
            two = qkv_ref[:, (block + 1) * LANES : (block + 2) * LANES].astype(f32)
            even = jnp.where(left, one, pltpu.roll(two, HEAD_DIM, 1))
            odd = jnp.where(left, pltpu.roll(one, HEAD_DIM, 1), two)
            put(block // 2 * LANES, jnp.where(lo == 0, even, odd).astype(bf16))
        columns = jnp.concatenate([vectors_ref[...].astype(f32), jnp.zeros((LANES - 4, rows), f32)], axis=0)
        put(scale_at, columns.T.astype(bf16))
        outs = jnp.where(lo == 0, out_ref[:half, :], out_ref[half:, :])
        put(out_at, jnp.concatenate([outs[:, : model // 2], outs[:, model // 2 :]], axis=0))
        for shard in range(shards):
            at = shard * 2 * unit
            put(up_at + shard * unit, jnp.where(lo == 0, up_ref[:, at : at + unit], up_ref[:, at + unit : at + 2 * unit]))
        first_ref[...] = own_ref[h, :, :up_at]
        up_half_ref[...] = own_ref[h, :, up_at:]

    return pl.pallas_call(
        kernel,
        in_specs=[pl.BlockSpec(memory_space=pltpu.SMEM)] + [pl.BlockSpec(memory_space=pltpu.VMEM)] * 4,
        out_specs=[pl.BlockSpec(memory_space=pltpu.VMEM)] * 3,
        out_shape=[shape_of(2, half, up_at + wide), shape_of(half, up_at), shape_of(half, wide)],
        compiler_params=pltpu.CompilerParams(vmem_limit_bytes=VMEM),
        cost_estimate=cost(2),
        name="prepare",
    )(place, far(w_qkv), far(w_out), far(w_up), vectors)


def finish_up(place, shards, own, other):
    rows, columns = own.shape
    unit = columns // shards

    def kernel(place_ref, own_ref, other_ref, out_ref):
        lo = place_ref[3]
        for shard in range(shards):
            at, mine, theirs = shard * 2 * unit, own_ref, other_ref
            one = mine[:, shard * unit : (shard + 1) * unit].astype(f32)
            two = theirs[:, shard * unit : (shard + 1) * unit].astype(f32)
            out_ref[:, at : at + unit] = jnp.where(lo == 0, one, two)
            out_ref[:, at + unit : at + 2 * unit] = jnp.where(lo == 0, two, one)

    return pl.pallas_call(
        kernel,
        in_specs=[pl.BlockSpec(memory_space=pltpu.SMEM)] + [pl.BlockSpec(memory_space=pltpu.VMEM)] * 2,
        out_specs=pl.BlockSpec(memory_space=pltpu.VMEM),
        out_shape=shape_of(rows, 2 * columns, dtype=f32),
        cost_estimate=cost(2),
        name="finish_up",
    )(place, own, other)


def finish_qkv(place, columns, owns, others):
    rows = owns[0].shape[0]
    half, pieces = rows // 2, len(owns)
    third = columns // 3
    model = 2 * (owns[0].shape[1] - columns - LANES)

    def kernel(place_ref, *refs):
        lo = place_ref[3]
        owns_refs, others_refs = refs[:pieces], refs[pieces : 2 * pieces]
        qkv_ref, out_ref, sums_ref = refs[2 * pieces :]
        left = lax.broadcasted_iota(jnp.int32, (rows, LANES), 1) < HEAD_DIM
        at = 0
        for j in range(3):
            for own_ref, other_ref in zip(owns_refs, others_refs):
                for first in range(j * third, (j + 1) * third, LANES):
                    mine = own_ref[:, first : first + LANES].astype(f32)
                    theirs = other_ref[:, first : first + LANES].astype(f32)
                    one, two = jnp.where(lo == 0, mine, theirs), jnp.where(lo == 0, theirs, mine)
                    qkv_ref[:, at : at + LANES] = jnp.where(left, one, pltpu.roll(two, HEAD_DIM, 1))
                    qkv_ref[:, at + LANES : at + 2 * LANES] = jnp.where(left, pltpu.roll(one, HEAD_DIM, 1), two)
                    at += 2 * LANES
        sums = jnp.zeros((rows, LANES), f32)
        for ref in refs[: 2 * pieces]:
            sums = sums + ref[:, columns : columns + LANES].astype(f32)
        sums_ref[...] = sums.T[:8, :]
        mine, theirs = (ref[:, columns + LANES :].astype(f32) for ref in (owns_refs[0], others_refs[0]))
        for at, value in ((0, jnp.where(lo == 0, mine, theirs)), (half, jnp.where(lo == 0, theirs, mine))):
            out_ref[at : at + half, : model // 2] = value[:half]
            out_ref[at : at + half, model // 2 :] = value[half:]

    return pl.pallas_call(
        kernel,
        in_specs=[pl.BlockSpec(memory_space=pltpu.SMEM)] + [pl.BlockSpec(memory_space=pltpu.VMEM)] * (2 * pieces),
        out_specs=[pl.BlockSpec(memory_space=pltpu.VMEM)] * 3,
        out_shape=[
            shape_of(rows, 2 * pieces * columns, dtype=f32),
            shape_of(rows, model, dtype=f32),
            shape_of(8, rows, dtype=f32),
        ],
        compiler_params=pltpu.CompilerParams(vmem_limit_bytes=VMEM),
        cost_estimate=cost(2),
        name="finish_qkv",
    )(place, *owns, *others)


def plus(left, right):
    return (left.astype(f32) + right.astype(f32)).astype(bf16)


def fold_one(place, keep, came, shape=shape_of):
    depth, top, columns = keep[0].shape
    low = top // 2

    def kernel(place_ref, keep_one, keep_two, came_one, came_two, kept_ref, send_one, send_two):
        at_x, at_h = place_ref[1] == 0, place_ref[2] == 0
        one, two = plus(keep_one[0], came_one[0]), plus(keep_two[0], came_two[0])
        kept_ref[0, 0] = jnp.where(at_h, one[:low], one[low:])
        send_one[0] = jnp.where(at_h, one[low:], one[:low])
        kept_ref[1, 0] = jnp.where(at_x, two[0], two[1])
        send_two[0] = jnp.where(at_x, two[1], two[0])

    one = pl.BlockSpec((1, top, columns), lambda i: (i, 0, 0))
    two = pl.BlockSpec((1, 2, low, columns), lambda i: (i, 0, 0, 0))
    send = pl.BlockSpec((1, low, columns), lambda i: (i, 0, 0))
    kept, *sends = pl.pallas_call(
        kernel,
        grid=(depth,),
        in_specs=[pl.BlockSpec(memory_space=pltpu.SMEM), one, two, one, two],
        out_specs=[pl.BlockSpec((2, 1, low, columns), lambda i: (0, i, 0, 0)), send, send],
        out_shape=[shape(2, depth, low, columns)] + [shape(depth, low, columns)] * 2,
        compiler_params=pltpu.CompilerParams(vmem_limit_bytes=VMEM),
        cost_estimate=cost(1),
        name="fold_one",
    )(place, *keep, *came)
    return kept, sends


def fold_two(place, kept, came):
    _, depth, low, columns = kept.shape

    def kernel(place_ref, kept_ref, came_one, came_two, *refs):
        *outs, sums = refs
        for half, came_ref in enumerate((came_one, came_two)):
            for at in range(depth):
                sums[at, half] = plus(kept_ref[half, at], came_ref[at])
        for k, out in enumerate(outs):
            out[...] = sums[lax.rem(place_ref[0] + k, depth)]

    own, *sends = pl.pallas_call(
        kernel,
        in_specs=[pl.BlockSpec(memory_space=pltpu.SMEM)] + [pl.BlockSpec(memory_space=pltpu.VMEM)] * 3,
        out_specs=[pl.BlockSpec(memory_space=pltpu.VMEM)] * depth,
        out_shape=[shape_of(2, low, columns)] * depth,
        scratch_shapes=[pltpu.VMEM((depth, 2, low, columns), bf16)],
        compiler_params=pltpu.CompilerParams(vmem_limit_bytes=VMEM),
        cost_estimate=cost(1),
        name="fold_two",
    )(place, kept, *came)
    return own, sends


def add_up(own, came):
    total = own.astype(f32)
    for piece in came:
        total = total + piece.astype(f32)
    return total.astype(bf16)


def row_block(tile, width):
    return pl.BlockSpec((tile, width), lambda i: (i, 0))


def whole_block(*shape):
    return pl.BlockSpec(shape, lambda i: (0,) * len(shape))


def weight_call(name, step, tiles, place, inputs, sets, outs, scratch, copies, micros):
    pieces = [piece for held in sets for piece in held]

    def kernel(place_ref, *refs):
        refs = list(refs)

        def take(count):
            taken = refs[:count]
            del refs[:count]
            return taken

        given = take(len(inputs))
        held = [take(len(one)) for one in sets]
        made = take(len(outs))
        step(place_ref, given, held, made, refs[:-1], refs[-1])

    return pl.pallas_call(
        kernel,
        grid=(tiles,),
        in_specs=[pl.BlockSpec(memory_space=pltpu.SMEM)]
        + [spec for _, spec in inputs]
        + [pl.BlockSpec(memory_space=pltpu.HBM)] * len(pieces),
        out_specs=[spec for _, spec in outs],
        out_shape=[shape for shape, _ in outs],
        scratch_shapes=list(scratch) + [pltpu.SemaphoreType.DMA((copies,))],
        compiler_params=pltpu.CompilerParams(vmem_limit_bytes=VMEM),
        cost_estimate=cost(micros),
        name=name,
    )(place, *[v for v, _ in inputs], *[far(piece) for piece in pieces])


def unit_of(values):
    centred = values - jnp.mean(values, axis=-1, keepdims=True)
    variance = jnp.mean(centred * centred, axis=-1, keepdims=True)
    inverse = lax.rsqrt(variance + epsilon)
    return centred * inverse, inverse


def unit_back(grad_unit, unit_rows, inverse):
    mean_grad = jnp.mean(grad_unit, axis=-1, keepdims=True)
    mean_cross = jnp.mean(grad_unit * unit_rows, axis=-1, keepdims=True)
    return inverse * (grad_unit - mean_grad - unit_rows * mean_cross)


def bell_and_slope(values):
    phi = 0.5 + 0.5 * lax.erf(values * math.sqrt(0.5))
    density = jnp.exp(values * values * -0.5) * (1.0 / math.sqrt(2.0 * math.pi))
    return values * phi, phi + values * density


def outer_whole(left, right):
    rows, across = left.shape
    block = min(256, across)

    def kernel(left_ref, right_ref, out_ref):
        out_ref[...] = mm_rows(left_ref[...], right_ref[...]).astype(bf16)

    return pl.pallas_call(
        kernel,
        grid=(across // block,),
        in_specs=[pl.BlockSpec((rows, block), lambda i: (0, i)), whole_block(*right.shape)],
        out_specs=row_block(block, right.shape[1]),
        out_shape=shape_of(across, right.shape[1]),
        compiler_params=pltpu.CompilerParams(vmem_limit_bytes=VMEM),
        cost_estimate=cost(7),
        name="outer_whole",
    )(left, right)


def outer(place, depth, left, right, out_pair=None, weight=None, scales=None, piece=0, sums=None):
    rows, own_rows = left.shape[0], left.shape[1] // (2 * depth)
    top, low = own_rows // 2, own_rows // 4
    parts = right.shape[0] if right.ndim == 3 else 1
    third = right.shape[-1]
    columns = parts * third
    given = [left, right]
    specs = [pl.BlockSpec((rows, 2 * own_rows), lambda i: (0, i)), whole_block(*right.shape)]
    total = columns
    if weight is not None:
        given += [weight, scales, sums]
        specs += [pl.BlockSpec((2 * own_rows, part.shape[1]), lambda i: (i, 0)) for part in (weight, scales)]
        specs.append(pl.BlockSpec((8, 2 * own_rows), lambda i: (0, i)))
        total += LANES
        width = weight.shape[1] // 3
    if out_pair is not None:
        out_block = out_pair[0].shape[1] // depth
        given += out_pair
        specs += [pl.BlockSpec((rows, out_block), lambda i: (0, i)), whole_block(*out_pair[1].shape)]
        half = out_pair[1].shape[1] // 2
        total += half

    def kernel(place_ref, *refs):
        ins, outs = list(refs[: len(given)]), refs[len(given) :]
        at_x, at_h = place_ref[1] == 0, place_ref[2] == 0
        keep_first, send_first, keep_second, send_second = outs

        def put(first, value):
            where = slice(first, first + value.shape[2])
            heads = value[:, :top].astype(bf16)
            keep_first[0, :, where] = jnp.where(at_x, heads[0], heads[1])
            send_first[0, :, where] = jnp.where(at_x, heads[1], heads[0])
            lower, upper = value[:, top : top + low].astype(bf16), value[:, top + low :].astype(bf16)
            keep_second[0, :, :, where] = jnp.where(at_h, lower, upper)
            send_second[0, :, :, where] = jnp.where(at_h, upper, lower)

        left_ref, right_ref = ins.pop(0), ins.pop(0)
        rights = [right_ref.at[j] for j in range(parts)] if parts > 1 else [right_ref]
        products = [mm_rows(left_ref[...], ref[...]) for ref in rights]
        for j, product in enumerate(products):
            put(j * third, product.reshape(2, own_rows, third))
        first = columns
        if weight is not None:
            weight_ref, scales_ref, sums_ref = ins.pop(0), ins.pop(0), ins.pop(0)
            bias_sum = cross = 0.0
            for j, product in enumerate(products):
                at = j * width + piece * third
                part = weight_ref[:, at : at + third].astype(f32)
                column_sums = jnp.sum(rights[j][...].astype(f32), axis=0, keepdims=True)
                bias_sum = bias_sum + jnp.sum(part * column_sums, axis=1, keepdims=True)
                cross = cross + jnp.sum(part * product, axis=1, keepdims=True)
            gain, bias = scales_ref[:, 0:1].astype(f32), scales_ref[:, 1:2].astype(f32)
            gain_sum = (cross - bias * bias_sum) / gain
            kept = jnp.concatenate(
                [jnp.zeros((2, 2 * own_rows), f32), sums_ref[0:2, :], jnp.zeros((LANES - 4, 2 * own_rows), f32)], axis=0
            ).T
            lane = lax.broadcasted_iota(jnp.int32, kept.shape, 1)
            kept = jnp.where(lane == 0, gain_sum, jnp.where(lane == 1, bias_sum, kept))
            put(first, kept.reshape(2, own_rows, LANES))
            first += LANES
        if out_pair is not None:
            product = mm_rows(ins.pop(0)[...], ins.pop(0)[...]).reshape(2, top, 2 * half)
            put(first, jnp.concatenate([product[:, :, :half], product[:, :, half:]], axis=1))

    def spec(*block):
        return pl.BlockSpec((1, *block), lambda i: (i,) + (0,) * len(block))

    first_shape, second_shape = (top, total), (2, low, total)
    made = pl.pallas_call(
        kernel,
        grid=(depth,),
        in_specs=[pl.BlockSpec(memory_space=pltpu.SMEM)] + specs,
        out_specs=[spec(*first_shape)] * 2 + [spec(*second_shape)] * 2,
        out_shape=[shape_of(depth, *first_shape)] * 2 + [shape_of(depth, *second_shape)] * 2,
        compiler_params=pltpu.CompilerParams(vmem_limit_bytes=VMEM),
        cost_estimate=cost(6),
        name="outer",
    )(place, *given)
    return (made[0], made[2]), (made[1], made[3])


def body(
    group,
    depth,
    tokens,
    segment_ids,
    norm1_gain,
    norm1_bias,
    w_qkv,
    w_out,
    norm2_gain,
    norm2_bias,
    w_up,
    w_down,
    cotangent,
):
    h, lo = lax.axis_index("hi"), lax.axis_index("lo")
    z, x = lax.axis_index("fz"), lax.axis_index("fx")
    micro, _, chunk, model = tokens.shape
    shards = 2 * depth
    rows = micro * group * chunk
    own_rows = w_out.shape[0]
    inner = w_up.shape[1] // group
    split_out = (own_rows // HEAD_DIM) % group == 0
    head_columns = model // group
    half_rows = own_rows // 2
    tile = min(TILE, rows)
    tiles = rows // tile
    scale_at = 3 * head_columns
    copies = 4 * shards
    wide = min(512, inner)
    shard_axes = ("fz", "fx")

    rest = range(1, depth)

    def whole_group(value, axis):
        if group == 2:
            return ordered(value, swap(value, "lo"), lo, axis)
        return lax.all_gather(value, "lo", axis=axis)

    def other_part(partial):
        if group == 2:
            return swap(partial, "lo")
        return (lax.psum(partial, "lo").astype(f32) - partial.astype(f32)).astype(bf16)

    def own_chunks(full):
        return pick(full.reshape(micro, group, chunk, -1), lo, 1)

    def other_own(partial):
        parts = partial.reshape(micro, group, chunk, model)
        if group == 2:
            return swap(pick(parts, 1 - lo, 1), "lo")
        return plus(lax.psum_scatter(parts, "lo", scatter_dimension=1), -pick(parts, lo, 1))

    def hop(values, parity):
        return [along(value, "fz", depth, k) for k, value in zip(rest, values) if k % 2 == parity]

    fused_out = split_out and group == 2
    out_rows, half_model = own_rows // group, model // 2
    place = jnp.stack([z, x, h, lo]).astype(jnp.int32)
    came = swap(jnp.stack([pick(tokens[:, 0], 1 - h, 0), pick(cotangent[:, 0], 1 - h, 0)]), "hi")
    vectors = jnp.stack([norm1_gain, norm1_bias, norm2_gain, norm2_bias])
    if fused_out:
        both_own, first_half, up_half = prepare(place, shards, w_qkv, w_out, w_up, vectors)
    else:
        if split_out:
            qkv_part = pick(w_qkv.reshape(own_rows, 3, shards, group, -1), lo, 3).reshape(own_rows, -1)
            out_part = pick(w_out.reshape(group, out_rows, model), lo, 0)
        else:
            qkv_part = pick(w_qkv.reshape(own_rows, 3, group, -1), lo, 2).reshape(own_rows, -1)
            out_part = w_out
        up_part = pick(w_up.reshape(own_rows, shards, group, -1), lo, 2).reshape(own_rows, -1)
        parts = [qkv_part, jnp.pad(vectors.T, ((0, 0), (0, LANES - 4)))]
        both_own = jnp.concatenate(parts + [up_part], axis=1).reshape(2, half_rows, -1)
        half = pick(both_own, h, 0)
        first_half, up_half = half[:, : scale_at + LANES], half[:, scale_at + LANES :]
        out_weight = lax.all_gather(out_part, shard_axes, axis=0, tiled=True)
    up_at = first_half.shape[1]
    down_rows = inner // shards
    fine_down = down_rows % 64 == 0
    down_part = pick(w_down.reshape(group, 2, down_rows // 2, model), lo, 0)
    first_far = [along(first_half, "fz", depth, k) for k in rest]
    side_own = swap(both_own, "fx")
    first_far, side_own, came, up_half = sync(first_far, side_own, came, up_half)

    def last_quarters(side_part, near_part):
        return swap(side_part, "hi"), swap(near_part, "fx")

    first_far = jnp.stack(first_far)
    first_side, first_near = swap(first_far, "fx"), swap(first_far, "hi")
    up_far = [along(up_half, "fz", depth, k) for k in rest]
    first_side, first_near, up_far, came, down_part = sync(first_side, first_near, up_far, came, down_part)

    cuts, came, tokens, up_far = sync(halve(first_side, first_near), came, tokens, up_far)
    first_last = last_quarters(*cuts)
    down_half = pick(down_part, h, 0)
    if not fine_down:
        downward = lax.all_gather(down_part.reshape(down_rows, model), shard_axes, axis=0, tiled=True)
    inputs = whole_group(ordered(pick(tokens[:, 0], h, 0), came[0], h, 0), 1).reshape(rows, model)
    up_far = jnp.stack(up_far)
    first_last, inputs, up_far, came, down_half, down_part = sync(
        first_last, inputs, up_far, came, down_half, down_part
    )
    first_set = [both_own, side_own, first_far, first_side, first_near, *first_last]

    segments = pick(segment_ids[:, 0], h, 0)
    seg_col, seg_row = segments[:, None], segments[None, :]

    def project(place_ref, given, held, made, scratch, sems):
        (rows_ref,), (normed_ref, joint_ref, scales_ref, weight, columns, *outs) = given, made

        @pl.when(pl.program_id(0) == 0)
        def _():
            targets = [
                (0, 3 * head_columns, below(weight, half_rows)),
                (scale_at, LANES, below(columns, half_rows)),
            ]
            if fused_out:
                targets.append((scale_at + LANES, half_model, below(scratch[0], half_rows)))
            for copy in load(depth, place_ref, held[0], sems, targets):
                copy.wait()
            scales_ref[...] = columns[...].astype(f32).T[:8, :]
            for shard in range(shards if fused_out else 0):
                for part in range(2):
                    at = shard * own_rows + part * out_rows
                    outs[0][
                        shard * out_rows : (shard + 1) * out_rows, part * half_model : (part + 1) * half_model
                    ] = scratch[0][at : at + out_rows, :]

        unit_rows, _ = unit_of(rows_ref[...].astype(f32))
        normed = (unit_rows * scales_ref[0:1, :] + scales_ref[1:2, :]).astype(bf16)
        normed_ref[...] = normed
        for at in range(0, 3 * head_columns, head_columns):
            part = mm(normed, weight[:, at : at + head_columns])
            if at == 0:
                part = part * (1.0 / math.sqrt(HEAD_DIM))
            joint_ref[:, at : at + head_columns] = part.astype(bf16)

    wholes = [(8, model, f32), (model, 3 * head_columns, bf16), (model, LANES, bf16)]
    if fused_out:
        wholes.append((head_columns, model, bf16))
    normed, joint, scales, joint_weight, scale_columns, *outs = weight_call(
        "project",
        project,
        tiles,
        place,
        [(inputs, row_block(tile, model))],
        [first_set],
        [
            (far_shape(rows, model), row_block(tile, model)),
            (far_shape(rows, 3 * head_columns), row_block(tile, 3 * head_columns)),
        ]
        + [(far_shape(*shape, dtype=dtype), whole_block(*shape)) for *shape, dtype in wholes],
        [pltpu.VMEM((model, half_model), bf16)] if fused_out else [],
        3 * copies,
        8,
    )
    if fused_out:
        (out_weight,) = outs
    pairs = head_columns // LANES
    pieces = 2 if pairs % 2 == 0 else 1
    count = pairs // pieces
    part_columns = count * LANES
    mixed = [attend(joint, seg_col, seg_row, 0, count)]
    up_side, up_near = swap(up_far, "fx"), swap(up_far, "hi")
    down_odd = down_even = down_side_own = None
    if fine_down:
        down_odd = [along(down_half, "fz", depth, k) for k in rest if k % 2]
        down_side_own = swap(down_part, "fx")
    mixed, joint, up_side, up_near, scales, out_weight, came, down_odd, down_side_own, down_half = sync(
        mixed, joint, up_side, up_near, scales, out_weight, came, down_odd, down_side_own, down_half
    )

    cuts, joint, came, down_half = sync(halve(up_side, up_near), joint, came, down_half)
    up_last = last_quarters(*cuts)
    for piece in range(1, pieces):
        mixed.append(attend(joint, seg_col, seg_row, piece * count, count))
    grad_result = whole_group(ordered(pick(cotangent[:, 0], h, 0), came[1], h, 0), 1).reshape(rows, model)
    if fine_down:
        down_even = [along(down_half, "fz", depth, k) for k in rest if k % 2 == 0]
    mixed, up_last, out_weight, grad_result, down_even = sync(mixed, up_last, out_weight, grad_result, down_even)
    up_set = [both_own, side_own, up_far, up_side, up_near, *up_last]
    lse = mixed[0][1] if pieces == 1 else jnp.concatenate([part for _, part in mixed], axis=1)

    def leave(place_ref, given, held, made, scratch, sems):
        *parts_refs, weight = given
        out_ref, attended_ref = made
        weight = own_out(weight, place_ref)
        total = jnp.zeros(out_ref.shape, f32)
        for piece, part_ref in enumerate(parts_refs):
            at = slice(piece * part_columns, (piece + 1) * part_columns)
            attended_ref[:, at] = part_ref[...]
            total = total + mm(part_ref[...], weight[at, :])
        out_ref[...] = total.astype(bf16)

    def own_out(weight, place_ref):
        if split_out:
            return weight[...]
        return weight[pl.ds(pl.multiple_of(place_ref[3] * head_columns, head_columns), head_columns), :]

    branch, attended = weight_call(
        "leave",
        leave,
        tiles,
        place,
        [(value, row_block(tile, part_columns)) for value, _ in mixed]
        + [(out_weight, whole_block(*out_weight.shape))],
        [],
        [
            (shape_of(rows, model), row_block(tile, model)),
            (far_shape(rows, head_columns), row_block(tile, head_columns)),
        ],
        [],
        1,
        3,
    )
    branch_other = other_part(branch)

    if fine_down:
        down_far = jnp.stack([down_odd[k // 2] if k % 2 else down_even[k // 2 - 1] for k in rest])
        down_side, down_near = swap(down_far, "fx"), swap(down_far, "hi")

    def widen(place_ref, given, held, made, scratch, sems):
        rows_ref, own_ref, other_ref, scales_ref = given
        middle_ref, normed_ref, hidden_ref, slope_ref = made
        (weight,) = scratch

        @pl.when(pl.program_id(0) == 0)
        def _():
            targets = [(0, inner, below(weight, half_rows))]
            for copy in load(depth, place_ref, held[0], sems, targets, up_at):
                copy.wait()

        added = own_ref[...].astype(f32) + other_ref[...].astype(f32)
        middle = rows_ref[...].astype(f32) + added
        middle_ref[...] = middle.astype(bf16)
        unit_rows, _ = unit_of(middle)
        normed = (unit_rows * scales_ref[2:3, :] + scales_ref[3:4, :]).astype(bf16)
        normed_ref[...] = normed
        for at in range(0, inner, wide):
            hidden, slope = bell_and_slope(mm(normed, weight[:, at : at + wide]))
            hidden_ref[:, at : at + wide] = hidden.astype(bf16)
            slope_ref[:, at : at + wide] = slope.astype(bf16)

    middle, normed_two, hidden, slope = weight_call(
        "widen",
        widen,
        tiles,
        place,
        [
            (inputs, row_block(tile, model)),
            (branch, row_block(tile, model)),
            (branch_other, row_block(tile, model)),
            (scales, whole_block(8, model)),
        ],
        [up_set],
        [
            (far_shape(rows, model), row_block(tile, model)),
            (far_shape(rows, model), row_block(tile, model)),
            (far_shape(rows, inner), row_block(tile, inner)),
            (far_shape(rows, inner), row_block(tile, inner)),
        ],
        [pltpu.VMEM((model, inner), bf16)],
        copies,
        13,
    )

    if fine_down:
        hidden, slope, normed_two, down_side, down_near, lse = sync(
            hidden, slope, normed_two, down_side, down_near, lse
        )
        cuts, hidden = sync(halve(down_side, down_near), hidden)
        down_last = last_quarters(*cuts)
        down_keep, down_send = outer(place, depth, far(hidden), grad_result)
        hidden, slope, down_keep, down_send, normed_two, down_last = sync(
            hidden, slope, down_keep, down_send, normed_two, down_last
        )
        down_set = [down_part, down_side_own, down_far, down_side, down_near, *down_last]
        down_came = swap(down_send[0], "fx"), swap(down_send[1], "hi")
    else:
        down_keep = down_came = outer_whole(hidden, grad_result)
        down_send = None

    by_chunk = group == 2 and tile == chunk

    def narrow(place_ref, given, held, made, scratch, sems):
        hidden_ref, grad_ref, slope_ref, *downs = given
        *out_refs, pre_ref, back_ref = made
        upward = scratch[0]
        down_ref = scratch[1] if fine_down else downs[0]

        @pl.when(pl.program_id(0) == 0)
        def _():
            started = []
            if fine_down:
                targets = [(0, model, below(down_ref, down_rows // 2))]
                started = load(depth, place_ref, held[1], sems, targets, sem=copies)
            targets = [(0, inner, below(upward, half_rows))]
            for copy in started + load(depth, place_ref, held[0], sems, targets, up_at):
                copy.wait()

        for at in range(0, inner, wide):
            grad = mm_cols(grad_ref[...], down_ref[at : at + wide, :])
            pre_ref[:, at : at + wide] = (grad * slope_ref[:, at : at + wide].astype(f32)).astype(bf16)
        back_ref[...] = mm_cols(pre_ref[...], upward[...]).astype(bf16)
        out = mm(hidden_ref[...], down_ref[...]).astype(bf16)
        if by_chunk:
            own = lax.rem(pl.program_id(0), 2) == place_ref[3]

            @pl.when(own)
            def _():
                out_refs[0][0] = out

            @pl.when(~own)
            def _():
                out_refs[1][0] = out
        else:
            out_refs[0][...] = out

    *results, grad_pre, back = weight_call(
        "narrow",
        narrow,
        tiles,
        place,
        [
            (far(hidden), row_block(tile, inner)),
            (far(grad_result), row_block(tile, model)),
            (far(slope), row_block(tile, inner)),
        ]
        + ([] if fine_down else [(far(downward), whole_block(inner, model))]),
        [up_set, down_set] if fine_down else [up_set],
        (
            [
                (shape(micro, chunk, model), pl.BlockSpec((1, chunk, model), lambda i: (i // 2, 0, 0)))
                for shape in (far_shape, shape_of)
            ]
            if by_chunk
            else [(far_shape(rows, model), row_block(tile, model))]
        )
        + [
            (far_shape(rows, inner), row_block(tile, inner)),
            (far_shape(rows, model), row_block(tile, model)),
        ],
        [pltpu.VMEM((model, inner), bf16), pltpu.VMEM((inner, model), bf16)],
        2 * copies,
        18,
    )
    down_kept = None
    if fine_down:
        down_kept, down_send = fold_one(place, down_keep, down_came, far_shape)
    results, grad_pre, back, normed_two, down_kept, down_send, down_came = sync(
        results, grad_pre, back, normed_two, down_kept, down_send, down_came
    )

    back_other = other_part(back)
    if by_chunk:
        result, result_other = results[0], swap(results[1], "lo")
    else:
        result, result_other = own_chunks(results[0]), other_own(results[0])
    if fine_down:
        down_came = swap(down_send[0], "hi"), swap(down_send[1], "fx")
    up_keep, up_send = outer(place, depth, far(normed_two), far(grad_pre))
    output = (own_chunks(middle).astype(f32) + result.astype(f32) + result_other.astype(f32)).astype(bf16)
    back, back_other, up_keep, up_send, down_came, output = sync(
        back, back_other, up_keep, up_send, down_came, output
    )
    if fine_down:
        down_sum, down_send = fold_two(place, down_kept, down_came)
        down_send, back, back_other, up_send = sync(down_send, back, back_other, up_send)
        down_came = hop(down_send, 1)

    def between(place_ref, given, held, made, scratch, sems):
        grad_ref, own_ref, other_ref, middle_ref, scales_ref, weight = given
        branch_ref, attended_ref, sums_ref = made

        @pl.when(pl.program_id(0) == 0)
        def _():
            sums_ref[...] = jnp.zeros_like(sums_ref)

        unit_rows, inverse = unit_of(middle_ref[...].astype(f32))
        own_back = own_ref[...].astype(f32)
        back_rows = own_back + other_ref[...].astype(f32)
        sums_ref[0:1, :] += jnp.sum(own_back * unit_rows, axis=0, keepdims=True)
        sums_ref[1:2, :] += jnp.sum(own_back, axis=0, keepdims=True)
        grads = grad_ref[...].astype(f32) + unit_back(back_rows * scales_ref[2:3, :], unit_rows, inverse)
        low = grads.astype(bf16)
        branch_ref[...] = low
        attended_ref[...] = mm_cols(low, own_out(weight, place_ref)).astype(bf16)

    grad_branch, grad_attended, sums_two = weight_call(
        "between",
        between,
        tiles,
        place,
        [
            (grad_result, row_block(tile, model)),
            (back, row_block(tile, model)),
            (back_other, row_block(tile, model)),
            (far(middle), row_block(tile, model)),
            (scales, whole_block(8, model)),
            (out_weight, whole_block(*out_weight.shape)),
        ],
        [],
        [
            (far_shape(rows, model), row_block(tile, model)),
            (shape_of(rows, head_columns), row_block(tile, head_columns)),
            (shape_of(8, model, dtype=f32), whole_block(8, model)),
        ],
        [],
        1,
        8,
    )
    if fine_down:
        grad_attended, down_came, down_send = sync(grad_attended, down_came, down_send)
        down_came = down_came + hop(down_send, 0)
    grad_joint = attend_back(joint, grad_attended, lse, seg_col, seg_row, 0, pairs)
    up_came = swap(up_send[0], "fx"), swap(up_send[1], "hi")
    output_came = swap(pick(output, 1 - h, 0), "hi")
    if fine_down:
        down_came = add_up(down_sum, down_came)
    grad_joint, grad_branch, up_came, output_came, down_came = sync(
        grad_joint, grad_branch, up_came, output_came, down_came
    )

    def both_halves(value):
        return ordered(value, swap(value, "hi"), h, 1).reshape(-1, value.shape[2])

    up_kept, up_send = fold_one(place, up_keep, up_came)
    up_kept, up_send, grad_joint = sync(up_kept, up_send, grad_joint)
    up_came = swap(up_send[0], "hi"), swap(up_send[1], "fx")
    if fine_down:
        down_own = both_halves(down_came)
    else:
        down_own = lax.psum(lax.psum_scatter(down_came, shard_axes, scatter_dimension=0, tiled=True), "hi")
    last_keep, last_send = outer(
        place,
        depth,
        normed,
        grad_joint,
        out_pair=[attended, grad_branch] if fused_out else None,
        weight=joint_weight,
        scales=scale_columns,
        sums=sums_two,
    )
    up_came, last_keep, last_send, down_own, grad_joint = sync(
        up_came, last_keep, last_send, down_own, grad_joint
    )

    up_sum, up_send = fold_two(place, up_kept, up_came)
    up_sum, up_send, last_send, grad_joint = sync(up_sum, up_send, last_send, grad_joint)
    last_came = swap(last_send[0], "fx"), swap(last_send[1], "hi")
    up_came = [along(value, "fz", depth, k) for k, value in zip(rest, up_send)]

    def enter(place_ref, given, held, made, scratch, sems):
        part_ref, weight = given
        (out_ref,) = made
        grads = jnp.zeros(out_ref.shape, f32)
        for j in range(3):
            grads = grads + mm_cols(part_ref[j], weight[:, j * head_columns : (j + 1) * head_columns])
        out_ref[...] = grads.astype(bf16)

    (entered,) = weight_call(
        "enter",
        enter,
        tiles,
        place,
        [
            (grad_joint, pl.BlockSpec((3, tile, head_columns), lambda i: (0, i, 0))),
            (joint_weight, whole_block(*joint_weight.shape)),
        ],
        [],
        [(shape_of(rows, model), row_block(tile, model))],
        [],
        1,
        14,
    )
    output = ordered(pick(output, h, 0), output_came, h, 0)[:, None]
    last_came, entered, up_sum, up_came, down_own, output = sync(
        last_came, entered, up_sum, up_came, down_own, output
    )

    last_kept, last_send = fold_one(place, last_keep, last_came)
    up_own = add_up(up_sum, up_came)
    last_kept, last_send, entered, up_own, down_own = sync(last_kept, last_send, entered, up_own, down_own)
    last_came = swap(last_send[0], "hi"), swap(last_send[1], "fx")
    entered_other = other_own(entered)
    grad_normed = own_chunks(entered).astype(f32) + entered_other.astype(f32)
    unit_own, inverse_own = unit_of(own_chunks(inputs).astype(f32))
    grad_tokens = own_chunks(grad_branch).astype(f32) + unit_back(grad_normed * scales[0], unit_own, inverse_own)
    grad_sent = pick(grad_tokens, 1 - h, 0).astype(bf16)
    last_came, grad_tokens, grad_sent, up_own, down_own = sync(last_came, grad_tokens, grad_sent, up_own, down_own)

    last_sum, last_send = fold_two(place, last_kept, last_came)
    last_came = [along(value, "fz", depth, k) for k, value in zip(rest, last_send)]
    grad_came = swap(grad_sent, "hi")
    up_own = both_halves(up_own)
    down_all = whole_group(down_own, 0).reshape(-1, model).astype(f32)
    up_all = None
    if fused_out:
        up_all = finish_up(place, shards, up_own, swap(up_own, "lo"))
    last_came, grad_came, grad_tokens, up_own, up_all, down_all = sync(
        last_came, grad_came, grad_tokens, up_own, up_all, down_all
    )

    last_own = both_halves(add_up(last_sum, last_came))
    grad_tokens = ordered(pick(grad_tokens, h, 0), grad_came.astype(f32), h, 0)[:, None]
    last_own, grad_tokens = sync(last_own, grad_tokens)
    if fused_out:
        qkv_all, out_all, sums = finish_qkv(place, 3 * head_columns, [last_own], [swap(last_own, "lo")])
    else:
        up_all = whole_group(up_own.reshape(own_rows, shards, -1), 2).reshape(own_rows, -1).astype(f32)
        columns = 3 * head_columns
        qkv_own = last_own[:, :columns]
        if split_out:
            qkv_all = whole_group(qkv_own.reshape(own_rows, 3, shards, -1), 3)
        else:
            qkv_all = whole_group(qkv_own.reshape(own_rows, 3, -1), 2)
        qkv_all = qkv_all.reshape(own_rows, -1).astype(f32)
        sums = jnp.sum(whole_group(last_own[:, columns : columns + 4].astype(f32), 0), axis=0).T
        grad_out = outer_whole(attended, grad_branch)
        if not split_out:
            empty = jnp.zeros((model, model), bf16)
            grad_out = lax.dynamic_update_slice_in_dim(empty, grad_out, lo * head_columns, 0)
        out_own = lax.psum(lax.psum_scatter(grad_out, shard_axes, scatter_dimension=0, tiled=True), "hi")
        out_all = whole_group(out_own, 0).reshape(own_rows, model) if split_out else lax.psum(out_own, "lo")
        out_all = out_all.astype(f32)

    return (
        output,
        grad_tokens,
        sums[0],
        sums[1],
        qkv_all,
        out_all,
        sums[2],
        sums[3],
        up_all,
        down_all,
    )


def solution(mesh):
    seq, fsdp = mesh.shape["seq"], mesh.shape["fsdp"]
    group, depth = seq // 2, fsdp // 2
    fine = Mesh(mesh.devices.reshape(2, group, depth, 2), ("hi", "lo", "fz", "fx"))
    s, f = ("hi", "lo"), ("fz", "fx")
    return jax.shard_map(
        functools.partial(body, group, depth),
        mesh=fine,
        in_specs=(
            P(None, f, s, None),
            P(None, f, None),
            P(f),
            P(f),
            P(f, None),
            P(f, None),
            P(f),
            P(f),
            P(f, None),
            P(f, None),
            P(None, f, s, None),
        ),
        out_specs=(
            P(None, f, s, None),
            P(None, f, s, None),
            P(f),
            P(f),
            P(f, None),
            P(f, None),
            P(f),
            P(f),
            P(f, None),
            P(f, None),
        ),
        check_vma=False,
    )
```

```python
import functools
import math

import jax
import jax.numpy as jnp
from jax import lax
from jax.experimental import pallas as pl
from jax.experimental.pallas import tpu as pltpu
from jax.sharding import Mesh
from jax.sharding import PartitionSpec as P

HEAD_DIM = 64
DOC_MOST = 512
TILE = 256
LANES = 128
VMEM = 26 * 1024 * 1024
epsilon = 1e-05
SWAP = [(0, 1), (1, 0)]
f32 = jnp.float32
bf16 = jnp.bfloat16


def dot(left, right, dims):
    return lax.dot_general(left, right, (dims, ((), ())), preferred_element_type=f32)


def mm(left, right):
    return dot(left, right, ((1,), (0,)))


def mm_rows(left, right):
    return dot(left, right, ((0,), (0,)))


def mm_cols(left, right):
    return dot(left, right, ((1,), (1,)))


def cost(micros):
    return pl.CostEstimate(flops=int(micros * 1.1e9), bytes_accessed=1000, transcendentals=0)


def far(array):
    return pltpu.with_memory_space_constraint(array, pltpu.HBM)


def sync(*values):
    return lax.optimization_barrier(values)


def pick(array, index, axis):
    return lax.dynamic_index_in_dim(array, index, axis, keepdims=False)


def swap(value, axis):
    return lax.ppermute(value, axis, SWAP)


def ordered(own, other, index, axis):
    first = jnp.where(index == 0, own, other)
    second = jnp.where(index == 0, other, own)
    return jnp.stack([first, second], axis)


def tile_spans(rows):
    tile = min(TILE, rows)
    spans = []
    for start in range(0, rows, tile):
        low = max(0, (start - DOC_MOST + 1) // tile * tile)
        spans.append((start, low, start + tile))
    return tile, spans


def fill_bias(bias, seg_col, seg_row, spans, tile):
    for i, (start, low, high) in enumerate(spans):
        width = high - low
        query_pos = start + lax.broadcasted_iota(jnp.int32, (tile, width), 0)
        key_pos = low + lax.broadcasted_iota(jnp.int32, (tile, width), 1)
        same = seg_col[start : start + tile, :] == seg_row[:, low:high]
        allowed = (key_pos <= query_pos) & same
        bias[i, :, :width] = jnp.where(allowed, 0.0, -1e30).astype(f32)


def pipelined(count, first, second, third):
    current, waiting = first(0), None
    for block in range(count):
        following = first(block + 1) if block + 1 < count else None
        middle = second(block, current)
        if waiting is not None:
            third(*waiting)
        waiting = (block, current, middle)
        current = following
    third(*waiting)


def own_half(left, head, rows):
    return jnp.where(left if head == 0 else ~left, rows, jnp.zeros_like(rows))


def attend_kernel(spans, tile, q_ref, k_ref, v_ref, seg_col, seg_row, out_ref, lse_ref, bias):
    @pl.when(pl.program_id(0) == 0)
    def _():
        fill_bias(bias, seg_col, seg_row, spans, tile)

    left = lax.broadcasted_iota(jnp.int32, (tile, LANES), 1) < HEAD_DIM
    done = {}

    def scores(block):
        (start, low, high), head = spans[block // 2], block % 2
        return mm_cols(own_half(left, head, q_ref[start : start + tile, :]), k_ref[low:high, :])

    def softmax(block, values):
        _, low, high = spans[block // 2]
        values = values + bias[block // 2, :, : high - low]
        top = jnp.max(values, axis=-1, keepdims=True)
        powers = jnp.exp(values - top)
        total = jnp.sum(powers, axis=-1, keepdims=True)
        return powers.astype(bf16), total, top + jnp.log(total)

    def mix(block, _, held):
        (start, low, high), head = spans[block // 2], block % 2
        powers, total, logs = held
        done[head] = mm(powers, v_ref[low:high, :]) * (1.0 / total), logs
        if head == 1:
            rows = slice(start, start + tile)
            out_ref[rows, :] = jnp.where(left, done[0][0], done[1][0]).astype(bf16)
            lse_ref[rows, :] = jnp.where(left, done[0][1], done[1][1])

    pipelined(2 * len(spans), scores, softmax, mix)


def attend(joint, seg_col, seg_row, begin, count):
    rows, width = joint.shape[0], joint.shape[1] // 3
    pairs = width // LANES
    tile, spans = tile_spans(rows)
    widest = max(high - low for _, low, high in spans)

    def part(which):
        return pl.BlockSpec((rows, LANES), lambda p: (0, which * pairs + begin + p))

    out = pl.BlockSpec((rows, LANES), lambda p: (0, p))
    return pl.pallas_call(
        functools.partial(attend_kernel, spans, tile),
        grid=(count,),
        in_specs=[
            part(0),
            part(1),
            part(2),
            pl.BlockSpec((rows, 1), lambda p: (0, 0)),
            pl.BlockSpec((1, rows), lambda p: (0, 0)),
        ],
        out_specs=[out, out],
        out_shape=[
            jax.ShapeDtypeStruct((rows, count * LANES), bf16),
            pltpu.HBM((rows, count * LANES), f32),
        ],
        scratch_shapes=[pltpu.VMEM((len(spans), tile, widest), f32)],
        compiler_params=pltpu.CompilerParams(vmem_limit_bytes=VMEM),
        cost_estimate=cost(4 * count),
        name="attend",
    )(far(joint), far(joint), far(joint), seg_col, seg_row)


def attend_back_kernel(
    spans, tile, q_ref, k_ref, v_ref, g_ref, lse_ref, seg_col, seg_row, out_ref, bias, keys_sum, values_sum
):
    @pl.when(pl.program_id(0) == 0)
    def _():
        fill_bias(bias, seg_col, seg_row, spans, tile)

    keys_sum[...] = jnp.zeros_like(keys_sum)
    values_sum[...] = jnp.zeros_like(values_sum)
    left = lax.broadcasted_iota(jnp.int32, (tile, LANES), 1) < HEAD_DIM
    done = {}

    def products(block):
        (start, low, high), head = spans[block // 2], block % 2
        rows = slice(start, start + tile)
        queries, grads = own_half(left, head, q_ref[rows, :]), own_half(left, head, g_ref[rows, :])
        return queries, grads, mm_cols(queries, k_ref[low:high, :]), mm_cols(grads, v_ref[low:high, :])

    def softmax_back(block, held):
        (start, low, high), lane = spans[block // 2], block % 2 * HEAD_DIM
        _, _, scores, grad_probs = held
        logs = lse_ref[start : start + tile, lane : lane + 1]
        probs = jnp.exp(scores + bias[block // 2, :, : high - low] - logs)
        both = probs * grad_probs
        inner = jnp.sum(both, axis=-1, keepdims=True)
        return (both - probs * inner).astype(bf16), probs.astype(bf16)

    def gather_up(block, held, middle):
        (start, low, high), head = spans[block // 2], block % 2
        queries, grads, _, _ = held
        grad_scores, probs = middle
        done[head] = mm(grad_scores, k_ref[low:high, :])
        keys_sum[low:high, :] += mm_rows(grad_scores, queries)
        values_sum[low:high, :] += mm_rows(probs, grads)
        if head == 1:
            grad_queries = jnp.where(left, done[0], done[1]).astype(bf16)
            out_ref[0, start : start + tile, :] = grad_queries * jnp.asarray(1.0 / math.sqrt(HEAD_DIM), bf16)

    pipelined(2 * len(spans), products, softmax_back, gather_up)
    out_ref[1] = keys_sum[...].astype(bf16)
    out_ref[2] = values_sum[...].astype(bf16)


def attend_back(joint, grads, lse, seg_col, seg_row, begin, count):
    rows, width = joint.shape[0], joint.shape[1] // 3
    pairs = width // LANES
    tile, spans = tile_spans(rows)
    widest = max(high - low for _, low, high in spans)

    def part(which):
        return pl.BlockSpec((rows, LANES), lambda p: (0, which * pairs + begin + p))

    return pl.pallas_call(
        functools.partial(attend_back_kernel, spans, tile),
        grid=(count,),
        in_specs=[
            part(0),
            part(1),
            part(2),
            part(0),
            pl.BlockSpec((rows, LANES), lambda p: (0, p)),
            pl.BlockSpec((rows, 1), lambda p: (0, 0)),
            pl.BlockSpec((1, rows), lambda p: (0, 0)),
        ],
        out_specs=pl.BlockSpec((3, rows, LANES), lambda p: (0, 0, p)),
        out_shape=jax.ShapeDtypeStruct((3, rows, count * LANES), bf16),
        scratch_shapes=[
            pltpu.VMEM((len(spans), tile, widest), f32),
            pltpu.VMEM((rows, LANES), f32),
            pltpu.VMEM((rows, LANES), f32),
        ],
        compiler_params=pltpu.CompilerParams(vmem_limit_bytes=VMEM),
        cost_estimate=cost(0.5 * count),
        name="attend_back",
    )(far(joint), far(joint), far(joint), grads, far(lse), seg_col, seg_row)


def shape_of(*shape, dtype=bf16):
    return jax.ShapeDtypeStruct(shape, dtype)


def far_shape(*shape, dtype=bf16):
    return pltpu.HBM(shape, dtype)


def along(value, axis, depth, step):
    return lax.ppermute(value, axis, [(i, (i + step) % depth) for i in range(depth)])


def load(depth, place, pieces, sems, targets, base=0, sem=0):
    z, x, h = place[0], place[1], place[2]
    copies = []

    def put(source, shard, half, at, shift=0):
        for first, columns, where in targets:
            taken = source
            if columns != source.shape[1]:
                taken = source.at[:, shift + first : shift + first + columns]
            copies.append(pltpu.make_async_copy(taken, where(shard, half, at, source.shape[0]), sems.at[sem + len(copies)]))
            copies[-1].start()

    own, side_own, far, side, near, last_side, last_near = pieces
    quarter = last_side.shape[1]
    for at_x, piece in ((x, own), (1 - x, side_own)):
        for half in range(2):
            put(piece.at[half], z * 2 + at_x, half, 0, base)
    for at_x, at_h, at, piece in (
        (x, h, 0, far),
        (1 - x, h, 0, side),
        (x, 1 - h, 0, near),
        (1 - x, 1 - h, 0, last_side),
        (1 - x, 1 - h, quarter, last_near),
    ):
        for k in range(1, depth):
            put(piece.at[k - 1], lax.rem(z - k + depth, depth) * 2 + at_x, at_h, at)
    return copies


def below(weight, half_rows):
    def where(shard, half, at, count):
        first = pl.multiple_of((shard * 2 + half) * half_rows + at, math.gcd(half_rows, at))
        return weight.at[pl.ds(first, count), :]

    return where


def halve(side, near):
    count, rows, columns = side.shape
    half = rows // 2

    def kernel(side_ref, near_ref, one_ref, two_ref):
        one_ref[...] = side_ref[:, :half, :]
        two_ref[...] = near_ref[:, half:, :]

    return pl.pallas_call(
        kernel,
        in_specs=[pl.BlockSpec(memory_space=pltpu.VMEM)] * 2,
        out_specs=[pl.BlockSpec(memory_space=pltpu.VMEM)] * 2,
        out_shape=[shape_of(count, half, columns)] * 2,
        compiler_params=pltpu.CompilerParams(vmem_limit_bytes=VMEM),
        cost_estimate=cost(1),
        name="halve",
    )(far(side), far(near))


def prepare(place, shards, w_qkv, w_out, w_up, vectors):
    rows, model = w_out.shape
    half, blocks = rows // 2, w_qkv.shape[1] // LANES
    qkv_columns, wide = w_qkv.shape[1] // 2, w_up.shape[1] // 2
    scale_at = qkv_columns
    out_at = scale_at + LANES
    up_at = out_at + model // 2
    unit = wide // shards

    def kernel(place_ref, qkv_ref, out_ref, up_ref, vectors_ref, own_ref, first_ref, up_half_ref):
        lo, h = place_ref[3], place_ref[2]
        left = lax.broadcasted_iota(jnp.int32, (rows, LANES), 1) < HEAD_DIM

        def put(at, value):
            own_ref[0, :, at : at + value.shape[1]] = value[:half]
            own_ref[1, :, at : at + value.shape[1]] = value[half:]

        for block in range(0, blocks, 2):
            one = qkv_ref[:, block * LANES : (block + 1) * LANES].astype(f32)
            two = qkv_ref[:, (block + 1) * LANES : (block + 2) * LANES].astype(f32)
            even = jnp.where(left, one, pltpu.roll(two, HEAD_DIM, 1))
            odd = jnp.where(left, pltpu.roll(one, HEAD_DIM, 1), two)
            put(block // 2 * LANES, jnp.where(lo == 0, even, odd).astype(bf16))
        columns = jnp.concatenate([vectors_ref[...].astype(f32), jnp.zeros((LANES - 4, rows), f32)], axis=0)
        put(scale_at, columns.T.astype(bf16))
        outs = jnp.where(lo == 0, out_ref[:half, :], out_ref[half:, :])
        put(out_at, jnp.concatenate([outs[:, : model // 2], outs[:, model // 2 :]], axis=0))
        for shard in range(shards):
            at = shard * 2 * unit
            put(up_at + shard * unit, jnp.where(lo == 0, up_ref[:, at : at + unit], up_ref[:, at + unit : at + 2 * unit]))
        first_ref[...] = own_ref[h, :, :up_at]
        up_half_ref[...] = own_ref[h, :, up_at:]

    return pl.pallas_call(
        kernel,
        in_specs=[pl.BlockSpec(memory_space=pltpu.SMEM)] + [pl.BlockSpec(memory_space=pltpu.VMEM)] * 4,
        out_specs=[pl.BlockSpec(memory_space=pltpu.VMEM)] * 3,
        out_shape=[shape_of(2, half, up_at + wide), shape_of(half, up_at), shape_of(half, wide)],
        compiler_params=pltpu.CompilerParams(vmem_limit_bytes=VMEM),
        cost_estimate=cost(2),
        name="prepare",
    )(place, far(w_qkv), far(w_out), far(w_up), vectors)


def finish_up(place, shards, own, other):
    rows, columns = own.shape
    unit = columns // shards

    def kernel(place_ref, own_ref, other_ref, out_ref):
        lo = place_ref[3]
        for shard in range(shards):
            at, mine, theirs = shard * 2 * unit, own_ref, other_ref
            one = mine[:, shard * unit : (shard + 1) * unit].astype(f32)
            two = theirs[:, shard * unit : (shard + 1) * unit].astype(f32)
            out_ref[:, at : at + unit] = jnp.where(lo == 0, one, two)
            out_ref[:, at + unit : at + 2 * unit] = jnp.where(lo == 0, two, one)

    return pl.pallas_call(
        kernel,
        in_specs=[pl.BlockSpec(memory_space=pltpu.SMEM)] + [pl.BlockSpec(memory_space=pltpu.VMEM)] * 2,
        out_specs=pl.BlockSpec(memory_space=pltpu.VMEM),
        out_shape=shape_of(rows, 2 * columns, dtype=f32),
        cost_estimate=cost(2),
        name="finish_up",
    )(place, own, other)


def finish_qkv(place, columns, owns, others):
    rows = owns[0].shape[0]
    half, pieces = rows // 2, len(owns)
    third = columns // 3
    model = 2 * (owns[0].shape[1] - columns - LANES)

    def kernel(place_ref, *refs):
        lo = place_ref[3]
        owns_refs, others_refs = refs[:pieces], refs[pieces : 2 * pieces]
        qkv_ref, out_ref, sums_ref = refs[2 * pieces :]
        left = lax.broadcasted_iota(jnp.int32, (rows, LANES), 1) < HEAD_DIM
        at = 0
        for j in range(3):
            for own_ref, other_ref in zip(owns_refs, others_refs):
                for first in range(j * third, (j + 1) * third, LANES):
                    mine = own_ref[:, first : first + LANES].astype(f32)
                    theirs = other_ref[:, first : first + LANES].astype(f32)
                    one, two = jnp.where(lo == 0, mine, theirs), jnp.where(lo == 0, theirs, mine)
                    qkv_ref[:, at : at + LANES] = jnp.where(left, one, pltpu.roll(two, HEAD_DIM, 1))
                    qkv_ref[:, at + LANES : at + 2 * LANES] = jnp.where(left, pltpu.roll(one, HEAD_DIM, 1), two)
                    at += 2 * LANES
        sums = jnp.zeros((rows, LANES), f32)
        for ref in refs[: 2 * pieces]:
            sums = sums + ref[:, columns : columns + LANES].astype(f32)
        sums_ref[...] = sums.T[:8, :]
        mine, theirs = (ref[:, columns + LANES :].astype(f32) for ref in (owns_refs[0], others_refs[0]))
        for at, value in ((0, jnp.where(lo == 0, mine, theirs)), (half, jnp.where(lo == 0, theirs, mine))):
            out_ref[at : at + half, : model // 2] = value[:half]
            out_ref[at : at + half, model // 2 :] = value[half:]

    return pl.pallas_call(
        kernel,
        in_specs=[pl.BlockSpec(memory_space=pltpu.SMEM)] + [pl.BlockSpec(memory_space=pltpu.VMEM)] * (2 * pieces),
        out_specs=[pl.BlockSpec(memory_space=pltpu.VMEM)] * 3,
        out_shape=[
            shape_of(rows, 2 * pieces * columns, dtype=f32),
            shape_of(rows, model, dtype=f32),
            shape_of(8, rows, dtype=f32),
        ],
        compiler_params=pltpu.CompilerParams(vmem_limit_bytes=VMEM),
        cost_estimate=cost(2),
        name="finish_qkv",
    )(place, *owns, *others)


def plus(left, right):
    return (left.astype(f32) + right.astype(f32)).astype(bf16)


def fold_one(place, keep, came, shape=shape_of):
    depth, top, columns = keep[0].shape
    low = top // 2

    def kernel(place_ref, keep_one, keep_two, came_one, came_two, kept_ref, send_one, send_two):
        at_x, at_h = place_ref[1] == 0, place_ref[2] == 0
        one, two = plus(keep_one[0], came_one[0]), plus(keep_two[0], came_two[0])
        kept_ref[0, 0] = jnp.where(at_h, one[:low], one[low:])
        send_one[0] = jnp.where(at_h, one[low:], one[:low])
        kept_ref[1, 0] = jnp.where(at_x, two[0], two[1])
        send_two[0] = jnp.where(at_x, two[1], two[0])

    one = pl.BlockSpec((1, top, columns), lambda i: (i, 0, 0))
    two = pl.BlockSpec((1, 2, low, columns), lambda i: (i, 0, 0, 0))
    send = pl.BlockSpec((1, low, columns), lambda i: (i, 0, 0))
    kept, *sends = pl.pallas_call(
        kernel,
        grid=(depth,),
        in_specs=[pl.BlockSpec(memory_space=pltpu.SMEM), one, two, one, two],
        out_specs=[pl.BlockSpec((2, 1, low, columns), lambda i: (0, i, 0, 0)), send, send],
        out_shape=[shape(2, depth, low, columns)] + [shape(depth, low, columns)] * 2,
        compiler_params=pltpu.CompilerParams(vmem_limit_bytes=VMEM),
        cost_estimate=cost(1),
        name="fold_one",
    )(place, *keep, *came)
    return kept, sends


def fold_two(place, kept, came):
    _, depth, low, columns = kept.shape

    def kernel(place_ref, kept_ref, came_one, came_two, *refs):
        *outs, sums = refs
        for half, came_ref in enumerate((came_one, came_two)):
            for at in range(depth):
                sums[at, half] = plus(kept_ref[half, at], came_ref[at])
        for k, out in enumerate(outs):
            out[...] = sums[lax.rem(place_ref[0] + k, depth)]

    own, *sends = pl.pallas_call(
        kernel,
        in_specs=[pl.BlockSpec(memory_space=pltpu.SMEM)] + [pl.BlockSpec(memory_space=pltpu.VMEM)] * 3,
        out_specs=[pl.BlockSpec(memory_space=pltpu.VMEM)] * depth,
        out_shape=[shape_of(2, low, columns)] * depth,
        scratch_shapes=[pltpu.VMEM((depth, 2, low, columns), bf16)],
        compiler_params=pltpu.CompilerParams(vmem_limit_bytes=VMEM),
        cost_estimate=cost(1),
        name="fold_two",
    )(place, kept, *came)
    return own, sends


def add_up(own, came):
    total = own.astype(f32)
    for piece in came:
        total = total + piece.astype(f32)
    return total.astype(bf16)


def row_block(tile, width):
    return pl.BlockSpec((tile, width), lambda i: (i, 0))


def whole_block(*shape):
    return pl.BlockSpec(shape, lambda i: (0,) * len(shape))


def weight_call(name, step, tiles, place, inputs, sets, outs, scratch, copies, micros):
    pieces = [piece for held in sets for piece in held]

    def kernel(place_ref, *refs):
        refs = list(refs)

        def take(count):
            taken = refs[:count]
            del refs[:count]
            return taken

        given = take(len(inputs))
        held = [take(len(one)) for one in sets]
        made = take(len(outs))
        step(place_ref, given, held, made, refs[:-1], refs[-1])

    return pl.pallas_call(
        kernel,
        grid=(tiles,),
        in_specs=[pl.BlockSpec(memory_space=pltpu.SMEM)]
        + [spec for _, spec in inputs]
        + [pl.BlockSpec(memory_space=pltpu.HBM)] * len(pieces),
        out_specs=[spec for _, spec in outs],
        out_shape=[shape for shape, _ in outs],
        scratch_shapes=list(scratch) + [pltpu.SemaphoreType.DMA((copies,))],
        compiler_params=pltpu.CompilerParams(vmem_limit_bytes=VMEM),
        cost_estimate=cost(micros),
        name=name,
    )(place, *[v for v, _ in inputs], *[far(piece) for piece in pieces])


def unit_of(values):
    centred = values - jnp.mean(values, axis=-1, keepdims=True)
    variance = jnp.mean(centred * centred, axis=-1, keepdims=True)
    inverse = lax.rsqrt(variance + epsilon)
    return centred * inverse, inverse


def unit_back(grad_unit, unit_rows, inverse):
    mean_grad = jnp.mean(grad_unit, axis=-1, keepdims=True)
    mean_cross = jnp.mean(grad_unit * unit_rows, axis=-1, keepdims=True)
    return inverse * (grad_unit - mean_grad - unit_rows * mean_cross)


def bell_and_slope(values):
    phi = 0.5 + 0.5 * lax.erf(values * math.sqrt(0.5))
    density = jnp.exp(values * values * -0.5) * (1.0 / math.sqrt(2.0 * math.pi))
    return values * phi, phi + values * density


def outer_whole(left, right):
    rows, across = left.shape
    block = min(256, across)

    def kernel(left_ref, right_ref, out_ref):
        out_ref[...] = mm_rows(left_ref[...], right_ref[...]).astype(bf16)

    return pl.pallas_call(
        kernel,
        grid=(across // block,),
        in_specs=[pl.BlockSpec((rows, block), lambda i: (0, i)), whole_block(*right.shape)],
        out_specs=row_block(block, right.shape[1]),
        out_shape=shape_of(across, right.shape[1]),
        compiler_params=pltpu.CompilerParams(vmem_limit_bytes=VMEM),
        cost_estimate=cost(7),
        name="outer_whole",
    )(left, right)


def outer(place, depth, left, right, out_pair=None, weight=None, scales=None, piece=0, sums=None):
    rows, own_rows = left.shape[0], left.shape[1] // (2 * depth)
    top, low = own_rows // 2, own_rows // 4
    parts = right.shape[0] if right.ndim == 3 else 1
    third = right.shape[-1]
    columns = parts * third
    given = [left, right]
    specs = [pl.BlockSpec((rows, 2 * own_rows), lambda i: (0, i)), whole_block(*right.shape)]
    total = columns
    if weight is not None:
        given += [weight, scales, sums]
        specs += [pl.BlockSpec((2 * own_rows, part.shape[1]), lambda i: (i, 0)) for part in (weight, scales)]
        specs.append(pl.BlockSpec((8, 2 * own_rows), lambda i: (0, i)))
        total += LANES
        width = weight.shape[1] // 3
    if out_pair is not None:
        out_block = out_pair[0].shape[1] // depth
        given += out_pair
        specs += [pl.BlockSpec((rows, out_block), lambda i: (0, i)), whole_block(*out_pair[1].shape)]
        half = out_pair[1].shape[1] // 2
        total += half

    def kernel(place_ref, *refs):
        ins, outs = list(refs[: len(given)]), refs[len(given) :]
        at_x, at_h = place_ref[1] == 0, place_ref[2] == 0
        keep_first, send_first, keep_second, send_second = outs

        def put(first, value):
            where = slice(first, first + value.shape[2])
            heads = value[:, :top].astype(bf16)
            keep_first[0, :, where] = jnp.where(at_x, heads[0], heads[1])
            send_first[0, :, where] = jnp.where(at_x, heads[1], heads[0])
            lower, upper = value[:, top : top + low].astype(bf16), value[:, top + low :].astype(bf16)
            keep_second[0, :, :, where] = jnp.where(at_h, lower, upper)
            send_second[0, :, :, where] = jnp.where(at_h, upper, lower)

        left_ref, right_ref = ins.pop(0), ins.pop(0)
        rights = [right_ref.at[j] for j in range(parts)] if parts > 1 else [right_ref]
        products = [mm_rows(left_ref[...], ref[...]) for ref in rights]
        for j, product in enumerate(products):
            put(j * third, product.reshape(2, own_rows, third))
        first = columns
        if weight is not None:
            weight_ref, scales_ref, sums_ref = ins.pop(0), ins.pop(0), ins.pop(0)
            bias_sum = cross = 0.0
            for j, product in enumerate(products):
                at = j * width + piece * third
                part = weight_ref[:, at : at + third].astype(f32)
                column_sums = jnp.sum(rights[j][...].astype(f32), axis=0, keepdims=True)
                bias_sum = bias_sum + jnp.sum(part * column_sums, axis=1, keepdims=True)
                cross = cross + jnp.sum(part * product, axis=1, keepdims=True)
            gain, bias = scales_ref[:, 0:1].astype(f32), scales_ref[:, 1:2].astype(f32)
            gain_sum = (cross - bias * bias_sum) / gain
            kept = jnp.concatenate(
                [jnp.zeros((2, 2 * own_rows), f32), sums_ref[0:2, :], jnp.zeros((LANES - 4, 2 * own_rows), f32)], axis=0
            ).T
            lane = lax.broadcasted_iota(jnp.int32, kept.shape, 1)
            kept = jnp.where(lane == 0, gain_sum, jnp.where(lane == 1, bias_sum, kept))
            put(first, kept.reshape(2, own_rows, LANES))
            first += LANES
        if out_pair is not None:
            product = mm_rows(ins.pop(0)[...], ins.pop(0)[...]).reshape(2, top, 2 * half)
            put(first, jnp.concatenate([product[:, :, :half], product[:, :, half:]], axis=1))

    def spec(*block):
        return pl.BlockSpec((1, *block), lambda i: (i,) + (0,) * len(block))

    first_shape, second_shape = (top, total), (2, low, total)
    made = pl.pallas_call(
        kernel,
        grid=(depth,),
        in_specs=[pl.BlockSpec(memory_space=pltpu.SMEM)] + specs,
        out_specs=[spec(*first_shape)] * 2 + [spec(*second_shape)] * 2,
        out_shape=[shape_of(depth, *first_shape)] * 2 + [shape_of(depth, *second_shape)] * 2,
        compiler_params=pltpu.CompilerParams(vmem_limit_bytes=VMEM),
        cost_estimate=cost(6),
        name="outer",
    )(place, *given)
    return (made[0], made[2]), (made[1], made[3])


def body(
    group,
    depth,
    tokens,
    segment_ids,
    norm1_gain,
    norm1_bias,
    w_qkv,
    w_out,
    norm2_gain,
    norm2_bias,
    w_up,
    w_down,
    cotangent,
):
    h, lo = lax.axis_index("hi"), lax.axis_index("lo")
    z, x = lax.axis_index("fz"), lax.axis_index("fx")
    micro, _, chunk, model = tokens.shape
    shards = 2 * depth
    rows = micro * group * chunk
    own_rows = w_out.shape[0]
    inner = w_up.shape[1] // group
    split_out = (own_rows // HEAD_DIM) % group == 0
    head_columns = model // group
    half_rows = own_rows // 2
    tile = min(TILE, rows)
    tiles = rows // tile
    scale_at = 3 * head_columns
    copies = 4 * shards
    wide = min(512, inner)
    shard_axes = ("fz", "fx")

    rest = range(1, depth)

    def whole_group(value, axis):
        if group == 2:
            return ordered(value, swap(value, "lo"), lo, axis)
        return lax.all_gather(value, "lo", axis=axis)

    def other_part(partial):
        if group == 2:
            return swap(partial, "lo")
        return (lax.psum(partial, "lo").astype(f32) - partial.astype(f32)).astype(bf16)

    def own_chunks(full):
        return pick(full.reshape(micro, group, chunk, -1), lo, 1)

    def other_own(partial):
        parts = partial.reshape(micro, group, chunk, model)
        if group == 2:
            return swap(pick(parts, 1 - lo, 1), "lo")
        return plus(lax.psum_scatter(parts, "lo", scatter_dimension=1), -pick(parts, lo, 1))

    def hop(values, parity):
        return [along(value, "fz", depth, k) for k, value in zip(rest, values) if k % 2 == parity]

    fused_out = split_out and group == 2
    out_rows, half_model = own_rows // group, model // 2
    place = jnp.stack([z, x, h, lo]).astype(jnp.int32)
    came = swap(jnp.stack([pick(tokens[:, 0], 1 - h, 0), pick(cotangent[:, 0], 1 - h, 0)]), "hi")
    vectors = jnp.stack([norm1_gain, norm1_bias, norm2_gain, norm2_bias])
    if fused_out:
        both_own, first_half, up_half = prepare(place, shards, w_qkv, w_out, w_up, vectors)
    else:
        if split_out:
            qkv_part = pick(w_qkv.reshape(own_rows, 3, shards, group, -1), lo, 3).reshape(own_rows, -1)
            out_part = pick(w_out.reshape(group, out_rows, model), lo, 0)
        else:
            qkv_part = pick(w_qkv.reshape(own_rows, 3, group, -1), lo, 2).reshape(own_rows, -1)
            out_part = w_out
        up_part = pick(w_up.reshape(own_rows, shards, group, -1), lo, 2).reshape(own_rows, -1)
        parts = [qkv_part, jnp.pad(vectors.T, ((0, 0), (0, LANES - 4)))]
        both_own = jnp.concatenate(parts + [up_part], axis=1).reshape(2, half_rows, -1)
        half = pick(both_own, h, 0)
        first_half, up_half = half[:, : scale_at + LANES], half[:, scale_at + LANES :]
        out_weight = lax.all_gather(out_part, shard_axes, axis=0, tiled=True)
    up_at = first_half.shape[1]
    down_rows = inner // shards
    fine_down = down_rows % 64 == 0
    down_part = pick(w_down.reshape(group, 2, down_rows // 2, model), lo, 0)
    first_far = [along(first_half, "fz", depth, k) for k in rest]
    side_own = swap(both_own, "fx")
    first_far, side_own, came, up_half = sync(first_far, side_own, came, up_half)

    def last_quarters(side_part, near_part):
        return swap(side_part, "hi"), swap(near_part, "fx")

    first_far = jnp.stack(first_far)
    first_side, first_near = swap(first_far, "fx"), swap(first_far, "hi")
    up_far = [along(up_half, "fz", depth, k) for k in rest]
    first_side, first_near, up_far, came, down_part = sync(first_side, first_near, up_far, came, down_part)

    cuts, came, tokens, up_far = sync(halve(first_side, first_near), came, tokens, up_far)
    first_last = last_quarters(*cuts)
    down_half = pick(down_part, h, 0)
    if not fine_down:
        downward = lax.all_gather(down_part.reshape(down_rows, model), shard_axes, axis=0, tiled=True)
    inputs = whole_group(ordered(pick(tokens[:, 0], h, 0), came[0], h, 0), 1).reshape(rows, model)
    up_far = jnp.stack(up_far)
    first_last, inputs, up_far, came, down_half, down_part = sync(
        first_last, inputs, up_far, came, down_half, down_part
    )
    first_set = [both_own, side_own, first_far, first_side, first_near, *first_last]

    segments = pick(segment_ids[:, 0], h, 0)
    seg_col, seg_row = segments[:, None], segments[None, :]

    def project(place_ref, given, held, made, scratch, sems):
        (rows_ref,), (normed_ref, joint_ref, scales_ref, weight, columns, *outs) = given, made

        @pl.when(pl.program_id(0) == 0)
        def _():
            targets = [
                (0, 3 * head_columns, below(weight, half_rows)),
                (scale_at, LANES, below(columns, half_rows)),
            ]
            if fused_out:
                targets.append((scale_at + LANES, half_model, below(scratch[0], half_rows)))
            for copy in load(depth, place_ref, held[0], sems, targets):
                copy.wait()
            scales_ref[...] = columns[...].astype(f32).T[:8, :]
            for shard in range(shards if fused_out else 0):
                for part in range(2):
                    at = shard * own_rows + part * out_rows
                    outs[0][
                        shard * out_rows : (shard + 1) * out_rows, part * half_model : (part + 1) * half_model
                    ] = scratch[0][at : at + out_rows, :]

        unit_rows, _ = unit_of(rows_ref[...].astype(f32))
        normed = (unit_rows * scales_ref[0:1, :] + scales_ref[1:2, :]).astype(bf16)
        normed_ref[...] = normed
        for at in range(0, 3 * head_columns, head_columns):
            part = mm(normed, weight[:, at : at + head_columns])
            if at == 0:
                part = part * (1.0 / math.sqrt(HEAD_DIM))
            joint_ref[:, at : at + head_columns] = part.astype(bf16)

    wholes = [(8, model, f32), (model, 3 * head_columns, bf16), (model, LANES, bf16)]
    if fused_out:
        wholes.append((head_columns, model, bf16))
    normed, joint, scales, joint_weight, scale_columns, *outs = weight_call(
        "project",
        project,
        tiles,
        place,
        [(inputs, row_block(tile, model))],
        [first_set],
        [
            (far_shape(rows, model), row_block(tile, model)),
            (far_shape(rows, 3 * head_columns), row_block(tile, 3 * head_columns)),
        ]
        + [(far_shape(*shape, dtype=dtype), whole_block(*shape)) for *shape, dtype in wholes],
        [pltpu.VMEM((model, half_model), bf16)] if fused_out else [],
        3 * copies,
        8,
    )
    if fused_out:
        (out_weight,) = outs
    pairs = head_columns // LANES
    pieces = 2 if pairs % 2 == 0 else 1
    count = pairs // pieces
    part_columns = count * LANES
    mixed = [attend(joint, seg_col, seg_row, 0, count)]
    up_side, up_near = swap(up_far, "fx"), swap(up_far, "hi")
    down_odd = down_even = down_side_own = None
    if fine_down:
        down_odd = [along(down_half, "fz", depth, k) for k in rest if k % 2]
        down_side_own = swap(down_part, "fx")
    mixed, joint, up_side, up_near, scales, out_weight, came, down_odd, down_side_own, down_half = sync(
        mixed, joint, up_side, up_near, scales, out_weight, came, down_odd, down_side_own, down_half
    )

    cuts, joint, came, down_half = sync(halve(up_side, up_near), joint, came, down_half)
    up_last = last_quarters(*cuts)
    for piece in range(1, pieces):
        mixed.append(attend(joint, seg_col, seg_row, piece * count, count))
    grad_result = whole_group(ordered(pick(cotangent[:, 0], h, 0), came[1], h, 0), 1).reshape(rows, model)
    if fine_down:
        down_even = [along(down_half, "fz", depth, k) for k in rest if k % 2 == 0]
    mixed, up_last, out_weight, grad_result, down_even = sync(mixed, up_last, out_weight, grad_result, down_even)
    up_set = [both_own, side_own, up_far, up_side, up_near, *up_last]
    lse = mixed[0][1] if pieces == 1 else jnp.concatenate([part for _, part in mixed], axis=1)

    def leave(place_ref, given, held, made, scratch, sems):
        *parts_refs, weight = given
        out_ref, attended_ref = made
        weight = own_out(weight, place_ref)
        total = jnp.zeros(out_ref.shape, f32)
        for piece, part_ref in enumerate(parts_refs):
            at = slice(piece * part_columns, (piece + 1) * part_columns)
            attended_ref[:, at] = part_ref[...]
            total = total + mm(part_ref[...], weight[at, :])
        out_ref[...] = total.astype(bf16)

    def own_out(weight, place_ref):
        if split_out:
            return weight[...]
        return weight[pl.ds(pl.multiple_of(place_ref[3] * head_columns, head_columns), head_columns), :]

    branch, attended = weight_call(
        "leave",
        leave,
        tiles,
        place,
        [(value, row_block(tile, part_columns)) for value, _ in mixed]
        + [(out_weight, whole_block(*out_weight.shape))],
        [],
        [
            (shape_of(rows, model), row_block(tile, model)),
            (far_shape(rows, head_columns), row_block(tile, head_columns)),
        ],
        [],
        1,
        3,
    )
    branch_other = other_part(branch)

    if fine_down:
        down_far = jnp.stack([down_odd[k // 2] if k % 2 else down_even[k // 2 - 1] for k in rest])
        down_side, down_near = swap(down_far, "fx"), swap(down_far, "hi")

    def widen(place_ref, given, held, made, scratch, sems):
        rows_ref, own_ref, other_ref, scales_ref = given
        middle_ref, normed_ref, hidden_ref, slope_ref = made
        (weight,) = scratch

        @pl.when(pl.program_id(0) == 0)
        def _():
            targets = [(0, inner, below(weight, half_rows))]
            for copy in load(depth, place_ref, held[0], sems, targets, up_at):
                copy.wait()

        added = own_ref[...].astype(f32) + other_ref[...].astype(f32)
        middle = rows_ref[...].astype(f32) + added
        middle_ref[...] = middle.astype(bf16)
        unit_rows, _ = unit_of(middle)
        normed = (unit_rows * scales_ref[2:3, :] + scales_ref[3:4, :]).astype(bf16)
        normed_ref[...] = normed
        for at in range(0, inner, wide):
            hidden, slope = bell_and_slope(mm(normed, weight[:, at : at + wide]))
            hidden_ref[:, at : at + wide] = hidden.astype(bf16)
            slope_ref[:, at : at + wide] = slope.astype(bf16)

    middle, normed_two, hidden, slope = weight_call(
        "widen",
        widen,
        tiles,
        place,
        [
            (inputs, row_block(tile, model)),
            (branch, row_block(tile, model)),
            (branch_other, row_block(tile, model)),
            (scales, whole_block(8, model)),
        ],
        [up_set],
        [
            (far_shape(rows, model), row_block(tile, model)),
            (far_shape(rows, model), row_block(tile, model)),
            (far_shape(rows, inner), row_block(tile, inner)),
            (far_shape(rows, inner), row_block(tile, inner)),
        ],
        [pltpu.VMEM((model, inner), bf16)],
        copies,
        13,
    )

    if fine_down:
        hidden, slope, normed_two, down_side, down_near, lse = sync(
            hidden, slope, normed_two, down_side, down_near, lse
        )
        cuts, hidden = sync(halve(down_side, down_near), hidden)
        down_last = last_quarters(*cuts)
        down_keep, down_send = outer(place, depth, far(hidden), grad_result)
        hidden, slope, down_keep, down_send, normed_two, down_last = sync(
            hidden, slope, down_keep, down_send, normed_two, down_last
        )
        down_set = [down_part, down_side_own, down_far, down_side, down_near, *down_last]
        down_came = swap(down_send[0], "fx"), swap(down_send[1], "hi")
    else:
        down_keep = down_came = outer_whole(hidden, grad_result)
        down_send = None

    by_chunk = group == 2 and tile == chunk

    def narrow(place_ref, given, held, made, scratch, sems):
        hidden_ref, grad_ref, slope_ref, *downs = given
        *out_refs, pre_ref, back_ref = made
        upward = scratch[0]
        down_ref = scratch[1] if fine_down else downs[0]

        @pl.when(pl.program_id(0) == 0)
        def _():
            started = []
            if fine_down:
                targets = [(0, model, below(down_ref, down_rows // 2))]
                started = load(depth, place_ref, held[1], sems, targets, sem=copies)
            targets = [(0, inner, below(upward, half_rows))]
            for copy in started + load(depth, place_ref, held[0], sems, targets, up_at):
                copy.wait()

        for at in range(0, inner, wide):
            grad = mm_cols(grad_ref[...], down_ref[at : at + wide, :])
            pre_ref[:, at : at + wide] = (grad * slope_ref[:, at : at + wide].astype(f32)).astype(bf16)
        back_ref[...] = mm_cols(pre_ref[...], upward[...]).astype(bf16)
        out = mm(hidden_ref[...], down_ref[...]).astype(bf16)
        if by_chunk:
            own = lax.rem(pl.program_id(0), 2) == place_ref[3]

            @pl.when(own)
            def _():
                out_refs[0][0] = out

            @pl.when(~own)
            def _():
                out_refs[1][0] = out
        else:
            out_refs[0][...] = out

    *results, grad_pre, back = weight_call(
        "narrow",
        narrow,
        tiles,
        place,
        [
            (far(hidden), row_block(tile, inner)),
            (far(grad_result), row_block(tile, model)),
            (far(slope), row_block(tile, inner)),
        ]
        + ([] if fine_down else [(far(downward), whole_block(inner, model))]),
        [up_set, down_set] if fine_down else [up_set],
        (
            [
                (shape(micro, chunk, model), pl.BlockSpec((1, chunk, model), lambda i: (i // 2, 0, 0)))
                for shape in (far_shape, shape_of)
            ]
            if by_chunk
            else [(far_shape(rows, model), row_block(tile, model))]
        )
        + [
            (far_shape(rows, inner), row_block(tile, inner)),
            (far_shape(rows, model), row_block(tile, model)),
        ],
        [pltpu.VMEM((model, inner), bf16), pltpu.VMEM((inner, model), bf16)],
        2 * copies,
        18,
    )
    down_kept = None
    if fine_down:
        down_kept, down_send = fold_one(place, down_keep, down_came, far_shape)
    results, grad_pre, back, normed_two, down_kept, down_send, down_came = sync(
        results, grad_pre, back, normed_two, down_kept, down_send, down_came
    )

    back_other = other_part(back)
    if by_chunk:
        result, result_other = results[0], swap(results[1], "lo")
    else:
        result, result_other = own_chunks(results[0]), other_own(results[0])
    if fine_down:
        down_came = swap(down_send[0], "hi"), swap(down_send[1], "fx")
    up_keep, up_send = outer(place, depth, far(normed_two), far(grad_pre))
    back, back_other, up_keep, up_send, result_other = sync(back, back_other, up_keep, up_send, result_other)

    def between(place_ref, given, held, made, scratch, sems):
        grad_ref, own_ref, other_ref, middle_ref, scales_ref, weight = given
        branch_ref, attended_ref, sums_ref = made

        @pl.when(pl.program_id(0) == 0)
        def _():
            sums_ref[...] = jnp.zeros_like(sums_ref)

        unit_rows, inverse = unit_of(middle_ref[...].astype(f32))
        own_back = own_ref[...].astype(f32)
        back_rows = own_back + other_ref[...].astype(f32)
        sums_ref[0:1, :] += jnp.sum(own_back * unit_rows, axis=0, keepdims=True)
        sums_ref[1:2, :] += jnp.sum(own_back, axis=0, keepdims=True)
        grads = grad_ref[...].astype(f32) + unit_back(back_rows * scales_ref[2:3, :], unit_rows, inverse)
        low = grads.astype(bf16)
        branch_ref[...] = low
        attended_ref[...] = mm_cols(low, own_out(weight, place_ref)).astype(bf16)

    grad_branch, grad_attended, sums_two = weight_call(
        "between",
        between,
        tiles,
        place,
        [
            (grad_result, row_block(tile, model)),
            (back, row_block(tile, model)),
            (back_other, row_block(tile, model)),
            (far(middle), row_block(tile, model)),
            (scales, whole_block(8, model)),
            (out_weight, whole_block(*out_weight.shape)),
        ],
        [],
        [
            (far_shape(rows, model), row_block(tile, model)),
            (shape_of(rows, head_columns), row_block(tile, head_columns)),
            (shape_of(8, model, dtype=f32), whole_block(8, model)),
        ],
        [],
        1,
        8,
    )
    up_came = swap(up_send[0], "fx"), swap(up_send[1], "hi")
    down_sum = None
    if fine_down:
        grad_attended, down_came, down_kept = sync(grad_attended, down_came, down_kept)
        down_sum, down_send = fold_two(place, down_kept, down_came)
        grad_attended, down_send = sync(grad_attended, down_send)
        down_came = [along(value, "fz", depth, k) for k, value in zip(rest, down_send)]
    grad_joint = attend_back(joint, grad_attended, lse, seg_col, seg_row, 0, pairs)
    grad_joint, grad_branch, up_came, result_other, down_came, down_sum = sync(
        grad_joint, grad_branch, up_came, result_other, down_came, down_sum
    )

    def both_halves(value):
        return ordered(value, swap(value, "hi"), h, 1).reshape(-1, value.shape[2])

    up_kept, up_send = fold_one(place, up_keep, up_came)
    up_kept, up_send, grad_joint = sync(up_kept, up_send, grad_joint)
    up_came = swap(up_send[0], "hi"), swap(up_send[1], "fx")
    if fine_down:
        down_own = both_halves(add_up(down_sum, down_came))
    else:
        down_own = lax.psum(lax.psum_scatter(down_came, shard_axes, scatter_dimension=0, tiled=True), "hi")
    last_keep, last_send = outer(
        place,
        depth,
        normed,
        grad_joint,
        out_pair=[attended, grad_branch] if fused_out else None,
        weight=joint_weight,
        scales=scale_columns,
        sums=sums_two,
    )
    up_came, last_keep, last_send, down_own, grad_joint, result_other = sync(
        up_came, last_keep, last_send, down_own, grad_joint, result_other
    )

    up_sum, up_send = fold_two(place, up_kept, up_came)
    up_sum, up_send, last_send, grad_joint = sync(up_sum, up_send, last_send, grad_joint)
    last_came = swap(last_send[0], "fx"), swap(last_send[1], "hi")
    up_came = [along(value, "fz", depth, k) for k, value in zip(rest, up_send)]

    def enter(place_ref, given, held, made, scratch, sems):
        part_ref, weight = given
        (out_ref,) = made
        grads = jnp.zeros(out_ref.shape, f32)
        for j in range(3):
            grads = grads + mm_cols(part_ref[j], weight[:, j * head_columns : (j + 1) * head_columns])
        out_ref[...] = grads.astype(bf16)

    (entered,) = weight_call(
        "enter",
        enter,
        tiles,
        place,
        [
            (grad_joint, pl.BlockSpec((3, tile, head_columns), lambda i: (0, i, 0))),
            (joint_weight, whole_block(*joint_weight.shape)),
        ],
        [],
        [(shape_of(rows, model), row_block(tile, model))],
        [],
        1,
        14,
    )
    output = (own_chunks(middle).astype(f32) + result.astype(f32) + result_other.astype(f32)).astype(bf16)
    last_came, entered, up_sum, up_came, down_own, output = sync(
        last_came, entered, up_sum, up_came, down_own, output
    )

    last_kept, last_send = fold_one(place, last_keep, last_came)
    up_own = add_up(up_sum, up_came)
    last_kept, last_send, entered, up_own, down_own = sync(last_kept, last_send, entered, up_own, down_own)
    last_came = swap(last_send[0], "hi"), swap(last_send[1], "fx")
    up_own = both_halves(up_own)
    down_all = whole_group(down_own, 0).reshape(-1, model).astype(f32)
    entered_other = other_own(entered)
    grad_normed = own_chunks(entered).astype(f32) + entered_other.astype(f32)
    unit_own, inverse_own = unit_of(own_chunks(inputs).astype(f32))
    grad_tokens = own_chunks(grad_branch).astype(f32) + unit_back(grad_normed * scales[0], unit_own, inverse_own)
    grad_sent = pick(grad_tokens, 1 - h, 0).astype(bf16)
    last_came, grad_tokens, grad_sent, up_own, down_all, output = sync(
        last_came, grad_tokens, grad_sent, up_own, down_all, output
    )

    last_sum, last_send = fold_two(place, last_kept, last_came)
    last_came = [along(value, "fz", depth, k) for k, value in zip(rest, last_send)]
    grad_came = swap(grad_sent, "hi")
    output_came = swap(pick(output, 1 - h, 0), "hi")
    up_all = None
    if fused_out:
        up_all = finish_up(place, shards, up_own, swap(up_own, "lo"))
    last_came, grad_came, grad_tokens, up_own, up_all, output_came = sync(
        last_came, grad_came, grad_tokens, up_own, up_all, output_came
    )

    last_own = both_halves(add_up(last_sum, last_came))
    output = ordered(pick(output, h, 0), output_came, h, 0)[:, None]
    grad_tokens = ordered(pick(grad_tokens, h, 0), grad_came.astype(f32), h, 0)[:, None]
    last_own, grad_tokens, output = sync(last_own, grad_tokens, output)
    if fused_out:
        qkv_all, out_all, sums = finish_qkv(place, 3 * head_columns, [last_own], [swap(last_own, "lo")])
    else:
        up_all = whole_group(up_own.reshape(own_rows, shards, -1), 2).reshape(own_rows, -1).astype(f32)
        columns = 3 * head_columns
        qkv_own = last_own[:, :columns]
        if split_out:
            qkv_all = whole_group(qkv_own.reshape(own_rows, 3, shards, -1), 3)
        else:
            qkv_all = whole_group(qkv_own.reshape(own_rows, 3, -1), 2)
        qkv_all = qkv_all.reshape(own_rows, -1).astype(f32)
        sums = jnp.sum(whole_group(last_own[:, columns : columns + 4].astype(f32), 0), axis=0).T
        grad_out = outer_whole(attended, grad_branch)
        if not split_out:
            empty = jnp.zeros((model, model), bf16)
            grad_out = lax.dynamic_update_slice_in_dim(empty, grad_out, lo * head_columns, 0)
        out_own = lax.psum(lax.psum_scatter(grad_out, shard_axes, scatter_dimension=0, tiled=True), "hi")
        out_all = whole_group(out_own, 0).reshape(own_rows, model) if split_out else lax.psum(out_own, "lo")
        out_all = out_all.astype(f32)

    return (
        output,
        grad_tokens,
        sums[0],
        sums[1],
        qkv_all,
        out_all,
        sums[2],
        sums[3],
        up_all,
        down_all,
    )


def solution(mesh):
    seq, fsdp = mesh.shape["seq"], mesh.shape["fsdp"]
    group, depth = seq // 2, fsdp // 2
    fine = Mesh(mesh.devices.reshape(2, group, depth, 2), ("hi", "lo", "fz", "fx"))
    s, f = ("hi", "lo"), ("fz", "fx")
    return jax.shard_map(
        functools.partial(body, group, depth),
        mesh=fine,
        in_specs=(
            P(None, f, s, None),
            P(None, f, None),
            P(f),
            P(f),
            P(f, None),
            P(f, None),
            P(f),
            P(f),
            P(f, None),
            P(f, None),
            P(None, f, s, None),
        ),
        out_specs=(
            P(None, f, s, None),
            P(None, f, s, None),
            P(f),
            P(f),
            P(f, None),
            P(f, None),
            P(f),
            P(f),
            P(f, None),
            P(f, None),
        ),
        check_vma=False,
    )
```

```python
import functools
import math

import jax
import jax.numpy as jnp
from jax import lax
from jax.experimental import pallas as pl
from jax.experimental.pallas import tpu as pltpu
from jax.sharding import Mesh
from jax.sharding import PartitionSpec as P

HEAD_DIM = 64
DOC_MOST = 512
TILE = 256
LANES = 128
VMEM = 26 * 1024 * 1024
epsilon = 1e-05
SWAP = [(0, 1), (1, 0)]
f32 = jnp.float32
bf16 = jnp.bfloat16


def dot(left, right, dims):
    return lax.dot_general(left, right, (dims, ((), ())), preferred_element_type=f32)


def mm(left, right):
    return dot(left, right, ((1,), (0,)))


def mm_rows(left, right):
    return dot(left, right, ((0,), (0,)))


def mm_cols(left, right):
    return dot(left, right, ((1,), (1,)))


def cost(micros):
    return pl.CostEstimate(flops=int(micros * 1.1e9), bytes_accessed=1000, transcendentals=0)


def far(array):
    return pltpu.with_memory_space_constraint(array, pltpu.HBM)


def sync(*values):
    return lax.optimization_barrier(values)


def pick(array, index, axis):
    return lax.dynamic_index_in_dim(array, index, axis, keepdims=False)


def swap(value, axis):
    return lax.ppermute(value, axis, SWAP)


def ordered(own, other, index, axis):
    first = jnp.where(index == 0, own, other)
    second = jnp.where(index == 0, other, own)
    return jnp.stack([first, second], axis)


def tile_spans(rows):
    tile = min(TILE, rows)
    spans = []
    for start in range(0, rows, tile):
        low = max(0, (start - DOC_MOST + 1) // tile * tile)
        spans.append((start, low, start + tile))
    return tile, spans


def fill_bias(bias, seg_col, seg_row, spans, tile):
    for i, (start, low, high) in enumerate(spans):
        width = high - low
        query_pos = start + lax.broadcasted_iota(jnp.int32, (tile, width), 0)
        key_pos = low + lax.broadcasted_iota(jnp.int32, (tile, width), 1)
        same = seg_col[start : start + tile, :] == seg_row[:, low:high]
        allowed = (key_pos <= query_pos) & same
        bias[i, :, :width] = jnp.where(allowed, 0.0, -1e30).astype(f32)


def pipelined(count, first, second, third, lead=1):
    ready, waiting = [first(block) for block in range(min(lead, count))], None
    for block in range(count):
        if block + lead < count:
            ready.append(first(block + lead))
        current = ready.pop(0)
        middle = second(block, current)
        if waiting is not None:
            third(*waiting)
        waiting = (block, current, middle)
    third(*waiting)


def own_half(left, head, rows):
    return jnp.where(left if head == 0 else ~left, rows, jnp.zeros_like(rows))


def attend_kernel(spans, tile, q_ref, k_ref, v_ref, seg_col, seg_row, out_ref, lse_ref, bias):
    @pl.when(pl.program_id(0) == 0)
    def _():
        fill_bias(bias, seg_col, seg_row, spans, tile)

    left = lax.broadcasted_iota(jnp.int32, (tile, LANES), 1) < HEAD_DIM
    done = {}

    def scores(block):
        (start, low, high), head = spans[block // 2], block % 2
        return mm_cols(own_half(left, head, q_ref[start : start + tile, :]), k_ref[low:high, :])

    def softmax(block, values):
        _, low, high = spans[block // 2]
        values = values + bias[block // 2, :, : high - low]
        top = jnp.max(values, axis=-1, keepdims=True)
        powers = jnp.exp(values - top)
        total = jnp.sum(powers, axis=-1, keepdims=True)
        return powers.astype(bf16), total, top + jnp.log(total)

    def mix(block, _, held):
        (start, low, high), head = spans[block // 2], block % 2
        powers, total, logs = held
        done[head] = mm(powers, v_ref[low:high, :]) * (1.0 / total), logs
        if head == 1:
            rows = slice(start, start + tile)
            out_ref[rows, :] = jnp.where(left, done[0][0], done[1][0]).astype(bf16)
            lse_ref[rows, :] = jnp.where(left, done[0][1], done[1][1])

    pipelined(2 * len(spans), scores, softmax, mix)


def attend(joint, seg_col, seg_row, begin, count):
    rows, width = joint.shape[0], joint.shape[1] // 3
    pairs = width // LANES
    tile, spans = tile_spans(rows)
    widest = max(high - low for _, low, high in spans)

    def part(which):
        return pl.BlockSpec((rows, LANES), lambda p: (0, which * pairs + begin + p))

    out = pl.BlockSpec((rows, LANES), lambda p: (0, p))
    return pl.pallas_call(
        functools.partial(attend_kernel, spans, tile),
        grid=(count,),
        in_specs=[
            part(0),
            part(1),
            part(2),
            pl.BlockSpec((rows, 1), lambda p: (0, 0)),
            pl.BlockSpec((1, rows), lambda p: (0, 0)),
        ],
        out_specs=[out, out],
        out_shape=[
            jax.ShapeDtypeStruct((rows, count * LANES), bf16),
            pltpu.HBM((rows, count * LANES), f32),
        ],
        scratch_shapes=[pltpu.VMEM((len(spans), tile, widest), f32)],
        compiler_params=pltpu.CompilerParams(vmem_limit_bytes=VMEM),
        cost_estimate=cost(4 * count),
        name="attend",
    )(far(joint), far(joint), far(joint), seg_col, seg_row)


def attend_back_kernel(
    spans, tile, q_ref, k_ref, v_ref, g_ref, lse_ref, seg_col, seg_row, out_ref, bias, keys_sum, values_sum
):
    @pl.when(pl.program_id(0) == 0)
    def _():
        fill_bias(bias, seg_col, seg_row, spans, tile)

    keys_sum[...] = jnp.zeros_like(keys_sum)
    values_sum[...] = jnp.zeros_like(values_sum)
    left = lax.broadcasted_iota(jnp.int32, (tile, LANES), 1) < HEAD_DIM
    done = {}

    def products(block):
        (start, low, high), head = spans[block // 2], block % 2
        rows = slice(start, start + tile)
        queries, grads = own_half(left, head, q_ref[rows, :]), own_half(left, head, g_ref[rows, :])
        return queries, grads, mm_cols(queries, k_ref[low:high, :]), mm_cols(grads, v_ref[low:high, :])

    def softmax_back(block, held):
        (start, low, high), lane = spans[block // 2], block % 2 * HEAD_DIM
        _, _, scores, grad_probs = held
        logs = lse_ref[start : start + tile, lane : lane + 1]
        probs = jnp.exp(scores + bias[block // 2, :, : high - low] - logs)
        both = probs * grad_probs
        inner = jnp.sum(both, axis=-1, keepdims=True)
        return (both - probs * inner).astype(bf16), probs.astype(bf16)

    def gather_up(block, held, middle):
        (start, low, high), head = spans[block // 2], block % 2
        queries, grads, _, _ = held
        grad_scores, probs = middle
        done[head] = mm(grad_scores, k_ref[low:high, :])
        keys_sum[low:high, :] += mm_rows(grad_scores, queries)
        values_sum[low:high, :] += mm_rows(probs, grads)
        if head == 1:
            grad_queries = jnp.where(left, done[0], done[1]).astype(bf16)
            out_ref[0, start : start + tile, :] = grad_queries * jnp.asarray(1.0 / math.sqrt(HEAD_DIM), bf16)

    pipelined(2 * len(spans), products, softmax_back, gather_up, lead=2)
    out_ref[1] = keys_sum[...].astype(bf16)
    out_ref[2] = values_sum[...].astype(bf16)


def attend_back(joint, grads, lse, seg_col, seg_row, begin, count):
    rows, width = joint.shape[0], joint.shape[1] // 3
    pairs = width // LANES
    tile, spans = tile_spans(rows)
    widest = max(high - low for _, low, high in spans)

    def part(which):
        return pl.BlockSpec((rows, LANES), lambda p: (0, which * pairs + begin + p))

    return pl.pallas_call(
        functools.partial(attend_back_kernel, spans, tile),
        grid=(count,),
        in_specs=[
            part(0),
            part(1),
            part(2),
            part(0),
            pl.BlockSpec((rows, LANES), lambda p: (0, p)),
            pl.BlockSpec((rows, 1), lambda p: (0, 0)),
            pl.BlockSpec((1, rows), lambda p: (0, 0)),
        ],
        out_specs=pl.BlockSpec((3, rows, LANES), lambda p: (0, 0, p)),
        out_shape=jax.ShapeDtypeStruct((3, rows, count * LANES), bf16),
        scratch_shapes=[
            pltpu.VMEM((len(spans), tile, widest), f32),
            pltpu.VMEM((rows, LANES), f32),
            pltpu.VMEM((rows, LANES), f32),
        ],
        compiler_params=pltpu.CompilerParams(vmem_limit_bytes=VMEM),
        cost_estimate=cost(0.5 * count),
        name="attend_back",
    )(far(joint), far(joint), far(joint), grads, far(lse), seg_col, seg_row)


def shape_of(*shape, dtype=bf16):
    return jax.ShapeDtypeStruct(shape, dtype)


def far_shape(*shape, dtype=bf16):
    return pltpu.HBM(shape, dtype)


def along(value, axis, depth, step):
    return lax.ppermute(value, axis, [(i, (i + step) % depth) for i in range(depth)])


def load(depth, place, pieces, sems, targets, base=0, sem=0):
    z, x, h = place[0], place[1], place[2]
    copies = []

    def put(source, shard, half, at, shift=0):
        for first, columns, where in targets:
            taken = source
            if columns != source.shape[1]:
                taken = source.at[:, shift + first : shift + first + columns]
            copies.append(pltpu.make_async_copy(taken, where(shard, half, at, source.shape[0]), sems.at[sem + len(copies)]))
            copies[-1].start()

    own, side_own, far, side, near, last_side, last_near = pieces
    quarter = last_side.shape[1]
    for at_x, piece in ((x, own), (1 - x, side_own)):
        for half in range(2):
            put(piece.at[half], z * 2 + at_x, half, 0, base)
    for at_x, at_h, at, piece in (
        (x, h, 0, far),
        (1 - x, h, 0, side),
        (x, 1 - h, 0, near),
        (1 - x, 1 - h, 0, last_side),
        (1 - x, 1 - h, quarter, last_near),
    ):
        for k in range(1, depth):
            put(piece.at[k - 1], lax.rem(z - k + depth, depth) * 2 + at_x, at_h, at)
    return copies


def below(weight, half_rows):
    def where(shard, half, at, count):
        first = pl.multiple_of((shard * 2 + half) * half_rows + at, math.gcd(half_rows, at))
        return weight.at[pl.ds(first, count), :]

    return where


def halve(side, near):
    count, rows, columns = side.shape
    half = rows // 2

    def kernel(side_ref, near_ref, one_ref, two_ref):
        one_ref[...] = side_ref[:, :half, :]
        two_ref[...] = near_ref[:, half:, :]

    return pl.pallas_call(
        kernel,
        in_specs=[pl.BlockSpec(memory_space=pltpu.VMEM)] * 2,
        out_specs=[pl.BlockSpec(memory_space=pltpu.VMEM)] * 2,
        out_shape=[shape_of(count, half, columns)] * 2,
        compiler_params=pltpu.CompilerParams(vmem_limit_bytes=VMEM),
        cost_estimate=cost(1),
        name="halve",
    )(far(side), far(near))


def prepare(place, shards, w_qkv, w_out, w_up, vectors):
    rows, model = w_out.shape
    half, blocks = rows // 2, w_qkv.shape[1] // LANES
    qkv_columns, wide = w_qkv.shape[1] // 2, w_up.shape[1] // 2
    scale_at = qkv_columns
    out_at = scale_at + LANES
    up_at = out_at + model // 2
    unit = wide // shards

    def kernel(place_ref, qkv_ref, out_ref, up_ref, vectors_ref, own_ref, first_ref, up_half_ref):
        lo, h = place_ref[3], place_ref[2]
        left = lax.broadcasted_iota(jnp.int32, (rows, LANES), 1) < HEAD_DIM

        def put(at, value):
            own_ref[0, :, at : at + value.shape[1]] = value[:half]
            own_ref[1, :, at : at + value.shape[1]] = value[half:]

        for block in range(0, blocks, 2):
            one = qkv_ref[:, block * LANES : (block + 1) * LANES].astype(f32)
            two = qkv_ref[:, (block + 1) * LANES : (block + 2) * LANES].astype(f32)
            even = jnp.where(left, one, pltpu.roll(two, HEAD_DIM, 1))
            odd = jnp.where(left, pltpu.roll(one, HEAD_DIM, 1), two)
            put(block // 2 * LANES, jnp.where(lo == 0, even, odd).astype(bf16))
        columns = jnp.concatenate([vectors_ref[...].astype(f32), jnp.zeros((LANES - 4, rows), f32)], axis=0)
        put(scale_at, columns.T.astype(bf16))
        outs = jnp.where(lo == 0, out_ref[:half, :], out_ref[half:, :])
        put(out_at, jnp.concatenate([outs[:, : model // 2], outs[:, model // 2 :]], axis=0))
        for shard in range(shards):
            at = shard * 2 * unit
            put(up_at + shard * unit, jnp.where(lo == 0, up_ref[:, at : at + unit], up_ref[:, at + unit : at + 2 * unit]))
        first_ref[...] = own_ref[h, :, :up_at]
        up_half_ref[...] = own_ref[h, :, up_at:]

    return pl.pallas_call(
        kernel,
        in_specs=[pl.BlockSpec(memory_space=pltpu.SMEM)] + [pl.BlockSpec(memory_space=pltpu.VMEM)] * 4,
        out_specs=[pl.BlockSpec(memory_space=pltpu.VMEM)] * 3,
        out_shape=[shape_of(2, half, up_at + wide), shape_of(half, up_at), shape_of(half, wide)],
        compiler_params=pltpu.CompilerParams(vmem_limit_bytes=VMEM),
        cost_estimate=cost(2),
        name="prepare",
    )(place, far(w_qkv), far(w_out), far(w_up), vectors)


def finish_up(place, shards, own, other):
    rows, columns = own.shape
    unit = columns // shards

    def kernel(place_ref, own_ref, other_ref, out_ref):
        lo = place_ref[3]
        for shard in range(shards):
            at, mine, theirs = shard * 2 * unit, own_ref, other_ref
            one = mine[:, shard * unit : (shard + 1) * unit].astype(f32)
            two = theirs[:, shard * unit : (shard + 1) * unit].astype(f32)
            out_ref[:, at : at + unit] = jnp.where(lo == 0, one, two)
            out_ref[:, at + unit : at + 2 * unit] = jnp.where(lo == 0, two, one)

    return pl.pallas_call(
        kernel,
        in_specs=[pl.BlockSpec(memory_space=pltpu.SMEM)] + [pl.BlockSpec(memory_space=pltpu.VMEM)] * 2,
        out_specs=pl.BlockSpec(memory_space=pltpu.VMEM),
        out_shape=shape_of(rows, 2 * columns, dtype=f32),
        cost_estimate=cost(2),
        name="finish_up",
    )(place, own, other)


def finish_qkv(place, columns, owns, others):
    rows = owns[0].shape[0]
    half, pieces = rows // 2, len(owns)
    third = columns // 3
    model = 2 * (owns[0].shape[1] - columns - LANES)

    def kernel(place_ref, *refs):
        lo = place_ref[3]
        owns_refs, others_refs = refs[:pieces], refs[pieces : 2 * pieces]
        qkv_ref, out_ref, sums_ref = refs[2 * pieces :]
        left = lax.broadcasted_iota(jnp.int32, (rows, LANES), 1) < HEAD_DIM
        at = 0
        for j in range(3):
            for own_ref, other_ref in zip(owns_refs, others_refs):
                for first in range(j * third, (j + 1) * third, LANES):
                    mine = own_ref[:, first : first + LANES].astype(f32)
                    theirs = other_ref[:, first : first + LANES].astype(f32)
                    one, two = jnp.where(lo == 0, mine, theirs), jnp.where(lo == 0, theirs, mine)
                    qkv_ref[:, at : at + LANES] = jnp.where(left, one, pltpu.roll(two, HEAD_DIM, 1))
                    qkv_ref[:, at + LANES : at + 2 * LANES] = jnp.where(left, pltpu.roll(one, HEAD_DIM, 1), two)
                    at += 2 * LANES
        sums = jnp.zeros((rows, LANES), f32)
        for ref in refs[: 2 * pieces]:
            sums = sums + ref[:, columns : columns + LANES].astype(f32)
        sums_ref[...] = sums.T[:8, :]
        mine, theirs = (ref[:, columns + LANES :].astype(f32) for ref in (owns_refs[0], others_refs[0]))
        for at, value in ((0, jnp.where(lo == 0, mine, theirs)), (half, jnp.where(lo == 0, theirs, mine))):
            out_ref[at : at + half, : model // 2] = value[:half]
            out_ref[at : at + half, model // 2 :] = value[half:]

    return pl.pallas_call(
        kernel,
        in_specs=[pl.BlockSpec(memory_space=pltpu.SMEM)] + [pl.BlockSpec(memory_space=pltpu.VMEM)] * (2 * pieces),
        out_specs=[pl.BlockSpec(memory_space=pltpu.VMEM)] * 3,
        out_shape=[
            shape_of(rows, 2 * pieces * columns, dtype=f32),
            shape_of(rows, model, dtype=f32),
            shape_of(8, rows, dtype=f32),
        ],
        compiler_params=pltpu.CompilerParams(vmem_limit_bytes=VMEM),
        cost_estimate=cost(2),
        name="finish_qkv",
    )(place, *owns, *others)


def plus(left, right):
    return (left.astype(f32) + right.astype(f32)).astype(bf16)


def fold_one(place, keep, came, shape=shape_of):
    depth, top, columns = keep[0].shape
    low = top // 2

    def kernel(place_ref, keep_one, keep_two, came_one, came_two, kept_ref, send_one, send_two):
        at_x, at_h = place_ref[1] == 0, place_ref[2] == 0
        one, two = plus(keep_one[0], came_one[0]), plus(keep_two[0], came_two[0])
        kept_ref[0, 0] = jnp.where(at_h, one[:low], one[low:])
        send_one[0] = jnp.where(at_h, one[low:], one[:low])
        kept_ref[1, 0] = jnp.where(at_x, two[0], two[1])
        send_two[0] = jnp.where(at_x, two[1], two[0])

    one = pl.BlockSpec((1, top, columns), lambda i: (i, 0, 0))
    two = pl.BlockSpec((1, 2, low, columns), lambda i: (i, 0, 0, 0))
    send = pl.BlockSpec((1, low, columns), lambda i: (i, 0, 0))
    kept, *sends = pl.pallas_call(
        kernel,
        grid=(depth,),
        in_specs=[pl.BlockSpec(memory_space=pltpu.SMEM), one, two, one, two],
        out_specs=[pl.BlockSpec((2, 1, low, columns), lambda i: (0, i, 0, 0)), send, send],
        out_shape=[shape(2, depth, low, columns)] + [shape(depth, low, columns)] * 2,
        compiler_params=pltpu.CompilerParams(vmem_limit_bytes=VMEM),
        cost_estimate=cost(1),
        name="fold_one",
    )(place, *keep, *came)
    return kept, sends


def fold_two(place, kept, came):
    _, depth, low, columns = kept.shape

    def kernel(place_ref, kept_ref, came_one, came_two, *refs):
        *outs, sums = refs
        for half, came_ref in enumerate((came_one, came_two)):
            for at in range(depth):
                sums[at, half] = plus(kept_ref[half, at], came_ref[at])
        for k, out in enumerate(outs):
            out[...] = sums[lax.rem(place_ref[0] + k, depth)]

    own, *sends = pl.pallas_call(
        kernel,
        in_specs=[pl.BlockSpec(memory_space=pltpu.SMEM)] + [pl.BlockSpec(memory_space=pltpu.VMEM)] * 3,
        out_specs=[pl.BlockSpec(memory_space=pltpu.VMEM)] * depth,
        out_shape=[shape_of(2, low, columns)] * depth,
        scratch_shapes=[pltpu.VMEM((depth, 2, low, columns), bf16)],
        compiler_params=pltpu.CompilerParams(vmem_limit_bytes=VMEM),
        cost_estimate=cost(1),
        name="fold_two",
    )(place, kept, *came)
    return own, sends


def add_up(own, came):
    total = own.astype(f32)
    for piece in came:
        total = total + piece.astype(f32)
    return total.astype(bf16)


def row_block(tile, width):
    return pl.BlockSpec((tile, width), lambda i: (i, 0))


def whole_block(*shape):
    return pl.BlockSpec(shape, lambda i: (0,) * len(shape))


def weight_call(name, step, tiles, place, inputs, sets, outs, scratch, copies, micros):
    pieces = [piece for held in sets for piece in held]

    def kernel(place_ref, *refs):
        refs = list(refs)

        def take(count):
            taken = refs[:count]
            del refs[:count]
            return taken

        given = take(len(inputs))
        held = [take(len(one)) for one in sets]
        made = take(len(outs))
        step(place_ref, given, held, made, refs[:-1], refs[-1])

    return pl.pallas_call(
        kernel,
        grid=(tiles,),
        in_specs=[pl.BlockSpec(memory_space=pltpu.SMEM)]
        + [spec for _, spec in inputs]
        + [pl.BlockSpec(memory_space=pltpu.HBM)] * len(pieces),
        out_specs=[spec for _, spec in outs],
        out_shape=[shape for shape, _ in outs],
        scratch_shapes=list(scratch) + [pltpu.SemaphoreType.DMA((copies,))],
        compiler_params=pltpu.CompilerParams(vmem_limit_bytes=VMEM),
        cost_estimate=cost(micros),
        name=name,
    )(place, *[v for v, _ in inputs], *[far(piece) for piece in pieces])


def unit_of(values):
    centred = values - jnp.mean(values, axis=-1, keepdims=True)
    variance = jnp.mean(centred * centred, axis=-1, keepdims=True)
    inverse = lax.rsqrt(variance + epsilon)
    return centred * inverse, inverse


def unit_back(grad_unit, unit_rows, inverse):
    mean_grad = jnp.mean(grad_unit, axis=-1, keepdims=True)
    mean_cross = jnp.mean(grad_unit * unit_rows, axis=-1, keepdims=True)
    return inverse * (grad_unit - mean_grad - unit_rows * mean_cross)


def bell_and_slope(values):
    phi = 0.5 + 0.5 * lax.erf(values * math.sqrt(0.5))
    density = jnp.exp(values * values * -0.5) * (1.0 / math.sqrt(2.0 * math.pi))
    return values * phi, phi + values * density


def outer_whole(left, right):
    rows, across = left.shape
    block = min(256, across)

    def kernel(left_ref, right_ref, out_ref):
        out_ref[...] = mm_rows(left_ref[...], right_ref[...]).astype(bf16)

    return pl.pallas_call(
        kernel,
        grid=(across // block,),
        in_specs=[pl.BlockSpec((rows, block), lambda i: (0, i)), whole_block(*right.shape)],
        out_specs=row_block(block, right.shape[1]),
        out_shape=shape_of(across, right.shape[1]),
        compiler_params=pltpu.CompilerParams(vmem_limit_bytes=VMEM),
        cost_estimate=cost(7),
        name="outer_whole",
    )(left, right)


def outer(place, depth, left, right, out_pair=None, weight=None, scales=None, piece=0, sums=None):
    rows, own_rows = left.shape[0], left.shape[1] // (2 * depth)
    top, low = own_rows // 2, own_rows // 4
    parts = right.shape[0] if right.ndim == 3 else 1
    third = right.shape[-1]
    columns = parts * third
    given = [left, right]
    specs = [pl.BlockSpec((rows, 2 * own_rows), lambda i: (0, i)), whole_block(*right.shape)]
    total = columns
    if weight is not None:
        given += [weight, scales, sums]
        specs += [pl.BlockSpec((2 * own_rows, part.shape[1]), lambda i: (i, 0)) for part in (weight, scales)]
        specs.append(pl.BlockSpec((8, 2 * own_rows), lambda i: (0, i)))
        total += LANES
        width = weight.shape[1] // 3
    if out_pair is not None:
        out_block = out_pair[0].shape[1] // depth
        given += out_pair
        specs += [pl.BlockSpec((rows, out_block), lambda i: (0, i)), whole_block(*out_pair[1].shape)]
        half = out_pair[1].shape[1] // 2
        total += half

    def kernel(place_ref, *refs):
        ins, outs = list(refs[: len(given)]), refs[len(given) :]
        at_x, at_h = place_ref[1] == 0, place_ref[2] == 0
        keep_first, send_first, keep_second, send_second = outs

        def put(first, value):
            where = slice(first, first + value.shape[2])
            heads = value[:, :top].astype(bf16)
            keep_first[0, :, where] = jnp.where(at_x, heads[0], heads[1])
            send_first[0, :, where] = jnp.where(at_x, heads[1], heads[0])
            lower, upper = value[:, top : top + low].astype(bf16), value[:, top + low :].astype(bf16)
            keep_second[0, :, :, where] = jnp.where(at_h, lower, upper)
            send_second[0, :, :, where] = jnp.where(at_h, upper, lower)

        left_ref, right_ref = ins.pop(0), ins.pop(0)
        rights = [right_ref.at[j] for j in range(parts)] if parts > 1 else [right_ref]
        products = [mm_rows(left_ref[...], ref[...]) for ref in rights]
        for j, product in enumerate(products):
            put(j * third, product.reshape(2, own_rows, third))
        first = columns
        if weight is not None:
            weight_ref, scales_ref, sums_ref = ins.pop(0), ins.pop(0), ins.pop(0)
            bias_sum = cross = 0.0
            for j, product in enumerate(products):
                at = j * width + piece * third
                part = weight_ref[:, at : at + third].astype(f32)
                column_sums = jnp.sum(rights[j][...].astype(f32), axis=0, keepdims=True)
                bias_sum = bias_sum + jnp.sum(part * column_sums, axis=1, keepdims=True)
                cross = cross + jnp.sum(part * product, axis=1, keepdims=True)
            gain, bias = scales_ref[:, 0:1].astype(f32), scales_ref[:, 1:2].astype(f32)
            gain_sum = (cross - bias * bias_sum) / gain
            kept = jnp.concatenate(
                [jnp.zeros((2, 2 * own_rows), f32), sums_ref[0:2, :], jnp.zeros((LANES - 4, 2 * own_rows), f32)], axis=0
            ).T
            lane = lax.broadcasted_iota(jnp.int32, kept.shape, 1)
            kept = jnp.where(lane == 0, gain_sum, jnp.where(lane == 1, bias_sum, kept))
            put(first, kept.reshape(2, own_rows, LANES))
            first += LANES
        if out_pair is not None:
            product = mm_rows(ins.pop(0)[...], ins.pop(0)[...]).reshape(2, top, 2 * half)
            put(first, jnp.concatenate([product[:, :, :half], product[:, :, half:]], axis=1))

    def spec(*block):
        return pl.BlockSpec((1, *block), lambda i: (i,) + (0,) * len(block))

    first_shape, second_shape = (top, total), (2, low, total)
    made = pl.pallas_call(
        kernel,
        grid=(depth,),
        in_specs=[pl.BlockSpec(memory_space=pltpu.SMEM)] + specs,
        out_specs=[spec(*first_shape)] * 2 + [spec(*second_shape)] * 2,
        out_shape=[shape_of(depth, *first_shape)] * 2 + [shape_of(depth, *second_shape)] * 2,
        compiler_params=pltpu.CompilerParams(vmem_limit_bytes=VMEM),
        cost_estimate=cost(6),
        name="outer",
    )(place, *given)
    return (made[0], made[2]), (made[1], made[3])


def body(
    group,
    depth,
    tokens,
    segment_ids,
    norm1_gain,
    norm1_bias,
    w_qkv,
    w_out,
    norm2_gain,
    norm2_bias,
    w_up,
    w_down,
    cotangent,
):
    h, lo = lax.axis_index("hi"), lax.axis_index("lo")
    z, x = lax.axis_index("fz"), lax.axis_index("fx")
    micro, _, chunk, model = tokens.shape
    shards = 2 * depth
    rows = micro * group * chunk
    own_rows = w_out.shape[0]
    inner = w_up.shape[1] // group
    split_out = (own_rows // HEAD_DIM) % group == 0
    head_columns = model // group
    half_rows = own_rows // 2
    tile = min(TILE, rows)
    tiles = rows // tile
    scale_at = 3 * head_columns
    copies = 4 * shards
    wide = min(512, inner)
    shard_axes = ("fz", "fx")

    rest = range(1, depth)

    def whole_group(value, axis):
        if group == 2:
            return ordered(value, swap(value, "lo"), lo, axis)
        return lax.all_gather(value, "lo", axis=axis)

    def other_part(partial):
        if group == 2:
            return swap(partial, "lo")
        return (lax.psum(partial, "lo").astype(f32) - partial.astype(f32)).astype(bf16)

    def own_chunks(full):
        return pick(full.reshape(micro, group, chunk, -1), lo, 1)

    def other_own(partial):
        parts = partial.reshape(micro, group, chunk, model)
        if group == 2:
            return swap(pick(parts, 1 - lo, 1), "lo")
        return plus(lax.psum_scatter(parts, "lo", scatter_dimension=1), -pick(parts, lo, 1))

    def hop(values, parity):
        return [along(value, "fz", depth, k) for k, value in zip(rest, values) if k % 2 == parity]

    fused_out = split_out and group == 2
    out_rows, half_model = own_rows // group, model // 2
    place = jnp.stack([z, x, h, lo]).astype(jnp.int32)
    came = swap(jnp.stack([pick(tokens[:, 0], 1 - h, 0), pick(cotangent[:, 0], 1 - h, 0)]), "hi")
    vectors = jnp.stack([norm1_gain, norm1_bias, norm2_gain, norm2_bias])
    if fused_out:
        both_own, first_half, up_half = prepare(place, shards, w_qkv, w_out, w_up, vectors)
    else:
        if split_out:
            qkv_part = pick(w_qkv.reshape(own_rows, 3, shards, group, -1), lo, 3).reshape(own_rows, -1)
            out_part = pick(w_out.reshape(group, out_rows, model), lo, 0)
        else:
            qkv_part = pick(w_qkv.reshape(own_rows, 3, group, -1), lo, 2).reshape(own_rows, -1)
            out_part = w_out
        up_part = pick(w_up.reshape(own_rows, shards, group, -1), lo, 2).reshape(own_rows, -1)
        parts = [qkv_part, jnp.pad(vectors.T, ((0, 0), (0, LANES - 4)))]
        both_own = jnp.concatenate(parts + [up_part], axis=1).reshape(2, half_rows, -1)
        half = pick(both_own, h, 0)
        first_half, up_half = half[:, : scale_at + LANES], half[:, scale_at + LANES :]
        out_weight = lax.all_gather(out_part, shard_axes, axis=0, tiled=True)
    up_at = first_half.shape[1]
    down_rows = inner // shards
    fine_down = down_rows % 64 == 0
    down_part = pick(w_down.reshape(group, 2, down_rows // 2, model), lo, 0)
    first_far = [along(first_half, "fz", depth, k) for k in rest]
    side_own = swap(both_own, "fx")
    first_far, side_own, came, up_half = sync(first_far, side_own, came, up_half)

    def last_quarters(side_part, near_part):
        return swap(side_part, "hi"), swap(near_part, "fx")

    first_far = jnp.stack(first_far)
    first_side, first_near = swap(first_far, "fx"), swap(first_far, "hi")
    up_far = [along(up_half, "fz", depth, k) for k in rest]
    first_side, first_near, up_far, came, down_part = sync(first_side, first_near, up_far, came, down_part)

    cuts, came, tokens, up_far = sync(halve(first_side, first_near), came, tokens, up_far)
    first_last = last_quarters(*cuts)
    down_half = pick(down_part, h, 0)
    if not fine_down:
        downward = lax.all_gather(down_part.reshape(down_rows, model), shard_axes, axis=0, tiled=True)
    inputs = whole_group(ordered(pick(tokens[:, 0], h, 0), came[0], h, 0), 1).reshape(rows, model)
    up_far = jnp.stack(up_far)
    first_last, inputs, up_far, came, down_half, down_part = sync(
        first_last, inputs, up_far, came, down_half, down_part
    )
    first_set = [both_own, side_own, first_far, first_side, first_near, *first_last]

    segments = pick(segment_ids[:, 0], h, 0)
    seg_col, seg_row = segments[:, None], segments[None, :]

    def project(place_ref, given, held, made, scratch, sems):
        (rows_ref,), (normed_ref, joint_ref, scales_ref, weight, columns, *outs) = given, made

        @pl.when(pl.program_id(0) == 0)
        def _():
            targets = [
                (0, 3 * head_columns, below(weight, half_rows)),
                (scale_at, LANES, below(columns, half_rows)),
            ]
            if fused_out:
                targets.append((scale_at + LANES, half_model, below(scratch[0], half_rows)))
            for copy in load(depth, place_ref, held[0], sems, targets):
                copy.wait()
            scales_ref[...] = columns[...].astype(f32).T[:8, :]
            for shard in range(shards if fused_out else 0):
                for part in range(2):
                    at = shard * own_rows + part * out_rows
                    outs[0][
                        shard * out_rows : (shard + 1) * out_rows, part * half_model : (part + 1) * half_model
                    ] = scratch[0][at : at + out_rows, :]

        unit_rows, _ = unit_of(rows_ref[...].astype(f32))
        normed = (unit_rows * scales_ref[0:1, :] + scales_ref[1:2, :]).astype(bf16)
        normed_ref[...] = normed
        for at in range(0, 3 * head_columns, head_columns):
            part = mm(normed, weight[:, at : at + head_columns])
            if at == 0:
                part = part * (1.0 / math.sqrt(HEAD_DIM))
            joint_ref[:, at : at + head_columns] = part.astype(bf16)

    wholes = [(8, model, f32), (model, 3 * head_columns, bf16), (model, LANES, bf16)]
    if fused_out:
        wholes.append((head_columns, model, bf16))
    normed, joint, scales, joint_weight, scale_columns, *outs = weight_call(
        "project",
        project,
        tiles,
        place,
        [(inputs, row_block(tile, model))],
        [first_set],
        [
            (far_shape(rows, model), row_block(tile, model)),
            (far_shape(rows, 3 * head_columns), row_block(tile, 3 * head_columns)),
        ]
        + [(far_shape(*shape, dtype=dtype), whole_block(*shape)) for *shape, dtype in wholes],
        [pltpu.VMEM((model, half_model), bf16)] if fused_out else [],
        3 * copies,
        8,
    )
    if fused_out:
        (out_weight,) = outs
    pairs = head_columns // LANES
    pieces = 2 if pairs % 2 == 0 else 1
    count = pairs // pieces
    part_columns = count * LANES
    mixed = [attend(joint, seg_col, seg_row, 0, count)]
    up_side, up_near = swap(up_far, "fx"), swap(up_far, "hi")
    down_odd = down_even = down_side_own = None
    if fine_down:
        down_odd = [along(down_half, "fz", depth, k) for k in rest if k % 2]
        down_side_own = swap(down_part, "fx")
    mixed, joint, up_side, up_near, scales, out_weight, came, down_odd, down_side_own, down_half = sync(
        mixed, joint, up_side, up_near, scales, out_weight, came, down_odd, down_side_own, down_half
    )

    cuts, joint, came, down_half = sync(halve(up_side, up_near), joint, came, down_half)
    up_last = last_quarters(*cuts)
    for piece in range(1, pieces):
        mixed.append(attend(joint, seg_col, seg_row, piece * count, count))
    grad_result = whole_group(ordered(pick(cotangent[:, 0], h, 0), came[1], h, 0), 1).reshape(rows, model)
    if fine_down:
        down_even = [along(down_half, "fz", depth, k) for k in rest if k % 2 == 0]
    mixed, up_last, out_weight, grad_result, down_even = sync(mixed, up_last, out_weight, grad_result, down_even)
    up_set = [both_own, side_own, up_far, up_side, up_near, *up_last]
    lse = mixed[0][1] if pieces == 1 else jnp.concatenate([part for _, part in mixed], axis=1)

    def leave(place_ref, given, held, made, scratch, sems):
        *parts_refs, weight = given
        out_ref, attended_ref = made
        weight = own_out(weight, place_ref)
        total = jnp.zeros(out_ref.shape, f32)
        for piece, part_ref in enumerate(parts_refs):
            at = slice(piece * part_columns, (piece + 1) * part_columns)
            attended_ref[:, at] = part_ref[...]
            total = total + mm(part_ref[...], weight[at, :])
        out_ref[...] = total.astype(bf16)

    def own_out(weight, place_ref):
        if split_out:
            return weight[...]
        return weight[pl.ds(pl.multiple_of(place_ref[3] * head_columns, head_columns), head_columns), :]

    branch, attended = weight_call(
        "leave",
        leave,
        tiles,
        place,
        [(value, row_block(tile, part_columns)) for value, _ in mixed]
        + [(out_weight, whole_block(*out_weight.shape))],
        [],
        [
            (shape_of(rows, model), row_block(tile, model)),
            (far_shape(rows, head_columns), row_block(tile, head_columns)),
        ],
        [],
        1,
        3,
    )
    branch_other = other_part(branch)

    if fine_down:
        down_far = jnp.stack([down_odd[k // 2] if k % 2 else down_even[k // 2 - 1] for k in rest])
        down_side, down_near = swap(down_far, "fx"), swap(down_far, "hi")

    def widen(place_ref, given, held, made, scratch, sems):
        rows_ref, own_ref, other_ref, scales_ref = given
        middle_ref, normed_ref, hidden_ref, slope_ref = made
        (weight,) = scratch

        @pl.when(pl.program_id(0) == 0)
        def _():
            targets = [(0, inner, below(weight, half_rows))]
            for copy in load(depth, place_ref, held[0], sems, targets, up_at):
                copy.wait()

        added = own_ref[...].astype(f32) + other_ref[...].astype(f32)
        middle = rows_ref[...].astype(f32) + added
        middle_ref[...] = middle.astype(bf16)
        unit_rows, _ = unit_of(middle)
        normed = (unit_rows * scales_ref[2:3, :] + scales_ref[3:4, :]).astype(bf16)
        normed_ref[...] = normed
        for at in range(0, inner, wide):
            hidden, slope = bell_and_slope(mm(normed, weight[:, at : at + wide]))
            hidden_ref[:, at : at + wide] = hidden.astype(bf16)
            slope_ref[:, at : at + wide] = slope.astype(bf16)

    middle, normed_two, hidden, slope = weight_call(
        "widen",
        widen,
        tiles,
        place,
        [
            (inputs, row_block(tile, model)),
            (branch, row_block(tile, model)),
            (branch_other, row_block(tile, model)),
            (scales, whole_block(8, model)),
        ],
        [up_set],
        [
            (far_shape(rows, model), row_block(tile, model)),
            (far_shape(rows, model), row_block(tile, model)),
            (far_shape(rows, inner), row_block(tile, inner)),
            (far_shape(rows, inner), row_block(tile, inner)),
        ],
        [pltpu.VMEM((model, inner), bf16)],
        copies,
        13,
    )

    if fine_down:
        hidden, slope, normed_two, down_side, down_near, lse = sync(
            hidden, slope, normed_two, down_side, down_near, lse
        )
        cuts, hidden = sync(halve(down_side, down_near), hidden)
        down_last = last_quarters(*cuts)
        down_keep, down_send = outer(place, depth, far(hidden), grad_result)
        hidden, slope, down_keep, down_send, normed_two, down_last = sync(
            hidden, slope, down_keep, down_send, normed_two, down_last
        )
        down_set = [down_part, down_side_own, down_far, down_side, down_near, *down_last]
        down_came = swap(down_send[0], "fx"), swap(down_send[1], "hi")
    else:
        down_keep = down_came = outer_whole(hidden, grad_result)
        down_send = None

    by_chunk = group == 2 and tile == chunk

    def narrow(place_ref, given, held, made, scratch, sems):
        hidden_ref, grad_ref, slope_ref, *downs = given
        *out_refs, pre_ref, back_ref = made
        upward = scratch[0]
        down_ref = scratch[1] if fine_down else downs[0]

        @pl.when(pl.program_id(0) == 0)
        def _():
            started = []
            if fine_down:
                targets = [(0, model, below(down_ref, down_rows // 2))]
                started = load(depth, place_ref, held[1], sems, targets, sem=copies)
            targets = [(0, inner, below(upward, half_rows))]
            for copy in started + load(depth, place_ref, held[0], sems, targets, up_at):
                copy.wait()

        for at in range(0, inner, wide):
            grad = mm_cols(grad_ref[...], down_ref[at : at + wide, :])
            pre_ref[:, at : at + wide] = (grad * slope_ref[:, at : at + wide].astype(f32)).astype(bf16)
        back_ref[...] = mm_cols(pre_ref[...], upward[...]).astype(bf16)
        out = mm(hidden_ref[...], down_ref[...]).astype(bf16)
        if by_chunk:
            own = lax.rem(pl.program_id(0), 2) == place_ref[3]

            @pl.when(own)
            def _():
                out_refs[0][0] = out

            @pl.when(~own)
            def _():
                out_refs[1][0] = out
        else:
            out_refs[0][...] = out

    *results, grad_pre, back = weight_call(
        "narrow",
        narrow,
        tiles,
        place,
        [
            (far(hidden), row_block(tile, inner)),
            (far(grad_result), row_block(tile, model)),
            (far(slope), row_block(tile, inner)),
        ]
        + ([] if fine_down else [(far(downward), whole_block(inner, model))]),
        [up_set, down_set] if fine_down else [up_set],
        (
            [
                (shape(micro, chunk, model), pl.BlockSpec((1, chunk, model), lambda i: (i // 2, 0, 0)))
                for shape in (far_shape, shape_of)
            ]
            if by_chunk
            else [(far_shape(rows, model), row_block(tile, model))]
        )
        + [
            (far_shape(rows, inner), row_block(tile, inner)),
            (far_shape(rows, model), row_block(tile, model)),
        ],
        [pltpu.VMEM((model, inner), bf16), pltpu.VMEM((inner, model), bf16)],
        2 * copies,
        18,
    )
    down_kept = None
    if fine_down:
        down_kept, down_send = fold_one(place, down_keep, down_came, far_shape)
    results, grad_pre, back, normed_two, down_kept, down_send, down_came = sync(
        results, grad_pre, back, normed_two, down_kept, down_send, down_came
    )

    back_other = other_part(back)
    if by_chunk:
        result, result_other = results[0], swap(results[1], "lo")
    else:
        result, result_other = own_chunks(results[0]), other_own(results[0])
    if fine_down:
        down_came = swap(down_send[0], "hi"), swap(down_send[1], "fx")
    up_keep, up_send = outer(place, depth, far(normed_two), far(grad_pre))
    back, back_other, up_keep, up_send, result_other = sync(back, back_other, up_keep, up_send, result_other)

    def between(place_ref, given, held, made, scratch, sems):
        grad_ref, own_ref, other_ref, middle_ref, scales_ref, weight = given
        branch_ref, attended_ref, sums_ref = made

        @pl.when(pl.program_id(0) == 0)
        def _():
            sums_ref[...] = jnp.zeros_like(sums_ref)

        unit_rows, inverse = unit_of(middle_ref[...].astype(f32))
        own_back = own_ref[...].astype(f32)
        back_rows = own_back + other_ref[...].astype(f32)
        sums_ref[0:1, :] += jnp.sum(own_back * unit_rows, axis=0, keepdims=True)
        sums_ref[1:2, :] += jnp.sum(own_back, axis=0, keepdims=True)
        grads = grad_ref[...].astype(f32) + unit_back(back_rows * scales_ref[2:3, :], unit_rows, inverse)
        low = grads.astype(bf16)
        branch_ref[...] = low
        attended_ref[...] = mm_cols(low, own_out(weight, place_ref)).astype(bf16)

    grad_branch, grad_attended, sums_two = weight_call(
        "between",
        between,
        tiles,
        place,
        [
            (grad_result, row_block(tile, model)),
            (back, row_block(tile, model)),
            (back_other, row_block(tile, model)),
            (far(middle), row_block(tile, model)),
            (scales, whole_block(8, model)),
            (out_weight, whole_block(*out_weight.shape)),
        ],
        [],
        [
            (far_shape(rows, model), row_block(tile, model)),
            (shape_of(rows, head_columns), row_block(tile, head_columns)),
            (shape_of(8, model, dtype=f32), whole_block(8, model)),
        ],
        [],
        1,
        8,
    )
    up_came = swap(up_send[0], "fx"), swap(up_send[1], "hi")
    down_sum = None
    if fine_down:
        grad_attended, down_came, down_kept = sync(grad_attended, down_came, down_kept)
        down_sum, down_send = fold_two(place, down_kept, down_came)
        grad_attended, down_send = sync(grad_attended, down_send)
        down_came = [along(value, "fz", depth, k) for k, value in zip(rest, down_send)]
    grad_joint = attend_back(joint, grad_attended, lse, seg_col, seg_row, 0, pairs)
    grad_joint, grad_branch, up_came, result_other, down_came, down_sum = sync(
        grad_joint, grad_branch, up_came, result_other, down_came, down_sum
    )

    def both_halves(value):
        return ordered(value, swap(value, "hi"), h, 1).reshape(-1, value.shape[2])

    up_kept, up_send = fold_one(place, up_keep, up_came)
    up_kept, up_send, grad_joint = sync(up_kept, up_send, grad_joint)
    up_came = swap(up_send[0], "hi"), swap(up_send[1], "fx")
    if fine_down:
        down_own = both_halves(add_up(down_sum, down_came))
    else:
        down_own = lax.psum(lax.psum_scatter(down_came, shard_axes, scatter_dimension=0, tiled=True), "hi")
    last_keep, last_send = outer(
        place,
        depth,
        normed,
        grad_joint,
        out_pair=[attended, grad_branch] if fused_out else None,
        weight=joint_weight,
        scales=scale_columns,
        sums=sums_two,
    )
    up_came, last_keep, last_send, down_own, grad_joint, result_other = sync(
        up_came, last_keep, last_send, down_own, grad_joint, result_other
    )

    up_sum, up_send = fold_two(place, up_kept, up_came)
    up_sum, up_send, last_send, grad_joint = sync(up_sum, up_send, last_send, grad_joint)
    last_came = swap(last_send[0], "fx"), swap(last_send[1], "hi")
    up_came = [along(value, "fz", depth, k) for k, value in zip(rest, up_send)]

    def enter(place_ref, given, held, made, scratch, sems):
        part_ref, weight = given
        (out_ref,) = made
        grads = jnp.zeros(out_ref.shape, f32)
        for j in range(3):
            grads = grads + mm_cols(part_ref[j], weight[:, j * head_columns : (j + 1) * head_columns])
        out_ref[...] = grads.astype(bf16)

    (entered,) = weight_call(
        "enter",
        enter,
        tiles,
        place,
        [
            (grad_joint, pl.BlockSpec((3, tile, head_columns), lambda i: (0, i, 0))),
            (joint_weight, whole_block(*joint_weight.shape)),
        ],
        [],
        [(shape_of(rows, model), row_block(tile, model))],
        [],
        1,
        14,
    )
    output = (own_chunks(middle).astype(f32) + result.astype(f32) + result_other.astype(f32)).astype(bf16)
    last_came, entered, up_sum, up_came, down_own, output = sync(
        last_came, entered, up_sum, up_came, down_own, output
    )

    last_kept, last_send = fold_one(place, last_keep, last_came)
    up_own = add_up(up_sum, up_came)
    last_kept, last_send, entered, up_own, down_own = sync(last_kept, last_send, entered, up_own, down_own)
    last_came = swap(last_send[0], "hi"), swap(last_send[1], "fx")
    up_own = both_halves(up_own)
    down_all = whole_group(down_own, 0).reshape(-1, model).astype(f32)
    entered_other = other_own(entered)
    grad_normed = own_chunks(entered).astype(f32) + entered_other.astype(f32)
    unit_own, inverse_own = unit_of(own_chunks(inputs).astype(f32))
    grad_tokens = own_chunks(grad_branch).astype(f32) + unit_back(grad_normed * scales[0], unit_own, inverse_own)
    grad_sent = pick(grad_tokens, 1 - h, 0).astype(bf16)
    last_came, grad_tokens, grad_sent, up_own, down_all, output = sync(
        last_came, grad_tokens, grad_sent, up_own, down_all, output
    )

    last_sum, last_send = fold_two(place, last_kept, last_came)
    last_came = [along(value, "fz", depth, k) for k, value in zip(rest, last_send)]
    grad_came = swap(grad_sent, "hi")
    output_came = swap(pick(output, 1 - h, 0), "hi")
    up_all = None
    if fused_out:
        up_all = finish_up(place, shards, up_own, swap(up_own, "lo"))
    last_came, grad_came, grad_tokens, up_own, up_all, output_came = sync(
        last_came, grad_came, grad_tokens, up_own, up_all, output_came
    )

    last_own = both_halves(add_up(last_sum, last_came))
    output = ordered(pick(output, h, 0), output_came, h, 0)[:, None]
    grad_tokens = ordered(pick(grad_tokens, h, 0), grad_came.astype(f32), h, 0)[:, None]
    last_own, grad_tokens, output = sync(last_own, grad_tokens, output)
    if fused_out:
        qkv_all, out_all, sums = finish_qkv(place, 3 * head_columns, [last_own], [swap(last_own, "lo")])
    else:
        up_all = whole_group(up_own.reshape(own_rows, shards, -1), 2).reshape(own_rows, -1).astype(f32)
        columns = 3 * head_columns
        qkv_own = last_own[:, :columns]
        if split_out:
            qkv_all = whole_group(qkv_own.reshape(own_rows, 3, shards, -1), 3)
        else:
            qkv_all = whole_group(qkv_own.reshape(own_rows, 3, -1), 2)
        qkv_all = qkv_all.reshape(own_rows, -1).astype(f32)
        sums = jnp.sum(whole_group(last_own[:, columns : columns + 4].astype(f32), 0), axis=0).T
        grad_out = outer_whole(attended, grad_branch)
        if not split_out:
            empty = jnp.zeros((model, model), bf16)
            grad_out = lax.dynamic_update_slice_in_dim(empty, grad_out, lo * head_columns, 0)
        out_own = lax.psum(lax.psum_scatter(grad_out, shard_axes, scatter_dimension=0, tiled=True), "hi")
        out_all = whole_group(out_own, 0).reshape(own_rows, model) if split_out else lax.psum(out_own, "lo")
        out_all = out_all.astype(f32)

    return (
        output,
        grad_tokens,
        sums[0],
        sums[1],
        qkv_all,
        out_all,
        sums[2],
        sums[3],
        up_all,
        down_all,
    )


def solution(mesh):
    seq, fsdp = mesh.shape["seq"], mesh.shape["fsdp"]
    group, depth = seq // 2, fsdp // 2
    fine = Mesh(mesh.devices.reshape(2, group, depth, 2), ("hi", "lo", "fz", "fx"))
    s, f = ("hi", "lo"), ("fz", "fx")
    return jax.shard_map(
        functools.partial(body, group, depth),
        mesh=fine,
        in_specs=(
            P(None, f, s, None),
            P(None, f, None),
            P(f),
            P(f),
            P(f, None),
            P(f, None),
            P(f),
            P(f),
            P(f, None),
            P(f, None),
            P(None, f, s, None),
        ),
        out_specs=(
            P(None, f, s, None),
            P(None, f, s, None),
            P(f),
            P(f),
            P(f, None),
            P(f, None),
            P(f),
            P(f),
            P(f, None),
            P(f, None),
        ),
        check_vma=False,
    )
```
